128 devices in a mesh: section: 2 (over core), fsdp: 64 (over y, x, z).
Axes of the slice: x: 4, y: 4, z: 4, core: 2. Of those that a mesh axis runs over, the one named last changes fastest.
Arguments:
- byte_states: bfloat16 [2, 64, 512, 1024], P('section', 'fsdp'), may hold values from -16 to 16
- patch_lengths: int32 [2, 64, 128], P(None, 'fsdp'), may hold values from 1 to 16, 512 in all within a row
- doc_ids: int32 [2, 64, 512], P(None, 'fsdp'), may hold values from 0 to 3, never falling along the last dimension, each value on 1 to 256 neighbouring positions
- proj_weights: bfloat16 [2, 3, 1024, 1024], P('section', None, 'fsdp'), may hold values from -0.1875 to 0.1875
- out_weights: bfloat16 [2, 1024, 1024], P('section', 'fsdp'), may hold values from -0.5 to 0.5
- norm_gains: bfloat16 [2, 2, 1024], P('section', None, 'fsdp'), may hold values from 0.099609375 to 1.8984375
- in_weights: bfloat16 [2, 1024, 2816], P(None, 'fsdp', 'section'), may hold values from -0.1875 to 0.1875
- down_weights: bfloat16 [1024, 2816], P('fsdp', 'section'), may hold values from -0.109375 to 0.109375
- cotangent: bfloat16 [2, 64, 128, 1024], P('section', 'fsdp'), may hold values from -16 to 16
Outputs:
- block_out: float32 [2, 64, 128, 1024], P('section', 'fsdp')
- byte_grad: float32 [2, 64, 512, 1024], P('section', 'fsdp')
- proj_grad: float32 [2, 3, 1024, 1024], P('section', None, 'fsdp')
- out_grad: float32 [2, 1024, 1024], P('section', 'fsdp')
- gain_grad: float32 [2, 2, 1024], P('section', None, 'fsdp')
- in_grad: float32 [2, 1024, 2816], P(None, 'fsdp', 'section')
- down_grad: float32 [1024, 2816], P('fsdp', 'section')
The draws below stay inside these ranges and needn't reach their ends.
Inputs may be any that keep to these rules, and one draw needn't show every extreme that they name: `patch_lengths`: the 128 patch lengths of a row sum to 512; some patch of every row has exactly 16 bytes. `doc_ids`: document numbers never fall along a row; each of the 4 documents of a row has at least one byte.
All inputs are finite; a program needn't handle non-finite values.
Results may differ from the reference program's by a relative error of at most 0.018.
Values may be sent and summed in bfloat16 or wider, within the bound.
No kernel may reach another device: no remote copies, remote signals or barrier semaphores. Data moves between devices by JAX's collectives and lax.ppermute only.
A program may use at most 320 MiB of HBM per device.

```python
import math
import jax
import jax.numpy as jnp
import numpy as np
from jax import lax

D = 1024
HEADS = 16
HEAD_DIM = 64
FF = 2816
PATCH_DEV = 128
MAXLEN = 16
DOCS = 4
BYTE_DEV = 512
MICRO = 2
NROWS = 64


def spiked(values, stream_key, source, target, blocks, factor):
    def block_of(dim):
        return (jnp.arange(values.shape[dim]) // (values.shape[dim] // blocks)).reshape((-1,) + (1,) * (values.ndim - 1 - dim))

    first = jax.random.permutation(stream_key, blocks)[block_of(target)]
    far = (block_of(target) + blocks // 2) % blocks
    return jnp.where((block_of(source) == first) | (block_of(source) == far), factor * values, values)


def level_of(own_key, dims, shards, low, high):
    def one(position, shards_of):
        draws = jax.random.uniform(jax.random.fold_in(jax.random.fold_in(own_key, 6), position), (shards_of,), jnp.float32, low / len(shards), high / len(shards))
        return jnp.repeat(jnp.exp(draws), dims[position] // shards_of).reshape((-1,) + (1,) * (len(dims) - position - 1))

    loudness = one(*shards[0])
    for cut in shards[1:]:
        loudness = loudness * one(*cut)
    return loudness


def profile(number_of, total, most, skew):
    portions = [(1 << 20) // math.isqrt(rank ** skew) + 1 for rank in range(2, number_of + 1)]
    surplus, holding = total - most - (number_of - 1), [1] * (number_of - 1)
    while surplus > 0:
        movable = [i for i in range(number_of - 1) if holding[i] < most]
        mass, budget = sum([portions[i] for i in movable]), surplus
        for i in movable:
            addition = min(most - holding[i], max(1, budget * portions[i] // mass), surplus)
            holding[i] = holding[i] + addition
            surplus = surplus - addition
    return np.array([most] + holding)


def uneven(key, amount, total, limit, lean):
    if amount == 2:
        one = jax.random.randint(key, (), max(1, total - limit), min(limit, total - 1) + 1)
        return jnp.stack([one, total - one])
    tallies = jnp.asarray(profile(amount, total, limit, lean), jnp.int32)
    pairs = (amount - 1) // 2
    source_of, taker = tallies[1:1 + 2 * pairs:2], tallies[2:2 + 2 * pairs:2]
    margin = jnp.minimum(source_of - 1, limit - taker)
    shifted = jax.random.randint(jax.random.fold_in(key, 1), (pairs,), 0, 1 << 20) % (margin + 1)
    tallies = tallies.at[1:1 + 2 * pairs:2].set(source_of - shifted).at[2:2 + 2 * pairs:2].set(taker + shifted)
    return tallies[jax.random.permutation(jax.random.fold_in(key, 2), amount)]


def centred(key, extent, width, bound, cuts=(), held_as=jnp.bfloat16):
    array = jax.random.normal(key, extent, jnp.float32) * width
    if len(cuts) > 0:
        array = level_of(key, extent, cuts, -0.22, 0.18) * array
    return jnp.clip(array, min=-bound, max=bound).astype(held_as)


def bell_draw_with(key, extent, width, bound, pieces, heavy, kind=jnp.bfloat16):
    values = width * jax.random.normal(key, extent, jnp.float32)
    if pieces:
        values = values * level_of(key, extent, pieces, -0.22, 0.18)
    return jnp.clip(spiked(values, jax.random.fold_in(key, 3), *heavy), -bound, bound).astype(kind)


def setup_inputs(seed: int = 0) -> dict:
    seeds = jax.random.split(jax.random.key(seed), 10)
    return {
        "byte_states": bell_draw_with(seeds[0], (MICRO, NROWS, BYTE_DEV, D), 1.0, 16.0, ((0, 2), (1, 64)), (1, 3, 64, 4.0)),
        "patch_lengths": jax.vmap(lambda own: uneven(own, PATCH_DEV, BYTE_DEV, MAXLEN, 1))(jax.random.split(seeds[1], MICRO * NROWS)).reshape((MICRO, NROWS, PATCH_DEV)).astype(jnp.int32),
        "doc_ids": jax.vmap(lambda own: jnp.searchsorted(jnp.cumsum(uneven(own, DOCS, BYTE_DEV, BYTE_DEV // 2, 1)), jnp.arange(BYTE_DEV), side="right"))(jax.random.split(seeds[2], MICRO * NROWS)).reshape((MICRO, NROWS, BYTE_DEV)).astype(jnp.int32),
        "proj_weights": centred(seeds[3], (2, 3, D, D), D ** -0.5, 0.1875, ((0, 2), (2, 64))),
        "out_weights": centred(seeds[4], (2, D, D), (D // 8) ** -0.5, 0.5, ((0, 2), (1, 64))),
        "norm_gains": jnp.clip(1.0 + 0.18 * jax.random.normal(seeds[5], (2, 2, D), jnp.float32), 0.099609375, 1.8984375).astype(jnp.bfloat16),
        "in_weights": centred(seeds[6], (2, D, FF), D ** -0.5, 0.1875, ((1, 64), (2, 2))),
        "down_weights": centred(seeds[7], (D, FF), FF ** -0.5, 0.109375, ((0, 64), (1, 2))),
        "cotangent": bell_draw_with(seeds[8], (MICRO, NROWS, PATCH_DEV, D), 1.0, 16.0, ((0, 2), (1, 64)), (1, 3, 64, 4.0)),
    }


epsilon = 1e-05
masked_score = -1e+30

@jax.custom_vjp
def low(v):
    return lax.optimization_barrier(v.astype(jnp.bfloat16)).astype(jnp.float32)

@jax.custom_vjp
def low_back(v):
    return v

def low_keep(v):
    return (low(v), None)

def low_pass(kept, grad):
    return (grad,)

def back_keep(v):
    return (v, None)

def back_low(kept, grad):
    return (low(grad),)
low.defvjp(low_keep, low_pass)
low_back.defvjp(back_keep, back_low)

def normalize(values, scales):
    return values * lax.rsqrt(lax.optimization_barrier(jnp.mean(values * values, axis=-1, keepdims=True)) + epsilon) * scales

def product(left, right):
    return jnp.dot(left, right, precision=lax.Precision.HIGHEST, preferred_element_type=jnp.float32)

def attend(queries, keys, values, allowed):
    query_heads = queries.reshape(queries.shape[0], HEADS, HEAD_DIM)
    key_heads = keys.reshape(keys.shape[0], HEADS, HEAD_DIM)
    value_heads = values.reshape(values.shape[0], HEADS, HEAD_DIM)
    raw = low_back(jnp.einsum('rhd,khd->hrk', query_heads, key_heads, precision=lax.Precision.HIGHEST))
    scores = jnp.where(allowed[None], raw * HEAD_DIM ** (-0.5), masked_score)
    highest = lax.optimization_barrier(jnp.max(scores, axis=-1, keepdims=True))
    weights = jnp.exp(scores - highest)
    probability = low(weights / lax.optimization_barrier(jnp.sum(weights, axis=-1, keepdims=True)))
    mixed = jnp.einsum('hrk,khd->rhd', probability, value_heads, precision=lax.Precision.HIGHEST)
    return mixed.reshape(queries.shape[0], HEADS * HEAD_DIM)

def patch_tables(lengths, documents):
    patch_end = jnp.cumsum(lengths, dtype=jnp.int32)
    starts = (patch_end - lengths).astype(jnp.int32)
    byte_pos = jnp.arange(BYTE_DEV, dtype=jnp.int32)
    member = (byte_pos[None, :] >= starts[:, None]) & (byte_pos[None, :] < patch_end[:, None])
    first_doc = documents[starts]
    return (member, first_doc)

def encoder_row(byte_rows, lengths, documents, projections, output_w, scales):
    member, first_doc = patch_tables(lengths, documents)
    allowed = member & (documents[None, :] == first_doc[:, None])
    pooled = product(member.astype(jnp.float32), byte_rows) / lengths.astype(jnp.float32)[:, None]
    query_low = low(normalize(pooled, scales[0]))
    queries = low(low_back(product(query_low, projections[0])))
    byte_low = low(normalize(byte_rows, scales[1]))
    keys = low(low_back(product(byte_low, projections[1])))
    values = low(low_back(product(byte_low, projections[2])))
    mixed = low(low_back(attend(queries, keys, values, allowed)))
    embedded = pooled + low_back(product(mixed, output_w))
    return low(low_back(embedded))

def global_row(hidden, lengths, documents, projections, output_w, scales, gate_up, down_w):
    member, first_doc = patch_tables(lengths, documents)
    order = jnp.arange(PATCH_DEV, dtype=jnp.int32)
    allowed = (order[None, :] <= order[:, None]) & (first_doc[None, :] == first_doc[:, None])
    normed_low = low(normalize(hidden, scales[0]))
    queries = low(low_back(product(normed_low, projections[0])))
    keys = low(low_back(product(normed_low, projections[1])))
    values = low(low_back(product(normed_low, projections[2])))
    mixed = low(low_back(attend(queries, keys, values, allowed)))
    middle = hidden + low_back(product(mixed, output_w))
    ffn_low = low(normalize(middle, scales[1]))
    gate = low_back(product(ffn_low, gate_up[0]))
    up_part = low_back(product(ffn_low, gate_up[1]))
    inner = low(jax.nn.silu(gate) * up_part)
    return middle + low_back(product(inner, down_w.T))

def reference(byte_states, patch_lengths, doc_ids, proj_weights, out_weights, norm_gains, in_weights, down_weights, cotangent):
    row_count = MICRO * NROWS
    lengths = patch_lengths.reshape(row_count, PATCH_DEV)
    documents = doc_ids.reshape(row_count, BYTE_DEV)

    def forward(byte_float, projections, output_w, scales, gate_up, down_w):

        def encoder_one(items):
            return encoder_row(items[0], items[1], items[2], projections[0], output_w[0], scales[0])

        def global_one(items):
            return global_row(items[0], items[1], items[2], projections[1], output_w[1], scales[1], gate_up, down_w)
        patches = lax.map(jax.checkpoint(encoder_one), (byte_float.reshape(row_count, BYTE_DEV, D), lengths, documents))
        results = lax.map(jax.checkpoint(global_one), (patches, lengths, documents))
        return results.reshape(MICRO, NROWS, PATCH_DEV, D)
    result, pullback = jax.vjp(forward, byte_states.astype(jnp.float32), proj_weights.astype(jnp.float32), out_weights.astype(jnp.float32), norm_gains.astype(jnp.float32), in_weights.astype(jnp.float32), down_weights.astype(jnp.float32))
    gradients = pullback(cotangent.astype(jnp.float32))
    return (result, gradients[0], gradients[1], gradients[2], gradients[3], gradients[4], gradients[5])
```

```python
import functools

import jax
import jax.numpy as jnp
from jax import lax
from jax.experimental import pallas as pl
from jax.experimental.pallas import tpu as pltpu
from jax.sharding import PartitionSpec as P

HEADS = 16
HEAD_DIM = 64
QUAD = 4
LANES = QUAD * HEAD_DIM
RING = 4
STRIDE = {"y": 16, "x": 4, "z": 1}
DIM = {"y": 0, "x": 1, "z": 2}

epsilon = 1e-05
masked_score = -1e30
bf16 = jnp.bfloat16
f32 = jnp.float32


def across(block):
    return lax.ppermute(block, "section", [(0, 1), (1, 0)])


def shift(block, ax, by):
    step = STRIDE[ax]

    def to(i):
        c = (i // step) % RING
        return i + ((c + by) % RING - c) * step

    return lax.ppermute(block, "fsdp", [(i, to(i)) for i in range(64)])


def place(ax):
    return (lax.axis_index("fsdp") // STRIDE[ax]) % RING


def ring_sum(g, ax, two_steps, out):
    dim, half = DIM[ax], 4
    c = place(ax)
    own, up, down, far = (
        lax.dynamic_slice_in_dim(g, (c + k) % RING, 1, dim) for k in (0, 1, 3, 2)
    )
    if two_steps:
        h = g.shape[half] // 2 // 128 * 128
        head = functools.partial(lax.slice_in_dim, start_index=0, limit_index=h, axis=half)
        tail = functools.partial(lax.slice_in_dim, start_index=h, limit_index=None, axis=half)
        a = shift(head(far), ax, 1)
        b = shift(tail(far), ax, -1)
        up_head = (head(up).astype(f32) + a.astype(f32)).astype(g.dtype)
        down_tail = (tail(down).astype(f32) + b.astype(f32)).astype(g.dtype)
        from_below = shift(jnp.concatenate([up_head, tail(up)], axis=half), ax, 1)
        from_above = shift(jnp.concatenate([head(down), down_tail], axis=half), ax, -1)
        total = own.astype(f32) + from_below.astype(f32) + from_above.astype(f32)
    else:
        r1, r2, r3 = shift(up, ax, 1), shift(down, ax, -1), shift(far, ax, 2)
        total = (own.astype(f32) + r3.astype(f32)) + (r1.astype(f32) + r2.astype(f32))
    return total.astype(out)


def scatter_sum(g, order):
    x = g.reshape(RING, RING, RING, 16, g.shape[1])
    for k, ax in enumerate(order):
        x = ring_sum(x, ax, k == 0, f32 if k == 2 else bf16)
    return x.reshape(16, g.shape[1])


def inverse_rms(values):
    return lax.rsqrt(jnp.mean(values * values, axis=-1, keepdims=True) + epsilon)


def normalize_back(values, inverse, scales, gradient):
    unit_rows = values * inverse
    scaled = gradient * scales
    inner_mean = jnp.mean(scaled * unit_rows, axis=-1, keepdims=True)
    return inverse * (scaled - unit_rows * inner_mean)


def matmul(left, right):
    return jnp.dot(left, right, preferred_element_type=f32)


def times_transposed(left, right):
    return lax.dot_general(left, right, (((1,), (1,)), ((), ())), preferred_element_type=f32)


def transposed_times(left, right):
    return lax.dot_general(left, right, (((0,), (0,)), ((), ())), preferred_element_type=f32)


def of_head(value, h):
    head = lax.broadcasted_iota(jnp.int32, value.shape, 1) // HEAD_DIM
    return jnp.where(head == h, value, jnp.zeros_like(value))


def stacked(value):
    return jnp.concatenate([of_head(value, h) for h in range(QUAD)], axis=0)


def unstacked(value, rows):
    total = of_head(value[:rows], 0)
    for h in range(1, QUAD):
        total = total + of_head(value[h * rows : (h + 1) * rows], h)
    return total


def probabilities(q4, keys, table, rows):
    raw = times_transposed(q4, keys)
    allowed = jnp.concatenate([table] * QUAD, axis=0) > 0
    scores = jnp.where(allowed, raw * HEAD_DIM ** (-0.5), masked_score)
    weights = jnp.exp(scores - jnp.max(scores, axis=-1, keepdims=True))
    return weights / jnp.sum(weights, axis=-1, keepdims=True)


def attend_kernel(q_ref, k_ref, v_ref, table_ref, out_ref):
    rows = q_ref.shape[0]
    q4 = stacked(q_ref[...])
    p = probabilities(q4, k_ref[...], table_ref[0], rows).astype(bf16)
    out_ref[...] = unstacked(matmul(p, v_ref[...]), rows).astype(bf16)


def attend_back_kernel(q_ref, k_ref, v_ref, table_ref, d_ref, dq_ref, dk_ref, dv_ref):
    rows = q_ref.shape[0]
    q4 = stacked(q_ref[...])
    d4 = stacked(d_ref[...])
    p = probabilities(q4, k_ref[...], table_ref[0], rows)
    dp = times_transposed(d4, v_ref[...])
    ds = p * (dp - jnp.sum(p * dp, axis=-1, keepdims=True)) * HEAD_DIM ** (-0.5)
    ds = ds.astype(bf16)
    dq_ref[...] = unstacked(matmul(ds, k_ref[...]), rows).astype(bf16)
    dk_ref[...] = transposed_times(ds, q4).astype(bf16)
    dv_ref[...] = transposed_times(p.astype(bf16), d4).astype(bf16)


def attention_specs(rows, keys):
    per_row = pl.BlockSpec((rows, LANES), lambda m, h: (m, h))
    per_key = pl.BlockSpec((keys, LANES), lambda m, h: (m, h))
    table = pl.BlockSpec((1, rows, keys), lambda m, h: (m, 0, 0))
    return per_row, per_key, table


def attend(q, k, v, table):
    micro, rows, keys = table.shape
    per_row, per_key, per_table = attention_specs(rows, keys)
    return pl.pallas_call(
        attend_kernel,
        grid=(micro, q.shape[1] // LANES),
        in_specs=[per_row, per_key, per_key, per_table],
        out_specs=per_row,
        out_shape=jax.ShapeDtypeStruct(q.shape, bf16),
        compiler_params=pltpu.CompilerParams(vmem_limit_bytes=32 << 20),
        cost_estimate=pl.CostEstimate(
            flops=2 * q.shape[0] * keys * LANES * 2 * q.shape[1] // HEAD_DIM,
            bytes_accessed=4 * (q.size + k.size),
            transcendentals=table.size * q.shape[1] // HEAD_DIM,
        ),
        name="attend",
    )(q, k, v, table)


def attend_back(q, k, v, table, d):
    micro, rows, keys = table.shape
    per_row, per_key, per_table = attention_specs(rows, keys)
    return pl.pallas_call(
        attend_back_kernel,
        grid=(micro, q.shape[1] // LANES),
        in_specs=[per_row, per_key, per_key, per_table, per_row],
        out_specs=[per_row, per_key, per_key],
        out_shape=[
            jax.ShapeDtypeStruct(q.shape, bf16),
            jax.ShapeDtypeStruct(k.shape, bf16),
            jax.ShapeDtypeStruct(v.shape, bf16),
        ],
        compiler_params=pltpu.CompilerParams(vmem_limit_bytes=48 << 20),
        cost_estimate=pl.CostEstimate(
            flops=5 * q.shape[0] * keys * LANES * 2 * q.shape[1] // HEAD_DIM,
            bytes_accessed=6 * (q.size + k.size),
            transcendentals=table.size * q.shape[1] // HEAD_DIM,
        ),
        name="attend_back",
    )(q, k, v, table, d)


def patch_tables(lengths, documents):
    patches, count = lengths.shape[1], documents.shape[1]
    ends = jnp.cumsum(lengths, axis=1, dtype=jnp.int32)
    starts = ends - lengths
    position = lax.broadcasted_iota(jnp.int32, (1, patches, count), 2)
    member = (position >= starts[:, :, None]) & (position < ends[:, :, None])
    first_doc = jnp.sum(
        jnp.where(position == starts[:, :, None], documents[:, None, :], 0), axis=2
    )
    allowed = member & (documents[:, None, :] == first_doc[:, :, None])
    order_rows = lax.broadcasted_iota(jnp.int32, (1, patches, patches), 1)
    order_cols = lax.broadcasted_iota(jnp.int32, (1, patches, patches), 2)
    causal = (order_cols <= order_rows) & (first_doc[:, None, :] == first_doc[:, :, None])
    return member.astype(bf16), allowed.astype(f32), causal.astype(f32)


def swapped(x):
    half = x.shape[0] // 2
    return jnp.concatenate([x[half:], x[:half]], axis=0)


def own_first(pair, section):
    return jnp.where(section == 0, pair, pair[::-1])


def both_halves(own, section):
    other = across(swapped(own))
    return jnp.where(
        section == 0,
        jnp.concatenate([own, other], axis=1),
        jnp.concatenate([other, own], axis=1),
    )


def core_sum(partial):
    return partial + across(swapped(partial.astype(bf16))).astype(f32)


def shards(
    byte_states,
    patch_lengths,
    doc_ids,
    proj_weights,
    out_weights,
    norm_gains,
    in_weights,
    down_weights,
    cotangent,
):
    section = lax.axis_index("section")
    width = byte_states.shape[-1]
    half = width // 2
    units = down_weights.shape[1]

    own_w = jnp.concatenate([proj_weights[0], out_weights], axis=0)
    own_w = own_w.transpose(1, 0, 2).reshape(16, 4, 2, half)
    keep = jnp.where(section == 0, own_w[:, :, 0], own_w[:, :, 1])
    give = jnp.where(section == 0, own_w[:, :, 1], own_w[:, :, 0])
    got = across(give)
    enc_shard = jnp.where(section == 0, keep, got).reshape(16, 4 * half)
    glob_shard = jnp.where(section == 0, got, keep).reshape(16, 4 * half)
    shard = jnp.concatenate(
        [enc_shard, glob_shard, in_weights[0], in_weights[1], down_weights], axis=1
    )
    gathered = lax.all_gather(shard, "fsdp", axis=0, tiled=True)
    cuts = [half * k for k in range(9)]
    cuts += [cuts[-1] + units * k for k in (1, 2, 3)]
    wq0, wk0, wv0, wo0, wq1, wk1, wv1, wo1, w_gate, w_up, w_down = (
        gathered[:, a:b] for a, b in zip(cuts[:-1], cuts[1:])
    )

    def whole_out(own):
        other = across(own)
        return jnp.where(
            section == 0,
            jnp.concatenate([own, other], axis=1),
            jnp.concatenate([other, own], axis=1),
        )

    out0, out1 = whole_out(wo0), whole_out(wo1)
    out0_rows = lax.dynamic_slice_in_dim(out0, section * half, half, 0)
    out1_rows = lax.dynamic_slice_in_dim(out1, section * half, half, 0)

    gains_sent = jnp.broadcast_to(norm_gains[0].astype(f32)[None], (128, 2, 16))
    gains = lax.all_to_all(gains_sent, ("section", "fsdp"), 0, 0, tiled=True)
    gains = gains.reshape(2, 64, 2, 16).transpose(0, 2, 1, 3).reshape(2, 2, width)

    own_bytes, own_target = byte_states[0, 0], cotangent[0, 0]
    raw = jnp.concatenate([own_bytes, across(own_bytes)], axis=0)
    target = jnp.concatenate([own_target, across(own_target)], axis=0)
    lengths = own_first(patch_lengths[:, 0], section)
    documents = own_first(doc_ids[:, 0], section)
    patches, count = lengths.shape[1], documents.shape[1]
    member, allowed, causal = patch_tables(lengths, documents)
    size = lengths.astype(f32).reshape(-1, 1)

    raw_f32 = raw.astype(f32)
    pooled = lax.dot_general(
        member,
        raw.reshape(2, count, width),
        (((2,), (1,)), ((0,), (0,))),
        preferred_element_type=f32,
    ).reshape(2 * patches, width)
    pooled = pooled / size
    query_inv = inverse_rms(pooled)
    query_low = (pooled * query_inv * gains[0, 0]).astype(bf16)
    byte_inv = inverse_rms(raw_f32)
    byte_low = (raw_f32 * byte_inv * gains[0, 1]).astype(bf16)
    q0 = matmul(query_low, wq0).astype(bf16)
    k0 = matmul(byte_low, wk0).astype(bf16)
    v0 = matmul(byte_low, wv0).astype(bf16)
    mixed0 = both_halves(attend(q0, k0, v0, allowed), section)
    hidden = (pooled + matmul(mixed0, out0)).astype(bf16).astype(f32)

    normed_inv = inverse_rms(hidden)
    normed_low = (hidden * normed_inv * gains[1, 0]).astype(bf16)
    q1 = matmul(normed_low, wq1).astype(bf16)
    k1 = matmul(normed_low, wk1).astype(bf16)
    v1 = matmul(normed_low, wv1).astype(bf16)
    mixed1 = both_halves(attend(q1, k1, v1, causal), section)
    middle = hidden + matmul(mixed1, out1)
    ffn_inv = inverse_rms(middle)
    ffn_low = (middle * ffn_inv * gains[1, 1]).astype(bf16)
    gate = matmul(ffn_low, w_gate)
    up = matmul(ffn_low, w_up)
    sigma = jax.nn.sigmoid(gate)
    inner = (gate * sigma * up).astype(bf16)

    down_sum = scatter_sum(transposed_times(target, inner).astype(bf16), "yxz")
    inner_grad = matmul(target, w_down)
    up_grad = (inner_grad * gate * sigma).astype(bf16)
    gate_grad = (inner_grad * up * sigma * (1.0 + gate * (1.0 - sigma))).astype(bf16)
    gate_sum = scatter_sum(transposed_times(ffn_low, gate_grad).astype(bf16), "xzy")
    up_sum = scatter_sum(transposed_times(ffn_low, up_grad).astype(bf16), "zyx")
    ffn_in_grad = core_sum(
        times_transposed(gate_grad, w_gate) + times_transposed(up_grad, w_up)
    )
    result = times_transposed(inner, w_down)
    block_out = middle[:patches] + result[:patches]
    block_out = block_out + across(result[patches:].astype(bf16)).astype(f32)

    middle_grad = target.astype(f32) + normalize_back(middle, ffn_inv, gains[1, 1], ffn_in_grad)
    middle_low = middle_grad.astype(bf16)

    def column_half(x):
        return lax.dynamic_slice_in_dim(x, section * half, half, 1)

    out1_grad = transposed_times(mixed1, column_half(middle_low)).astype(bf16)
    mixed_grad = times_transposed(middle_low, out1_rows).astype(bf16)
    dq, dk, dv = attend_back(q1, k1, v1, causal, mixed_grad)
    glob_grads = jnp.concatenate(
        [transposed_times(normed_low, d).astype(bf16) for d in (dq, dk, dv)] + [out1_grad], axis=1
    )
    glob_sum = scatter_sum(glob_grads, "zyx")
    normed_grad = core_sum(
        times_transposed(dq, wq1) + times_transposed(dk, wk1) + times_transposed(dv, wv1)
    )
    hidden_grad = middle_grad + normalize_back(hidden, normed_inv, gains[1, 0], normed_grad)
    embed_grad = hidden_grad.astype(bf16)

    out0_grad = transposed_times(mixed0, column_half(embed_grad)).astype(bf16)
    mixed_grad = times_transposed(embed_grad, out0_rows).astype(bf16)
    dq, dk, dv = attend_back(q0, k0, v0, allowed, mixed_grad)
    kv_grads = jnp.concatenate(
        [transposed_times(byte_low, d).astype(bf16) for d in (dk, dv)], axis=1
    )
    qo_grads = jnp.concatenate([transposed_times(query_low, dq).astype(bf16), out0_grad], axis=1)
    kv_sum = scatter_sum(kv_grads, "yxz")
    qo_sum = scatter_sum(qo_grads, "xzy")

    def own_share(partial):
        rows = partial.shape[0] // 2
        return partial[:rows] + across(partial[rows:].astype(bf16)).astype(f32)

    query_in_grad = own_share(times_transposed(dq, wq0))
    byte_in_grad = own_share(times_transposed(dk, wk0) + times_transposed(dv, wv0))
    pooled_grad = embed_grad[:patches].astype(f32) + normalize_back(
        pooled[:patches], query_inv[:patches], gains[0, 0], query_in_grad
    )
    share = pooled_grad / size[:patches]
    share_high = share.astype(bf16)
    share_low = (share - share_high.astype(f32)).astype(bf16)
    spread = transposed_times(member[0], share_high) + transposed_times(member[0], share_low)
    byte_grad = spread + normalize_back(
        raw_f32[:count], byte_inv[:count], gains[0, 1], byte_in_grad
    )

    def gain_grad(values, inverse, gradient):
        rows = gradient.shape[0]
        return jnp.sum(gradient * (values[:rows] * inverse[:rows]), axis=0)

    gain_parts = jnp.stack(
        [
            gain_grad(pooled, query_inv, query_in_grad),
            gain_grad(raw_f32, byte_inv, byte_in_grad),
            gain_grad(hidden, normed_inv, normed_grad[:patches]),
            gain_grad(middle, ffn_inv, ffn_in_grad[:patches]),
        ]
    )
    gain_parts = gain_parts.reshape(2, 2, 64, 16).transpose(0, 2, 1, 3).reshape(128, 2, 16)
    gain_parts = lax.all_to_all(gain_parts, ("section", "fsdp"), 0, 0, tiled=True)
    gain_sum = jnp.sum(gain_parts, axis=0)

    kq, kv = jnp.split(kv_sum, 2, axis=1)
    qq, qo = jnp.split(qo_sum, 2, axis=1)
    enc_sum = jnp.stack([qq, kq, kv, qo])
    glob_sum = jnp.stack(jnp.split(glob_sum, 4, axis=1))
    mine = jnp.where(section == 0, enc_sum, glob_sum)
    theirs = across(jnp.where(section == 0, glob_sum, enc_sum))
    sums = jnp.where(
        section == 0,
        jnp.concatenate([mine, theirs], axis=2),
        jnp.concatenate([theirs, mine], axis=2),
    )
    return (
        block_out[None, None],
        byte_grad[None, None],
        sums[None, :3],
        sums[3:],
        gain_sum[None],
        jnp.stack([gate_sum, up_sum]),
        down_sum,
    )


def solution(mesh):
    in_specs = (
        P("section", "fsdp", None, None),
        P(None, "fsdp", None),
        P(None, "fsdp", None),
        P("section", None, "fsdp", None),
        P("section", "fsdp", None),
        P("section", None, "fsdp"),
        P(None, "fsdp", "section"),
        P("fsdp", "section"),
        P("section", "fsdp", None, None),
    )
    out_specs = (
        P("section", "fsdp", None, None),
        P("section", "fsdp", None, None),
        P("section", None, "fsdp", None),
        P("section", "fsdp", None),
        P("section", None, "fsdp"),
        P(None, "fsdp", "section"),
        P("fsdp", "section"),
    )
    return jax.shard_map(shards, mesh=mesh, in_specs=in_specs, out_specs=out_specs, check_vma=False)
```

```python
import jax
import jax.numpy as jnp
from jax import lax
from jax.experimental import pallas as pl
from jax.experimental.pallas import tpu as pltpu
from jax.sharding import PartitionSpec as P

HEADS = 16
HEAD_DIM = 64
QUAD = 4
LANES = QUAD * HEAD_DIM
RING = 4
STRIDE = {"y": 16, "x": 4, "z": 1}

epsilon = 1e-05
masked_score = -1e30
bf16 = jnp.bfloat16
f32 = jnp.float32


def across(block):
    return lax.ppermute(block, "section", [(0, 1), (1, 0)])


def shift(block, ax, by):
    step = STRIDE[ax]

    def to(i):
        c = (i // step) % RING
        return i + ((c + by) % RING - c) * step

    return lax.ppermute(block, "fsdp", [(i, to(i)) for i in range(64)])


def place(ax):
    return (lax.axis_index("fsdp") // STRIDE[ax]) % RING


def plane(ax):
    rows = {}
    for i in range(64):
        rows.setdefault((i // STRIDE[ax]) % RING, []).append(i)
    return [rows[c] for c in range(RING)]


def line(ax):
    rows = {}
    for i in range(64):
        c = (i // STRIDE[ax]) % RING
        rows.setdefault(i - c * STRIDE[ax], []).append(i)
    return list(rows.values())


def put(whole, piece, at, dim):
    where = [0] * whole.ndim
    where[dim] = at
    return lax.dynamic_update_slice(whole, piece, where)


def gather_direct(block, ax, dim):
    c = place(ax)
    whole = jnp.zeros((*block.shape[:dim], RING, *block.shape[dim + 1 :]), block.dtype)
    arrived = [(shift(block, ax, by), (c - by) % RING) for by in (1, -1, 2)]
    for piece, at in [(block, c)] + arrived:
        whole = put(whole, piece, at, dim)
    return whole


def gather_ring(block, ax, dim):
    c = place(ax)
    half = block.shape[-1] // 256 * 128
    last = block.ndim - 1
    whole = jnp.zeros((*block.shape[:dim], RING, *block.shape[dim + 1 :]), block.dtype)
    below, above = shift(block, ax, 1), shift(block, ax, -1)
    first = shift(lax.slice_in_dim(below, 0, half, axis=last), ax, 1)
    second = shift(lax.slice_in_dim(above, half, None, axis=last), ax, -1)
    for piece, at in ((block, c), (below, (c + 3) % RING), (above, (c + 1) % RING)):
        whole = put(whole, piece, at, dim)
    where = [0] * whole.ndim
    where[dim] = (c + 2) % RING
    whole = lax.dynamic_update_slice(whole, first, where)
    where[last] = half
    return lax.dynamic_update_slice(whole, second, where)


def turned(width, ax, turn):
    block = width // 64
    source = lax.broadcasted_iota(jnp.int32, (width, width), 0)
    column = lax.broadcasted_iota(jnp.int32, (width, width), 1)
    owner, within = source // block, source % block
    step = STRIDE[ax]
    c = (owner // step) % RING
    rest = owner % step + owner // (step * RING) * step
    target = ((c + RING - turn) % RING) * (width // RING) + rest * block + within
    return (column == target).astype(bf16)


def quarter(x, k):
    size = x.shape[1] // RING
    return x[:, k * size : (k + 1) * size]


def far_parts(x, d):
    far = transposed_times(quarter(x, 2), d).astype(bf16)
    half = far.shape[1] // 256 * 128
    return far[:, :half], far[:, half:]


def send_far(parts, ax):
    return shift(parts[0], ax, 1), shift(parts[1], ax, -1)


def near_parts(x, d, arrived):
    a, b = arrived
    up = transposed_times(quarter(x, 1), d)
    down = transposed_times(quarter(x, 3), d)
    up = up + jnp.pad(a.astype(f32), ((0, 0), (0, b.shape[1])))
    down = down + jnp.pad(b.astype(f32), ((0, 0), (a.shape[1], 0)))
    return up.astype(bf16), down.astype(bf16)


def send_near(parts, ax):
    return shift(parts[0], ax, 1), shift(parts[1], ax, -1)


def line_total(x, d, arrived):
    own = transposed_times(quarter(x, 0), d)
    return (own + (arrived[0].astype(f32) + arrived[1].astype(f32))).astype(bf16)


def line_sum(g, ax):
    parts = g.reshape(RING, g.shape[0] // RING, g.shape[1])
    return lax.psum_scatter(
        parts, "fsdp", scatter_dimension=0, axis_index_groups=line(ax), tiled=False
    )


def plane_sum(part, ax):
    blocks = part.reshape(16, part.shape[0] // 16, part.shape[1])
    blocks = lax.all_to_all(blocks, "fsdp", 0, 0, axis_index_groups=plane(ax), tiled=True)
    return jnp.sum(blocks.astype(f32), axis=0)


def stage(*values):
    return lax.optimization_barrier(values)


def inverse_rms(values):
    return lax.rsqrt(jnp.mean(values * values, axis=-1, keepdims=True) + epsilon)


def normalize_back(values, inverse, scales, gradient):
    unit_rows = values * inverse
    scaled = gradient * scales
    inner_mean = jnp.mean(scaled * unit_rows, axis=-1, keepdims=True)
    return inverse * (scaled - unit_rows * inner_mean)


def matmul(left, right):
    return jnp.dot(left, right, preferred_element_type=f32)


def times_transposed(left, right):
    return lax.dot_general(left, right, (((1,), (1,)), ((), ())), preferred_element_type=f32)


def transposed_times(left, right):
    return lax.dot_general(left, right, (((0,), (0,)), ((), ())), preferred_element_type=f32)


def of_head(value, h):
    head = lax.broadcasted_iota(jnp.int32, value.shape, 1) // HEAD_DIM
    return jnp.where(head == h, value, jnp.zeros_like(value))


def stacked(value):
    return jnp.concatenate([of_head(value, h) for h in range(QUAD)], axis=0)


def unstacked(value, rows):
    total = of_head(value[:rows], 0)
    for h in range(1, QUAD):
        total = total + of_head(value[h * rows : (h + 1) * rows], h)
    return total


def probabilities(q4, keys, table, rows):
    raw = times_transposed(q4, keys)
    allowed = jnp.concatenate([table] * QUAD, axis=0) > 0
    scores = jnp.where(allowed, raw * HEAD_DIM ** (-0.5), masked_score)
    weights = jnp.exp(scores - jnp.max(scores, axis=-1, keepdims=True))
    return weights / jnp.sum(weights, axis=-1, keepdims=True)


def attend_kernel(q_ref, k_ref, v_ref, table_ref, out_ref):
    rows = q_ref.shape[0]
    q4 = stacked(q_ref[...])
    p = probabilities(q4, k_ref[...], table_ref[0], rows).astype(bf16)
    out_ref[...] = unstacked(matmul(p, v_ref[...]), rows).astype(bf16)


def attend_back_kernel(q_ref, k_ref, v_ref, table_ref, d_ref, dq_ref, dk_ref, dv_ref):
    rows = q_ref.shape[0]
    q4 = stacked(q_ref[...])
    d4 = stacked(d_ref[...])
    p = probabilities(q4, k_ref[...], table_ref[0], rows)
    dp = times_transposed(d4, v_ref[...])
    ds = p * (dp - jnp.sum(p * dp, axis=-1, keepdims=True)) * HEAD_DIM ** (-0.5)
    ds = ds.astype(bf16)
    dq_ref[...] = unstacked(matmul(ds, k_ref[...]), rows).astype(bf16)
    dk_ref[...] = transposed_times(ds, q4).astype(bf16)
    dv_ref[...] = transposed_times(p.astype(bf16), d4).astype(bf16)


def attention_specs(rows, keys):
    per_row = pl.BlockSpec((rows, LANES), lambda m, h: (m, h))
    per_key = pl.BlockSpec((keys, LANES), lambda m, h: (m, h))
    table = pl.BlockSpec((1, rows, keys), lambda m, h: (m, 0, 0))
    return per_row, per_key, table


def attend(q, k, v, table):
    micro, rows, keys = table.shape
    per_row, per_key, per_table = attention_specs(rows, keys)
    return pl.pallas_call(
        attend_kernel,
        grid=(micro, q.shape[1] // LANES),
        in_specs=[per_row, per_key, per_key, per_table],
        out_specs=per_row,
        out_shape=jax.ShapeDtypeStruct(q.shape, bf16),
        compiler_params=pltpu.CompilerParams(vmem_limit_bytes=32 << 20),
        cost_estimate=pl.CostEstimate(
            flops=2 * q.shape[0] * keys * LANES * 2 * q.shape[1] // HEAD_DIM,
            bytes_accessed=4 * (q.size + k.size),
            transcendentals=table.size * q.shape[1] // HEAD_DIM,
        ),
        name="attend",
    )(q, k, v, table)


def attend_back(q, k, v, table, d):
    micro, rows, keys = table.shape
    per_row, per_key, per_table = attention_specs(rows, keys)
    return pl.pallas_call(
        attend_back_kernel,
        grid=(micro, q.shape[1] // LANES),
        in_specs=[per_row, per_key, per_key, per_table, per_row],
        out_specs=[per_row, per_key, per_key],
        out_shape=[
            jax.ShapeDtypeStruct(q.shape, bf16),
            jax.ShapeDtypeStruct(k.shape, bf16),
            jax.ShapeDtypeStruct(v.shape, bf16),
        ],
        compiler_params=pltpu.CompilerParams(vmem_limit_bytes=48 << 20),
        cost_estimate=pl.CostEstimate(
            flops=5 * q.shape[0] * keys * LANES * 2 * q.shape[1] // HEAD_DIM,
            bytes_accessed=6 * (q.size + k.size),
            transcendentals=table.size * q.shape[1] // HEAD_DIM,
        ),
        name="attend_back",
    )(q, k, v, table, d)


def patch_tables(lengths, documents):
    patches, count = lengths.shape[1], documents.shape[1]
    ends = jnp.cumsum(lengths, axis=1, dtype=jnp.int32)
    starts = ends - lengths
    position = lax.broadcasted_iota(jnp.int32, (1, patches, count), 2)
    member = (position >= starts[:, :, None]) & (position < ends[:, :, None])
    first_doc = jnp.sum(
        jnp.where(position == starts[:, :, None], documents[:, None, :], 0), axis=2
    )
    allowed = member & (documents[:, None, :] == first_doc[:, :, None])
    order_rows = lax.broadcasted_iota(jnp.int32, (1, patches, patches), 1)
    order_cols = lax.broadcasted_iota(jnp.int32, (1, patches, patches), 2)
    causal = (order_cols <= order_rows) & (first_doc[:, None, :] == first_doc[:, :, None])
    return member.astype(bf16), allowed.astype(f32), causal.astype(f32)


def swapped(x):
    half = x.shape[0] // 2
    return jnp.concatenate([x[half:], x[:half]], axis=0)


def own_first(pair, section):
    return jnp.where(section == 0, pair, pair[::-1])


def both_halves(own, section):
    other = across(swapped(own))
    return jnp.where(
        section == 0,
        jnp.concatenate([own, other], axis=1),
        jnp.concatenate([other, own], axis=1),
    )


def core_sum(partial):
    return partial + across(swapped(partial.astype(bf16))).astype(f32)


def shards(
    byte_states,
    patch_lengths,
    doc_ids,
    proj_weights,
    out_weights,
    norm_gains,
    in_weights,
    down_weights,
    cotangent,
):
    section = lax.axis_index("section")
    width = byte_states.shape[-1]
    half = width // 2
    units = down_weights.shape[1]

    ffn = jnp.concatenate([in_weights[0], in_weights[1], down_weights], axis=1)
    ffn = lax.all_gather(ffn, "fsdp", axis=0, tiled=True)
    w_gate, w_up, w_down = ffn[:, :units], ffn[:, units : 2 * units], ffn[:, 2 * units :]

    own_w = jnp.concatenate([proj_weights[0], out_weights], axis=0)
    own_w = own_w.transpose(1, 0, 2).reshape(16, 4, 2, half)
    gains_own = jnp.pad(norm_gains[0].T, ((0, 0), (0, 126)))
    keep = jnp.where(section == 0, own_w[:, :, 0], own_w[:, :, 1]).reshape(16, 4 * half)
    give = jnp.where(section == 0, own_w[:, :, 1], own_w[:, :, 0]).reshape(16, 4 * half)
    keep = jnp.concatenate([keep, gains_own], axis=1)
    got = across(jnp.concatenate([give, gains_own], axis=1))
    enc = jnp.where(section == 0, keep, got)
    glob = jnp.where(section == 0, got, keep)

    def of(shard, *names):
        cut = {n: (k * half, (k + 1) * half) for k, n in enumerate("qkvo")}
        cut["g"] = (4 * half, 4 * half + 128)
        return [shard[:, cut[n][0] : cut[n][1]] for n in names]

    pack = jnp.concatenate(
        of(enc, *"kvg") + of(glob, *"kvg") + of(enc, *"qo") + of(glob, *"qo"), axis=1
    )
    first = 2 * (2 * half + 128)
    pack = gather_direct(pack[None], "z", 0).reshape(64, -1)
    on_y, on_x = pack[:, :first], pack[:, first:]
    on_y = gather_direct(on_y[None], "x", 0).reshape(256, -1)
    on_x = gather_direct(on_x[None], "y", 0)
    enc_kv = gather_ring(on_y[None, :, : first // 2], "y", 0).reshape(width, -1)
    enc_qo = gather_ring(on_x[:, None, :, : 2 * half], "x", 1).reshape(width, -1)
    glob_kv = gather_ring(on_y[None, :, first // 2 :], "y", 0).reshape(width, -1)
    glob_qo = gather_ring(on_x[:, None, :, 2 * half :], "x", 1).reshape(width, -1)
    wq0, wo0 = enc_qo[:, :half], enc_qo[:, half:]
    wk0, wv0, gains0 = enc_kv[:, :half], enc_kv[:, half : 2 * half], enc_kv[:, 2 * half :]
    wq1, wo1 = glob_qo[:, :half], glob_qo[:, half:]
    wk1, wv1, gains1 = glob_kv[:, :half], glob_kv[:, half : 2 * half], glob_kv[:, 2 * half :]
    gains0 = gains0.astype(f32).T[:2]
    gains1 = gains1.astype(f32).T[:2]
    wo0_other, wo1_other = across(wo0), across(wo1)

    def times_out(x, own, other):
        mine, theirs = matmul(x, own), matmul(x, other)
        return jnp.concatenate(
            [jnp.where(section == 0, mine, theirs), jnp.where(section == 0, theirs, mine)], axis=1
        )

    def column_half(x, which):
        return lax.dynamic_slice_in_dim(x, which * half, half, 1)

    def times_out_back(d, own, other):
        rows = [lax.dynamic_slice_in_dim(w, section * half, half, 0) for w in (own, other)]
        return times_transposed(column_half(d, section), rows[0]) + times_transposed(
            column_half(d, 1 - section), rows[1]
        )

    own_bytes, own_target = byte_states[0, 0], cotangent[0, 0]
    raw = jnp.concatenate([own_bytes, across(own_bytes)], axis=0)
    target = jnp.concatenate([own_target, across(own_target)], axis=0)
    lengths = own_first(patch_lengths[:, 0], section)
    documents = own_first(doc_ids[:, 0], section)
    patches, count = lengths.shape[1], documents.shape[1]
    member, allowed, causal = patch_tables(lengths, documents)
    size = lengths.astype(f32).reshape(-1, 1)

    raw_f32 = raw.astype(f32)
    pooled = lax.dot_general(
        member,
        raw.reshape(2, count, width),
        (((2,), (1,)), ((0,), (0,))),
        preferred_element_type=f32,
    ).reshape(2 * patches, width)
    pooled = pooled / size
    query_inv = inverse_rms(pooled)
    query_low = (pooled * query_inv * gains0[0]).astype(bf16)
    byte_inv = inverse_rms(raw_f32)
    byte_low = (raw_f32 * byte_inv * gains0[1]).astype(bf16)
    q0 = matmul(query_low, wq0).astype(bf16)
    k0 = matmul(byte_low, wk0).astype(bf16)
    v0 = matmul(byte_low, wv0).astype(bf16)
    mixed0 = both_halves(attend(q0, k0, v0, allowed), section)
    hidden = (pooled + times_out(mixed0, wo0, wo0_other)).astype(bf16).astype(f32)

    normed_inv = inverse_rms(hidden)
    normed_low = (hidden * normed_inv * gains1[0]).astype(bf16)
    q1 = matmul(normed_low, wq1).astype(bf16)
    k1 = matmul(normed_low, wk1).astype(bf16)
    v1 = matmul(normed_low, wv1).astype(bf16)
    mixed1 = both_halves(attend(q1, k1, v1, causal), section)
    middle = hidden + times_out(mixed1, wo1, wo1_other)
    ffn_inv = inverse_rms(middle)
    ffn_low = (middle * ffn_inv * gains1[1]).astype(bf16)
    gate = matmul(ffn_low, w_gate)
    up = matmul(ffn_low, w_up)
    sigma = jax.nn.sigmoid(gate)
    inner = (gate * sigma * up).astype(bf16)

    target_z = matmul(target, turned(width, "z", 0)).astype(bf16)
    turn_x = turned(width, "x", place("x"))
    turn_y = turned(width, "y", place("y"))
    turn_z = turned(width, "z", place("z"))
    byte_x = matmul(byte_low, turn_x).astype(bf16)
    query_z = matmul(query_low, turn_z).astype(bf16)
    mixed_z = matmul(mixed0, turn_z).astype(bf16)

    down_line = line_sum(transposed_times(target_z, inner).astype(bf16), "z")
    inner_grad = matmul(target, w_down)
    up_grad = (inner_grad * gate * sigma).astype(bf16)
    gate_grad = (inner_grad * up * sigma * (1.0 + gate * (1.0 - sigma))).astype(bf16)
    ffn_y = matmul(ffn_low, turn_y).astype(bf16)
    ffn_x = matmul(ffn_low, turn_x).astype(bf16)
    gate_far = far_parts(ffn_y, gate_grad)
    up_far = far_parts(ffn_x, up_grad)
    gate_far, up_far, gate_grad, up_grad = stage(gate_far, up_far, gate_grad, up_grad)

    gate_came, up_came = send_far(gate_far, "y"), send_far(up_far, "x")
    ffn_in_grad = core_sum(
        times_transposed(gate_grad, w_gate) + times_transposed(up_grad, w_up)
    )
    middle_grad = target.astype(f32) + normalize_back(middle, ffn_inv, gains1[1], ffn_in_grad)
    middle_low = middle_grad.astype(bf16)
    mixed_grad = times_out_back(middle_low, wo1, wo1_other).astype(bf16)
    gate_came, up_came, mixed_grad, middle_low = stage(gate_came, up_came, mixed_grad, middle_low)

    gate_near, up_near = near_parts(ffn_y, gate_grad, gate_came), near_parts(ffn_x, up_grad, up_came)
    gate_near, up_near, mixed_grad = stage(gate_near, up_near, mixed_grad)
    gate_came, up_came = send_near(gate_near, "y"), send_near(up_near, "x")
    dq, dk, dv = attend_back(q1, k1, v1, causal, mixed_grad)
    dqkv = jnp.concatenate([dq, dk, dv], axis=1)
    glob_grads = jnp.concatenate(
        [
            transposed_times(normed_low, dqkv).astype(bf16),
            transposed_times(mixed1, column_half(middle_low, section)).astype(bf16),
        ],
        axis=1,
    )
    normed_grad = core_sum(
        times_transposed(dq, wq1) + times_transposed(dk, wk1) + times_transposed(dv, wv1)
    )
    hidden_grad = middle_grad + normalize_back(hidden, normed_inv, gains1[0], normed_grad)
    embed_grad = hidden_grad.astype(bf16)
    gate_came, up_came, glob_grads, embed_grad = stage(gate_came, up_came, glob_grads, embed_grad)

    glob_line = line_sum(glob_grads, "y")
    gate_line = line_total(ffn_y, gate_grad, gate_came)
    up_line = line_total(ffn_x, up_grad, up_came)
    gate_sum = plane_sum(gate_line, "y")
    mixed_grad = times_out_back(embed_grad, wo0, wo0_other).astype(bf16)
    dq, dk, dv = attend_back(q0, k0, v0, allowed, mixed_grad)
    dkv = jnp.concatenate([dk, dv], axis=1)
    embed_half = column_half(embed_grad, section)
    kv_far = far_parts(byte_x, dkv)
    q_far, o_far = far_parts(query_z, dq), far_parts(mixed_z, embed_half)
    qo_far = tuple(jnp.concatenate(p, axis=1) for p in zip(q_far, o_far))
    gate_sum, kv_far, qo_far, dq, dkv, up_line = stage(gate_sum, kv_far, qo_far, dq, dkv, up_line)

    def own_share(partial):
        rows = partial.shape[0] // 2
        return partial[:rows] + across(partial[rows:].astype(bf16)).astype(f32)

    kv_came, qo_came = send_far(kv_far, "x"), send_far(qo_far, "z")
    up_sum = plane_sum(up_line, "x")
    dk, dv = dkv[:, :half], dkv[:, half:]
    query_in_grad = own_share(times_transposed(dq, wq0))
    byte_in_grad = own_share(times_transposed(dk, wk0) + times_transposed(dv, wv0))
    kv_came, qo_came, up_sum, down_line, query_in_grad, byte_in_grad = stage(
        kv_came, qo_came, up_sum, down_line, query_in_grad, byte_in_grad
    )

    kv_near = near_parts(byte_x, dkv, kv_came)
    q_part = tuple(x[:, : x.shape[1] // 2] for x in qo_came)
    o_part = tuple(x[:, x.shape[1] // 2 :] for x in qo_came)
    q_near, o_near = near_parts(query_z, dq, q_part), near_parts(mixed_z, embed_half, o_part)
    qo_near = tuple(jnp.concatenate(p, axis=1) for p in zip(q_near, o_near))
    kv_near, qo_near = stage(kv_near, qo_near)
    kv_came, qo_came = send_near(kv_near, "x"), send_near(qo_near, "z")
    down_sum = plane_sum(down_line, "z")
    pooled_grad = embed_grad[:patches].astype(f32) + normalize_back(
        pooled[:patches], query_inv[:patches], gains0[0], query_in_grad
    )
    share = pooled_grad / size[:patches]
    share_high = share.astype(bf16)
    share_low = (share - share_high.astype(f32)).astype(bf16)
    spread = transposed_times(member[0], share_high) + transposed_times(member[0], share_low)
    byte_grad = spread + normalize_back(
        raw_f32[:count], byte_inv[:count], gains0[1], byte_in_grad
    )

    def gain_grad(values, inverse, gradient):
        rows = gradient.shape[0]
        return jnp.sum(gradient * (values[:rows] * inverse[:rows]), axis=0)

    gain_parts = jnp.stack(
        [
            gain_grad(pooled, query_inv, query_in_grad),
            gain_grad(raw_f32, byte_inv, byte_in_grad),
            gain_grad(hidden, normed_inv, normed_grad[:patches]),
            gain_grad(middle, ffn_inv, ffn_in_grad[:patches]),
        ]
    )
    gain_parts = gain_parts.reshape(2, 2, 64, 16).transpose(0, 2, 1, 3).reshape(128, 2, 16)
    result = times_transposed(inner, w_down)
    block_out = middle[:patches] + result[:patches]
    block_out = block_out + across(result[patches:].astype(bf16)).astype(f32)
    kv_came, qo_came, gain_parts, down_sum, byte_grad, block_out, glob_line = stage(
        kv_came, qo_came, gain_parts, down_sum, byte_grad, block_out, glob_line
    )

    kv_line = line_total(byte_x, dkv, kv_came)
    q_part = tuple(x[:, :half] for x in qo_came)
    o_part = tuple(x[:, half:] for x in qo_came)
    qo_line = jnp.concatenate(
        [line_total(query_z, dq, q_part), line_total(mixed_z, embed_half, o_part)], axis=1
    )
    glob_sum = plane_sum(glob_line[:, :], "y")
    kv_sum = plane_sum(kv_line, "x")
    qo_sum = plane_sum(qo_line, "z")
    gain_parts = lax.all_to_all(gain_parts, ("section", "fsdp"), 0, 0, tiled=True)
    gain_sum = jnp.sum(gain_parts, axis=0)

    kq, kv = jnp.split(kv_sum, 2, axis=1)
    qq, qo = jnp.split(qo_sum, 2, axis=1)
    enc_sum = jnp.stack([qq, kq, kv, qo])
    glob_sum = jnp.stack(jnp.split(glob_sum, 4, axis=1))
    mine = jnp.where(section == 0, enc_sum, glob_sum)
    theirs = across(jnp.where(section == 0, glob_sum, enc_sum))
    sums = jnp.where(
        section == 0,
        jnp.concatenate([mine, theirs], axis=2),
        jnp.concatenate([theirs, mine], axis=2),
    )
    return (
        block_out[None, None],
        byte_grad[None, None],
        sums[None, :3],
        sums[3:],
        gain_sum[None],
        jnp.stack([gate_sum, up_sum]),
        down_sum,
    )


def solution(mesh):
    in_specs = (
        P("section", "fsdp", None, None),
        P(None, "fsdp", None),
        P(None, "fsdp", None),
        P("section", None, "fsdp", None),
        P("section", "fsdp", None),
        P("section", None, "fsdp"),
        P(None, "fsdp", "section"),
        P("fsdp", "section"),
        P("section", "fsdp", None, None),
    )
    out_specs = (
        P("section", "fsdp", None, None),
        P("section", "fsdp", None, None),
        P("section", None, "fsdp", None),
        P("section", "fsdp", None),
        P("section", None, "fsdp"),
        P(None, "fsdp", "section"),
        P("fsdp", "section"),
    )
    return jax.shard_map(shards, mesh=mesh, in_specs=in_specs, out_specs=out_specs, check_vma=False)
```

```python
import jax
import jax.numpy as jnp
from jax import lax
from jax.experimental import pallas as pl
from jax.experimental.pallas import tpu as pltpu
from jax.sharding import PartitionSpec as P

HEADS = 16
HEAD_DIM = 64
QUAD = 4
LANES = QUAD * HEAD_DIM
RING = 4
STRIDE = {"y": 16, "x": 4, "z": 1}

epsilon = 1e-05
masked_score = -1e30
bf16 = jnp.bfloat16
f32 = jnp.float32


def across(block):
    return lax.ppermute(block, "section", [(0, 1), (1, 0)])


def shift(block, ax, by):
    step = STRIDE[ax]

    def to(i):
        c = (i // step) % RING
        return i + ((c + by) % RING - c) * step

    return lax.ppermute(block, "fsdp", [(i, to(i)) for i in range(64)])


def place(ax):
    return (lax.axis_index("fsdp") // STRIDE[ax]) % RING


def plane(ax):
    rows = {}
    for i in range(64):
        rows.setdefault((i // STRIDE[ax]) % RING, []).append(i)
    return [rows[c] for c in range(RING)]


def line(ax):
    rows = {}
    for i in range(64):
        c = (i // STRIDE[ax]) % RING
        rows.setdefault(i - c * STRIDE[ax], []).append(i)
    return list(rows.values())


def put(whole, piece, at, dim):
    where = [0] * whole.ndim
    where[dim] = at
    return lax.dynamic_update_slice(whole, piece, where)


def gather_direct(block, ax, dim):
    c = place(ax)
    whole = jnp.zeros((*block.shape[:dim], RING, *block.shape[dim + 1 :]), block.dtype)
    arrived = [(shift(block, ax, by), (c - by) % RING) for by in (1, -1, 2)]
    for piece, at in [(block, c)] + arrived:
        whole = put(whole, piece, at, dim)
    return whole


def ring_pieces(block, ax):
    half = block.shape[-1] // 256 * 128
    last = block.ndim - 1
    below, above = shift(block, ax, 1), shift(block, ax, -1)
    first = shift(lax.slice_in_dim(below, 0, half, axis=last), ax, 1)
    second = shift(lax.slice_in_dim(above, half, None, axis=last), ax, -1)
    return block, above, below, first, second


def lay_kernel(c_ref, *refs):
    ins, outs = refs[:10], refs[10:]
    for ax, pieces, targets in (("y", ins[:5], outs[:3]), ("x", ins[5:], outs[3:])):
        c = c_ref[0 if ax == "y" else 1]
        half = pieces[3].shape[-1]
        for k, piece in ((0, pieces[0]), (1, pieces[1]), (3, pieces[2])):
            at = lax.rem(c + k, RING)
            column = 0
            for out in targets:
                wide = out.shape[-1]
                value = piece[..., column : column + wide]
                if ax == "y":
                    out[at] = value
                else:
                    out[:, at] = value
                column += wide
        at = lax.rem(c + 2, RING)
        column = 0
        for out in targets:
            wide = out.shape[-1]
            source = pieces[3] if column < half else pieces[4]
            begin = column if column < half else column - half
            value = source[..., begin : begin + wide]
            if ax == "y":
                out[at] = value
            else:
                out[:, at] = value
            column += wide


def lay(places, on_y, on_x, half):
    rows = on_y[0].shape[0]
    block = rows // RING
    wide = (half, half, on_y[0].shape[1] - 2 * half)
    outs = [jax.ShapeDtypeStruct((RING, rows, w), bf16) for w in wide]
    outs += [jax.ShapeDtypeStruct((RING, RING, block, half), bf16)] * 2
    made = pl.pallas_call(
        lay_kernel,
        in_specs=[pl.BlockSpec(memory_space=pltpu.SMEM)] + [pl.BlockSpec(memory_space=pltpu.VMEM)] * 10,
        out_specs=[pl.BlockSpec(memory_space=pltpu.VMEM)] * 5,
        out_shape=outs,
        compiler_params=pltpu.CompilerParams(vmem_limit_bytes=32 << 20),
        cost_estimate=pl.CostEstimate(flops=0, bytes_accessed=10 << 20, transcendentals=0),
        name="lay",
    )(places, *on_y, *on_x)
    return [m.reshape(RING * rows, m.shape[-1]) for m in made]


def quarters_kernel(ax, c_ref, x_ref, d_ref, *refs):
    outs, turned = refs[:-1], refs[-1]
    features, block = x_ref.shape[1], x_ref.shape[1] // 64
    turned[...] = x_ref[...].T.reshape(turned.shape)
    c = c_ref[0]
    for k in range(RING):
        at = lax.rem(c + k, RING)
        if ax == "y":
            rows = turned[at]
        elif ax == "x":
            rows = turned[:, at]
        else:
            rows = turned[:, :, at]
        rows = rows.reshape(features // RING, x_ref.shape[0])
        value = matmul(rows, d_ref[...]).astype(bf16)
        if len(outs) == 1:
            outs[0][k] = value
        else:
            outs[k][...] = value


def quarters(x, d, ax, first=None):
    tokens, features = x.shape
    shape = (features // RING, d.shape[1])
    if first is None:
        outs = [jax.ShapeDtypeStruct((RING, *shape), bf16)]
        first = jnp.int32(0)
    else:
        outs = [jax.ShapeDtypeStruct(shape, bf16)] * RING
    made = pl.pallas_call(
        lambda *refs: quarters_kernel(ax, *refs),
        in_specs=[pl.BlockSpec(memory_space=pltpu.SMEM)] + [pl.BlockSpec(memory_space=pltpu.VMEM)] * 2,
        out_specs=[pl.BlockSpec(memory_space=pltpu.VMEM)] * len(outs),
        out_shape=outs,
        scratch_shapes=[pltpu.VMEM((RING, RING, RING, features // 64, tokens), bf16)],
        compiler_params=pltpu.CompilerParams(vmem_limit_bytes=32 << 20),
        cost_estimate=pl.CostEstimate(
            flops=2 * x.size * d.shape[1],
            bytes_accessed=2 * (x.size + d.size + features * d.shape[1]),
            transcendentals=0,
        ),
        name="quarters_" + ax,
    )(first.reshape(1), x, d)
    return made[0] if len(outs) == 1 else made


def send_quarters(parts, ax):
    return shift(parts[1], ax, 1), shift(parts[3], ax, -1), shift(parts[2], ax, 2)


def line_total(own, arrived):
    total = own.astype(f32)
    for part in arrived:
        total = total + part.astype(f32)
    return total.astype(bf16)


def line_sum(parts, ax):
    return lax.psum_scatter(
        parts, "fsdp", scatter_dimension=0, axis_index_groups=line(ax), tiled=False
    )


def plane_sum(part, ax):
    blocks = part.reshape(16, part.shape[0] // 16, part.shape[1])
    blocks = lax.all_to_all(blocks, "fsdp", 0, 0, axis_index_groups=plane(ax), tiled=True)
    return jnp.sum(blocks.astype(f32), axis=0)


def stage(*values):
    return lax.optimization_barrier(values)


def inverse_rms(values):
    return lax.rsqrt(jnp.mean(values * values, axis=-1, keepdims=True) + epsilon)


def normalize_back(values, inverse, scales, gradient):
    unit_rows = values * inverse
    scaled = gradient * scales
    inner_mean = jnp.mean(scaled * unit_rows, axis=-1, keepdims=True)
    return inverse * (scaled - unit_rows * inner_mean)


def matmul(left, right):
    return jnp.dot(left, right, preferred_element_type=f32)


def times_transposed(left, right):
    return lax.dot_general(left, right, (((1,), (1,)), ((), ())), preferred_element_type=f32)


def transposed_times(left, right):
    return lax.dot_general(left, right, (((0,), (0,)), ((), ())), preferred_element_type=f32)


def of_head(value, h):
    head = lax.broadcasted_iota(jnp.int32, value.shape, 1) // HEAD_DIM
    return jnp.where(head == h, value, jnp.zeros_like(value))


def stacked(value):
    return jnp.concatenate([of_head(value, h) for h in range(QUAD)], axis=0)


def unstacked(value, rows):
    total = of_head(value[:rows], 0)
    for h in range(1, QUAD):
        total = total + of_head(value[h * rows : (h + 1) * rows], h)
    return total


def probabilities(q4, keys, table, rows):
    raw = times_transposed(q4, keys)
    allowed = jnp.concatenate([table] * QUAD, axis=0) > 0
    scores = jnp.where(allowed, raw * HEAD_DIM ** (-0.5), masked_score)
    weights = jnp.exp(scores - jnp.max(scores, axis=-1, keepdims=True))
    return weights / jnp.sum(weights, axis=-1, keepdims=True)


def attend_kernel(q_ref, k_ref, v_ref, table_ref, out_ref):
    rows = q_ref.shape[0]
    q4 = stacked(q_ref[...])
    p = probabilities(q4, k_ref[...], table_ref[0], rows).astype(bf16)
    out_ref[...] = unstacked(matmul(p, v_ref[...]), rows).astype(bf16)


def attend_back_kernel(q_ref, k_ref, v_ref, table_ref, d_ref, dq_ref, dk_ref, dv_ref):
    rows = q_ref.shape[0]
    q4 = stacked(q_ref[...])
    d4 = stacked(d_ref[...])
    p = probabilities(q4, k_ref[...], table_ref[0], rows)
    dp = times_transposed(d4, v_ref[...])
    ds = p * (dp - jnp.sum(p * dp, axis=-1, keepdims=True)) * HEAD_DIM ** (-0.5)
    ds = ds.astype(bf16)
    dq_ref[...] = unstacked(matmul(ds, k_ref[...]), rows).astype(bf16)
    dk_ref[...] = transposed_times(ds, q4).astype(bf16)
    dv_ref[...] = transposed_times(p.astype(bf16), d4).astype(bf16)


def attention_specs(rows, keys):
    per_row = pl.BlockSpec((rows, LANES), lambda m, h: (m, h))
    per_key = pl.BlockSpec((keys, LANES), lambda m, h: (m, h))
    table = pl.BlockSpec((1, rows, keys), lambda m, h: (m, 0, 0))
    return per_row, per_key, table


def attend(q, k, v, table):
    micro, rows, keys = table.shape
    per_row, per_key, per_table = attention_specs(rows, keys)
    return pl.pallas_call(
        attend_kernel,
        grid=(micro, q.shape[1] // LANES),
        in_specs=[per_row, per_key, per_key, per_table],
        out_specs=per_row,
        out_shape=jax.ShapeDtypeStruct(q.shape, bf16),
        compiler_params=pltpu.CompilerParams(vmem_limit_bytes=32 << 20),
        cost_estimate=pl.CostEstimate(
            flops=2 * q.shape[0] * keys * LANES * 2 * q.shape[1] // HEAD_DIM,
            bytes_accessed=4 * (q.size + k.size),
            transcendentals=table.size * q.shape[1] // HEAD_DIM,
        ),
        name="attend",
    )(q, k, v, table)


def attend_back(q, k, v, table, d):
    micro, rows, keys = table.shape
    per_row, per_key, per_table = attention_specs(rows, keys)
    return pl.pallas_call(
        attend_back_kernel,
        grid=(micro, q.shape[1] // LANES),
        in_specs=[per_row, per_key, per_key, per_table, per_row],
        out_specs=[per_row, per_key, per_key],
        out_shape=[
            jax.ShapeDtypeStruct(q.shape, bf16),
            jax.ShapeDtypeStruct(k.shape, bf16),
            jax.ShapeDtypeStruct(v.shape, bf16),
        ],
        compiler_params=pltpu.CompilerParams(vmem_limit_bytes=48 << 20),
        cost_estimate=pl.CostEstimate(
            flops=5 * q.shape[0] * keys * LANES * 2 * q.shape[1] // HEAD_DIM,
            bytes_accessed=6 * (q.size + k.size),
            transcendentals=table.size * q.shape[1] // HEAD_DIM,
        ),
        name="attend_back",
    )(q, k, v, table, d)


def patch_tables(lengths, documents):
    patches, count = lengths.shape[1], documents.shape[1]
    ends = jnp.cumsum(lengths, axis=1, dtype=jnp.int32)
    starts = ends - lengths
    position = lax.broadcasted_iota(jnp.int32, (1, patches, count), 2)
    member = (position >= starts[:, :, None]) & (position < ends[:, :, None])
    first_doc = jnp.sum(
        jnp.where(position == starts[:, :, None], documents[:, None, :], 0), axis=2
    )
    allowed = member & (documents[:, None, :] == first_doc[:, :, None])
    order_rows = lax.broadcasted_iota(jnp.int32, (1, patches, patches), 1)
    order_cols = lax.broadcasted_iota(jnp.int32, (1, patches, patches), 2)
    causal = (order_cols <= order_rows) & (first_doc[:, None, :] == first_doc[:, :, None])
    return member.astype(bf16), allowed.astype(f32), causal.astype(f32)


def swapped(x):
    half = x.shape[0] // 2
    return jnp.concatenate([x[half:], x[:half]], axis=0)


def own_first(pair, section):
    return jnp.where(section == 0, pair, pair[::-1])


def both_halves(own, section):
    other = across(swapped(own))
    return jnp.where(
        section == 0,
        jnp.concatenate([own, other], axis=1),
        jnp.concatenate([other, own], axis=1),
    )


def core_sum(partial):
    return partial + across(swapped(partial.astype(bf16))).astype(f32)


def shards(
    byte_states,
    patch_lengths,
    doc_ids,
    proj_weights,
    out_weights,
    norm_gains,
    in_weights,
    down_weights,
    cotangent,
):
    section = lax.axis_index("section")
    width = byte_states.shape[-1]
    half = width // 2
    units = down_weights.shape[1]

    ffn = jnp.concatenate([in_weights[0], in_weights[1], down_weights], axis=1)
    ffn = lax.all_gather(ffn, "fsdp", axis=0, tiled=True)
    w_gate, w_up, w_down = ffn[:, :units], ffn[:, units : 2 * units], ffn[:, 2 * units :]

    own_w = jnp.concatenate([proj_weights[0], out_weights], axis=0)
    own_w = own_w.transpose(1, 0, 2).reshape(16, 4, 2, half)
    gains_own = jnp.pad(norm_gains[0].T, ((0, 0), (0, 126)))
    keep = jnp.where(section == 0, own_w[:, :, 0], own_w[:, :, 1]).reshape(16, 4 * half)
    give = jnp.where(section == 0, own_w[:, :, 1], own_w[:, :, 0]).reshape(16, 4 * half)
    keep = jnp.concatenate([keep, gains_own], axis=1)
    got = across(jnp.concatenate([give, gains_own], axis=1))
    enc = jnp.where(section == 0, keep, got)
    glob = jnp.where(section == 0, got, keep)

    def of(shard, *names):
        cut = {n: (k * half, (k + 1) * half) for k, n in enumerate("qkvo")}
        cut["g"] = (4 * half, 4 * half + 128)
        return [shard[:, cut[n][0] : cut[n][1]] for n in names]

    pack = jnp.concatenate(
        of(enc, *"kvg") + of(glob, *"kvg") + of(enc, *"qo") + of(glob, *"qo"), axis=1
    )
    first = 2 * (2 * half + 128)
    pack = gather_direct(pack[None], "z", 0).reshape(64, -1)
    on_y, on_x = pack[:, :first], pack[:, first:]
    on_y = gather_direct(on_y[None], "x", 0).reshape(256, -1)
    on_x = gather_direct(on_x[None], "y", 0)
    places = jnp.stack([place("y"), place("x")])
    enc_y = ring_pieces(on_y[:, : first // 2], "y")
    enc_x = ring_pieces(on_x[..., : 2 * half], "x")
    glob_y = ring_pieces(on_y[:, first // 2 :], "y")
    glob_x = ring_pieces(on_x[..., 2 * half :], "x")
    wk0, wv0, gains0, wq0, wo0 = lay(places, enc_y, enc_x, half)
    wk1, wv1, gains1, wq1, wo1 = lay(places, glob_y, glob_x, half)
    pick = (
        lax.broadcasted_iota(jnp.int32, (8, 128), 0) == lax.broadcasted_iota(jnp.int32, (8, 128), 1)
    ).astype(bf16)
    gains0, gains1 = times_transposed(pick, gains0), times_transposed(pick, gains1)
    wo0_other, wo1_other = across(wo0), across(wo1)

    def times_out(x, own, other):
        mine, theirs = matmul(x, own), matmul(x, other)
        return jnp.concatenate(
            [jnp.where(section == 0, mine, theirs), jnp.where(section == 0, theirs, mine)], axis=1
        )

    def column_half(x, which):
        return lax.dynamic_slice_in_dim(x, which * half, half, 1)

    def times_out_back(d, own, other):
        rows = [lax.dynamic_slice_in_dim(w, section * half, half, 0) for w in (own, other)]
        return times_transposed(column_half(d, section), rows[0]) + times_transposed(
            column_half(d, 1 - section), rows[1]
        )

    own_bytes, own_target = byte_states[0, 0], cotangent[0, 0]
    raw = jnp.concatenate([own_bytes, across(own_bytes)], axis=0)
    target = jnp.concatenate([own_target, across(own_target)], axis=0)
    lengths = own_first(patch_lengths[:, 0], section)
    documents = own_first(doc_ids[:, 0], section)
    patches, count = lengths.shape[1], documents.shape[1]
    member, allowed, causal = patch_tables(lengths, documents)
    size = lengths.astype(f32).reshape(-1, 1)

    raw_f32 = raw.astype(f32)
    pooled = lax.dot_general(
        member,
        raw.reshape(2, count, width),
        (((2,), (1,)), ((0,), (0,))),
        preferred_element_type=f32,
    ).reshape(2 * patches, width)
    pooled = pooled / size
    query_inv = inverse_rms(pooled)
    query_low = (pooled * query_inv * gains0[0]).astype(bf16)
    byte_inv = inverse_rms(raw_f32)
    byte_low = (raw_f32 * byte_inv * gains0[1]).astype(bf16)
    q0 = matmul(query_low, wq0).astype(bf16)
    k0 = matmul(byte_low, wk0).astype(bf16)
    v0 = matmul(byte_low, wv0).astype(bf16)
    mixed0 = both_halves(attend(q0, k0, v0, allowed), section)
    hidden = (pooled + times_out(mixed0, wo0, wo0_other)).astype(bf16).astype(f32)

    normed_inv = inverse_rms(hidden)
    normed_low = (hidden * normed_inv * gains1[0]).astype(bf16)
    q1 = matmul(normed_low, wq1).astype(bf16)
    k1 = matmul(normed_low, wk1).astype(bf16)
    v1 = matmul(normed_low, wv1).astype(bf16)
    mixed1 = both_halves(attend(q1, k1, v1, causal), section)
    middle = hidden + times_out(mixed1, wo1, wo1_other)
    ffn_inv = inverse_rms(middle)
    ffn_low = (middle * ffn_inv * gains1[1]).astype(bf16)
    gate = matmul(ffn_low, w_gate)
    up = matmul(ffn_low, w_up)
    sigma = jax.nn.sigmoid(gate)
    inner = (gate * sigma * up).astype(bf16)

    down_line = line_sum(quarters(target, inner, "z"), "z")
    inner_grad = matmul(target, w_down)
    up_grad = (inner_grad * gate * sigma).astype(bf16)
    gate_grad = (inner_grad * up * sigma * (1.0 + gate * (1.0 - sigma))).astype(bf16)
    gate_parts = quarters(ffn_low, gate_grad, "y", place("y"))
    up_parts = quarters(ffn_low, up_grad, "x", place("x"))
    gate_parts, up_parts, gate_grad, up_grad = stage(gate_parts, up_parts, gate_grad, up_grad)

    gate_came, up_came = send_quarters(gate_parts, "y"), send_quarters(up_parts, "x")
    ffn_in_grad = core_sum(
        times_transposed(gate_grad, w_gate) + times_transposed(up_grad, w_up)
    )
    middle_grad = target.astype(f32) + normalize_back(middle, ffn_inv, gains1[1], ffn_in_grad)
    middle_low = middle_grad.astype(bf16)
    mixed_grad = times_out_back(middle_low, wo1, wo1_other).astype(bf16)
    dq, dk, dv = attend_back(q1, k1, v1, causal, mixed_grad)
    dqkv = jnp.concatenate([dq, dk, dv], axis=1)
    normed_grad = core_sum(
        times_transposed(dq, wq1) + times_transposed(dk, wk1) + times_transposed(dv, wv1)
    )
    hidden_grad = middle_grad + normalize_back(hidden, normed_inv, gains1[0], normed_grad)
    embed_grad = hidden_grad.astype(bf16)
    qkv_parts = quarters(normed_low, dqkv, "y")
    out_parts = quarters(mixed1, column_half(middle_low, section), "y")
    glob_line = line_sum(jnp.concatenate([qkv_parts, out_parts], axis=2), "y")
    gate_came, up_came, embed_grad = stage(gate_came, up_came, embed_grad)

    gate_line = line_total(gate_parts[0], gate_came)
    up_line = line_total(up_parts[0], up_came)
    gate_sum = plane_sum(gate_line, "y")
    mixed_grad = times_out_back(embed_grad, wo0, wo0_other).astype(bf16)
    dq, dk, dv = attend_back(q0, k0, v0, allowed, mixed_grad)
    kv_parts = quarters(byte_low, jnp.concatenate([dk, dv], axis=1), "x", place("x"))
    q_parts = quarters(query_low, dq, "z", place("z"))
    o_parts = quarters(mixed0, column_half(embed_grad, section), "z", place("z"))
    qo_parts = [jnp.concatenate(p, axis=1) for p in zip(q_parts, o_parts)]
    gate_sum, kv_parts, qo_parts, dq, dk, dv, up_line = stage(
        gate_sum, kv_parts, qo_parts, dq, dk, dv, up_line
    )

    def own_share(partial):
        rows = partial.shape[0] // 2
        return partial[:rows] + across(partial[rows:].astype(bf16)).astype(f32)

    kv_came, qo_came = send_quarters(kv_parts, "x"), send_quarters(qo_parts, "z")
    up_sum = plane_sum(up_line, "x")
    down_sum = plane_sum(down_line, "z")
    query_in_grad = own_share(times_transposed(dq, wq0))
    byte_in_grad = own_share(times_transposed(dk, wk0) + times_transposed(dv, wv0))
    pooled_grad = embed_grad[:patches].astype(f32) + normalize_back(
        pooled[:patches], query_inv[:patches], gains0[0], query_in_grad
    )
    share = pooled_grad / size[:patches]
    share_high = share.astype(bf16)
    share_low = (share - share_high.astype(f32)).astype(bf16)
    spread = transposed_times(member[0], share_high) + transposed_times(member[0], share_low)
    byte_grad = spread + normalize_back(
        raw_f32[:count], byte_inv[:count], gains0[1], byte_in_grad
    )
    result = times_transposed(inner, w_down)
    block_out = middle[:patches] + result[:patches]
    block_out = block_out + across(result[patches:].astype(bf16)).astype(f32)
    kv_came, qo_came, down_sum, up_sum, byte_grad, block_out, glob_line = stage(
        kv_came, qo_came, down_sum, up_sum, byte_grad, block_out, glob_line
    )

    kv_sum = plane_sum(line_total(kv_parts[0], kv_came), "x")
    qo_sum = plane_sum(line_total(qo_parts[0], qo_came), "z")
    glob_sum = plane_sum(glob_line, "y")

    kq, kv = jnp.split(kv_sum, 2, axis=1)
    qq, qo = jnp.split(qo_sum, 2, axis=1)
    enc_sum = jnp.stack([qq, kq, kv, qo])
    glob_sum = jnp.stack(jnp.split(glob_sum, 4, axis=1))
    mine = jnp.where(section == 0, enc_sum, glob_sum)
    theirs = across(jnp.where(section == 0, glob_sum, enc_sum))
    sums = jnp.where(
        section == 0,
        jnp.concatenate([mine, theirs], axis=2),
        jnp.concatenate([theirs, mine], axis=2),
    )
    def against(weight, grad):
        return jnp.sum(weight.astype(f32) * grad, axis=-1)

    own_dots = against(proj_weights[0], sums[:3])
    ffn_dots = against(in_weights[0], gate_sum) + against(in_weights[1], up_sum)
    ffn_dots = ffn_dots + across(ffn_dots)
    gain_sum = jnp.where(
        section == 0,
        jnp.stack([own_dots[0], own_dots[1] + own_dots[2]]),
        jnp.stack([own_dots[0] + own_dots[1] + own_dots[2], ffn_dots]),
    )
    gain_sum = gain_sum / norm_gains[0].astype(f32)
    return (
        block_out[None, None],
        byte_grad[None, None],
        sums[None, :3],
        sums[3:],
        gain_sum[None],
        jnp.stack([gate_sum, up_sum]),
        down_sum,
    )


def solution(mesh):
    in_specs = (
        P("section", "fsdp", None, None),
        P(None, "fsdp", None),
        P(None, "fsdp", None),
        P("section", None, "fsdp", None),
        P("section", "fsdp", None),
        P("section", None, "fsdp"),
        P(None, "fsdp", "section"),
        P("fsdp", "section"),
        P("section", "fsdp", None, None),
    )
    out_specs = (
        P("section", "fsdp", None, None),
        P("section", "fsdp", None, None),
        P("section", None, "fsdp", None),
        P("section", "fsdp", None),
        P("section", None, "fsdp"),
        P(None, "fsdp", "section"),
        P("fsdp", "section"),
    )
    return jax.shard_map(shards, mesh=mesh, in_specs=in_specs, out_specs=out_specs, check_vma=False)
```

```python
import functools

import jax
import jax.numpy as jnp
from jax import lax
from jax.experimental import pallas as pl
from jax.experimental.pallas import tpu as pltpu
from jax.sharding import PartitionSpec as P

HEADS = 16
HEAD_DIM = 64
QUAD = 4
LANES = QUAD * HEAD_DIM
RING = 4
STRIDE = {"y": 16, "x": 4, "z": 1}

FFN_AXES = ("y", "x")
ENC_AXES = ("x", "y")
GLOB_AXES = ("z", "z")

epsilon = 1e-05
masked_score = -1e30
bf16 = jnp.bfloat16
f32 = jnp.float32

SCALAR = pl.BlockSpec(memory_space=pltpu.SMEM)
WHOLE = pl.BlockSpec(memory_space=pltpu.VMEM)
ANYWHERE = pl.BlockSpec(memory_space=pl.ANY)
QUICK = pl.CostEstimate(flops=1, bytes_accessed=1, transcendentals=0)


def of(shape, kind):
    return jax.ShapeDtypeStruct(shape, kind)


def kernel_call(body, name, **options):
    return pl.pallas_call(
        body,
        name=name,
        cost_estimate=QUICK,
        compiler_params=pltpu.CompilerParams(vmem_limit_bytes=56 << 20),
        **options,
    )


def across(block):
    return lax.ppermute(block, "section", [(0, 1), (1, 0)])


def moved(i, ax, by):
    step = STRIDE[ax]
    c = (i // step) % RING
    return i + ((c + by) % RING - c) * step


def shift(block, ax, by):
    return lax.ppermute(block, "fsdp", [(i, moved(i, ax, by)) for i in range(64)])


def shift_by_core(block, axes, by):
    route = [(64 * s + i, 64 * s + moved(i, ax, by)) for s, ax in enumerate(axes) for i in range(64)]
    return lax.ppermute(block, ("section", "fsdp"), route)


def place(ax):
    return (lax.axis_index("fsdp") // STRIDE[ax]) % RING


def planes(axes):
    rows = {}
    for s, ax in enumerate(axes):
        for i in range(64):
            rows.setdefault((s, (i // STRIDE[ax]) % RING), []).append(64 * s + i)
    return list(rows.values())


def lines(axes):
    rows = {}
    for s, ax in enumerate(axes):
        for i in range(64):
            c = (i // STRIDE[ax]) % RING
            rows.setdefault((s, i - c * STRIDE[ax]), []).append(64 * s + i)
    return list(rows.values())


def put(whole, piece, at, dim):
    where = [0] * whole.ndim
    where[dim] = at
    return lax.dynamic_update_slice(whole, piece, where)


def gather_direct(block, ax, dim):
    c = place(ax)
    whole = jnp.zeros((*block.shape[:dim], RING, *block.shape[dim + 1 :]), block.dtype)
    arrived = [(shift(block, ax, by), (c - by) % RING) for by in (1, -1, 2)]
    for piece, at in [(block, c)] + arrived:
        whole = put(whole, piece, at, dim)
    return whole


def ring_pieces(block, ax):
    half = block.shape[-1] // 256 * 128
    last = block.ndim - 1
    below, above = shift(block, ax, 1), shift(block, ax, -1)
    first = shift(lax.slice_in_dim(below, 0, half, axis=last), ax, 1)
    second = shift(lax.slice_in_dim(above, half, None, axis=last), ax, -1)
    return block, above, below, first, second


def lay_kernel(c_ref, *refs):
    ins, outs = refs[:10], refs[10:]
    for ax, pieces, targets in (("y", ins[:5], outs[:3]), ("x", ins[5:], outs[3:])):
        c = c_ref[0 if ax == "y" else 1]
        half = pieces[3].shape[-1]
        for k in range(RING):
            at = lax.rem(c + k, RING)
            column = 0
            for out in targets:
                wide = out.shape[-1]
                if k == 2:
                    source = pieces[3] if column < half else pieces[4]
                    begin = column if column < half else column - half
                else:
                    source, begin = pieces[(0, 1, None, 2)[k]], column
                value = source[..., begin : begin + wide]
                if ax == "y":
                    out[at] = value
                else:
                    out[:, at] = value
                column += wide


def lay(places, on_y, on_x, half):
    rows = on_y[0].shape[0]
    wide = (half, half, on_y[0].shape[1] - 2 * half)
    outs = [of((RING, rows, w), bf16) for w in wide]
    outs += [of((RING, RING, rows // RING, half), bf16)] * 2
    made = kernel_call(
        lay_kernel,
        "lay",
        in_specs=[SCALAR] + [WHOLE] * 10,
        out_specs=[WHOLE] * 5,
        out_shape=outs,
    )(places, *on_y, *on_x)
    return [m.reshape(RING * rows, m.shape[-1]) for m in made]


def send_quarters(parts, axes):
    return [shift_by_core(parts[k], axes, by) for k, by in ((2, 2), (1, 1), (3, -1))]


def total_kernel(*refs):
    total = refs[0][...].astype(f32)
    for part in refs[1:-1]:
        total = total + part[...].astype(f32)
    refs[-1][...] = total.astype(bf16)


def line_total(*parts):
    return kernel_call(
        total_kernel,
        "line_total",
        in_specs=[WHOLE] * len(parts),
        out_specs=WHOLE,
        out_shape=of(parts[0].shape, bf16),
    )(*parts)


def near_kernel(up, down, a, b, up_out, down_out):
    cut = a.shape[1]
    up_out[:, :cut] = (up[:, :cut].astype(f32) + a[...].astype(f32)).astype(bf16)
    up_out[:, cut:] = up[:, cut:]
    down_out[:, cut:] = (down[:, cut:].astype(f32) + b[...].astype(f32)).astype(bf16)
    down_out[:, :cut] = down[:, :cut]


def near(up, down, a, b):
    return kernel_call(
        near_kernel,
        "near",
        in_specs=[WHOLE] * 4,
        out_specs=[WHOLE] * 2,
        out_shape=[of(up.shape, bf16)] * 2,
    )(up, down, a, b)


def line_sum(parts, axes):
    return lax.psum_scatter(
        parts,
        ("section", "fsdp"),
        scatter_dimension=0,
        axis_index_groups=lines(axes),
        tiled=False,
    )


def plane_sum(part, axes):
    blocks = part.reshape(16, part.shape[0] // 16, part.shape[1])
    blocks = lax.all_to_all(
        blocks, ("section", "fsdp"), 0, 0, axis_index_groups=planes(axes), tiled=True
    )
    return jnp.sum(blocks.astype(f32), axis=0)


def stage(*values):
    return lax.optimization_barrier(values)


def inverse_rms(values):
    return lax.rsqrt(jnp.mean(values * values, axis=-1, keepdims=True) + epsilon)


def normalize_back(values, inverse, scales, gradient):
    unit_rows = values * inverse
    scaled = gradient * scales
    inner_mean = jnp.mean(scaled * unit_rows, axis=-1, keepdims=True)
    return inverse * (scaled - unit_rows * inner_mean)


def matmul(left, right):
    return jnp.dot(left, right, preferred_element_type=f32)


def times_transposed(left, right):
    return lax.dot_general(left, right, (((1,), (1,)), ((), ())), preferred_element_type=f32)


def transposed_times(left, right):
    return lax.dot_general(left, right, (((0,), (0,)), ((), ())), preferred_element_type=f32)


def of_head(value, h):
    head = lax.broadcasted_iota(jnp.int32, value.shape, 1) // HEAD_DIM
    return jnp.where(head == h, value, jnp.zeros_like(value))


def stacked(value):
    return jnp.concatenate([of_head(value, h) for h in range(QUAD)], axis=0)


def unstacked(value, rows):
    total = of_head(value[:rows], 0)
    for h in range(1, QUAD):
        total = total + of_head(value[h * rows : (h + 1) * rows], h)
    return total


def probabilities(q4, keys, table):
    raw = times_transposed(q4, keys)
    allowed = jnp.concatenate([table] * QUAD, axis=0) > 0
    scores = jnp.where(allowed, raw * HEAD_DIM ** (-0.5), masked_score)
    weights = jnp.exp(scores - jnp.max(scores, axis=-1, keepdims=True))
    return weights / jnp.sum(weights, axis=-1, keepdims=True)


def attend(q, k, v, table):
    p = probabilities(stacked(q), k, table).astype(bf16)
    return unstacked(matmul(p, v), q.shape[0]).astype(bf16)


def attend_back(q, k, v, table, d):
    rows = q.shape[0]
    q4, d4 = stacked(q), stacked(d)
    p = probabilities(q4, k, table)
    dp = times_transposed(d4, v)
    ds = p * (dp - jnp.sum(p * dp, axis=-1, keepdims=True)) * HEAD_DIM ** (-0.5)
    ds = ds.astype(bf16)
    dq = unstacked(matmul(ds, k), rows).astype(bf16)
    dk = transposed_times(ds, q4).astype(bf16)
    dv = transposed_times(p.astype(bf16), d4).astype(bf16)
    return dq, dk, dv


def lanes_of(section, half):
    mine = pl.ds(pl.multiple_of(section * half, half), half)
    theirs = pl.ds(pl.multiple_of((1 - section) * half, half), half)
    return mine, theirs


def merge(scratch, section, own, other):
    mine, theirs = lanes_of(section, own.shape[1])
    scratch[:, mine] = own
    scratch[:, theirs] = other


def swap_rows(x):
    half = x.shape[0] // 2
    return jnp.concatenate([x[half:], x[:half]], axis=0)


def quarter(turned, ax, at):
    if ax == "y":
        rows = turned[at]
    elif ax == "x":
        rows = turned[:, at]
    else:
        rows = turned[:, :, at]
    return rows.reshape(turned.shape[0] ** 2 * turned.shape[3], turned.shape[4])


def fill_quarters(x_ref, turned, rows, s_ref, axes, first):
    turned[...] = x_ref[...].T.reshape(turned.shape)
    for s, ax in enumerate(axes):

        @pl.when(s_ref[0] == s)
        def _():
            c = s_ref[1 + "yxz".index(ax)] if first else 0
            for k in range(RING):
                rows[k] = quarter(turned, ax, lax.rem(c + k, RING))


def quarter_scratch(tokens, features):
    return [
        pltpu.VMEM((RING, RING, RING, features // RING**3, tokens), bf16),
        pltpu.VMEM((RING, features // RING, tokens), bf16),
    ]


def encoder_kernel(x_ref, b_ref, wq, wk, wv, table, q_ref, k_ref, v_ref, mixed, mixed_swapped):
    q = matmul(x_ref[...], wq[...]).astype(bf16)
    k = matmul(b_ref[...], wk[...]).astype(bf16)
    v = matmul(b_ref[...], wv[...]).astype(bf16)
    q_ref[...], k_ref[...], v_ref[...] = q, k, v
    out = attend(q, k, v, table[0])
    mixed[...] = out
    mixed_swapped[...] = out


def encoder_forward(query_low, byte_low, wq, wk, wv, table):
    micro, rows, keys = table.shape
    width, half = wq.shape
    weight = pl.BlockSpec((width, LANES), lambda h, m: (0, h))
    per_row = pl.BlockSpec((rows, LANES), lambda h, m: (m, h))
    per_key = pl.BlockSpec((keys, LANES), lambda h, m: (m, h))
    return kernel_call(
        encoder_kernel,
        "encoder_forward",
        grid=(half // LANES, micro),
        in_specs=[
            pl.BlockSpec((rows, width), lambda h, m: (m, 0)),
            pl.BlockSpec((keys, width), lambda h, m: (m, 0)),
            weight,
            weight,
            weight,
            pl.BlockSpec((1, rows, keys), lambda h, m: (m, 0, 0)),
        ],
        out_specs=[
            per_row,
            per_key,
            per_key,
            per_row,
            pl.BlockSpec((rows, LANES), lambda h, m: (1 - m, h)),
        ],
        out_shape=[
            of((micro * rows, half), bf16),
            of((micro * keys, half), bf16),
            of((micro * keys, half), bf16),
            of((micro * rows, half), bf16),
            of((micro * rows, half), bf16),
        ],
    )(query_low, byte_low, wq, wk, wv, table)


def global_kernel(
    s_ref, pooled, own, other, wo, wo_other, gains, wq, wk, wv, table,
    mixed_whole, hidden_ref, low_ref, q_ref, k_ref, v_ref, mixed, mixed_swapped,
):
    rows = table.shape[1]
    m = pl.program_id(1)

    @pl.when((pl.program_id(0) == 0) & (m == 0))
    def _():
        section = s_ref[0]
        merge(mixed_whole, section, own[...], other[...])
        whole = mixed_whole[...]
        merge(hidden_ref, section, matmul(whole, wo[...]), matmul(whole, wo_other[...]))
        hidden = (pooled[...] + hidden_ref[...]).astype(bf16).astype(f32)
        hidden_ref[...] = hidden
        low_ref[...] = (hidden * inverse_rms(hidden) * gains[2:3]).astype(bf16)

    here = pl.ds(pl.multiple_of(m * rows, rows), rows)
    x = low_ref[here]
    q = matmul(x, wq[...]).astype(bf16)
    k = matmul(x, wk[...]).astype(bf16)
    v = matmul(x, wv[...]).astype(bf16)
    q_ref[...], k_ref[...], v_ref[...] = q, k, v
    out = attend(q, k, v, table[0])
    mixed[...] = out
    mixed_swapped[...] = out


def global_forward(section, pooled, own, other, wo, wo_other, gains, packed, table):
    micro, rows, _ = table.shape
    width, half = wo.shape
    count = half // LANES
    per_row = pl.BlockSpec((rows, LANES), lambda h, m: (m, h))

    def weight(which):
        return pl.BlockSpec((width, LANES), lambda h, m: (0, which * count + h))

    def fixed(shape):
        return pl.BlockSpec(shape, lambda h, m: (0, 0))

    tokens = micro * rows
    return kernel_call(
        global_kernel,
        "global_forward",
        grid=(count, micro),
        in_specs=[
            SCALAR,
            fixed((tokens, width)),
            fixed((tokens, half)),
            fixed((tokens, half)),
            fixed((width, half)),
            fixed((width, half)),
            fixed(gains.shape),
            weight(0),
            weight(1),
            weight(2),
            pl.BlockSpec((1, rows, rows), lambda h, m: (m, 0, 0)),
        ],
        out_specs=[
            fixed((tokens, width)),
            fixed((tokens, width)),
            fixed((tokens, width)),
            per_row,
            per_row,
            per_row,
            per_row,
            pl.BlockSpec((rows, LANES), lambda h, m: (1 - m, h)),
        ],
        out_shape=[of((tokens, width), bf16), of((tokens, width), f32), of((tokens, width), bf16)]
        + [of((tokens, half), bf16)] * 5,
    )(section, pooled, own, other, wo, wo_other, gains, packed, packed, packed, table)


def ffn_kernel(
    units, at, axes, s_ref, hidden, own, other, wo, wo_other, gains, target, packed,
    mixed_whole, middle_ref, partial, partial_sent, result, result_sent, far_a, far_b, up_part,
    down_part, own_part, w_gate, w_up, w_down, turned, rows, turned_target, rows_target, sems,
):
    copies = [
        pltpu.make_async_copy(packed.at[:, pl.ds(at + k * units, units)], w, sems.at[k])
        for k, w in enumerate((w_gate, w_up, w_down))
    ]
    for copy in copies:
        copy.start()
    section = s_ref[0]
    merge(mixed_whole, section, own[...], other[...])
    whole = mixed_whole[...]
    merge(middle_ref, section, matmul(whole, wo[...]), matmul(whole, wo_other[...]))
    middle = hidden[...] + middle_ref[...]
    middle_ref[...] = middle
    low = (middle * inverse_rms(middle) * gains[3:4]).astype(bf16)
    copies[0].wait()
    gate = matmul(low, w_gate[...])
    copies[1].wait()
    up = matmul(low, w_up[...])
    sigma = jax.nn.sigmoid(gate)
    inner = (gate * sigma * up).astype(bf16)
    copies[2].wait()
    inner_grad = matmul(target[...], w_down[...])
    up_grad = (inner_grad * gate * sigma).astype(bf16)
    gate_grad = (inner_grad * up * sigma * (1.0 + gate * (1.0 - sigma))).astype(bf16)
    half = partial.shape[0] // 2
    total = times_transposed(gate_grad, w_gate[...]) + times_transposed(up_grad, w_up[...])
    partial[...] = total
    partial_sent[...] = swap_rows(total.astype(bf16))
    out = times_transposed(inner, w_down[...])
    result[...] = middle[:half] + out[:half]
    result_sent[...] = out[half:].astype(bf16)
    fill_quarters(low, turned, rows, s_ref, axes, True)
    fill_quarters(target, turned_target, rows_target, s_ref, axes, True)
    cut = far_a.shape[1]
    for k, part in ((0, own_part), (1, up_part), (2, None), (3, down_part)):
        for j, (x, d) in enumerate(((rows, gate_grad), (rows, up_grad), (rows_target, inner))):
            value = matmul(x[k], d).astype(bf16)
            begin, end = j * units, (j + 1) * units
            if part is not None:
                part[:, begin:end] = value
            elif end <= cut:
                far_a[:, begin:end] = value
            elif begin >= cut:
                far_b[:, begin - cut : end - cut] = value
            else:
                far_a[:, begin:] = value[:, : cut - begin]
                far_b[:, : end - cut] = value[:, cut - begin :]


def feed_forward(scalars, hidden, own, other, wo, wo_other, gains, target, packed, units, at, axes):
    tokens, width = hidden.shape
    rows = tokens // 2
    block = width // RING
    cut = 3 * units // 256 * 128
    return kernel_call(
        functools.partial(ffn_kernel, units, at, axes),
        "feed_forward",
        in_specs=[SCALAR] + [WHOLE] * 7 + [ANYWHERE],
        out_specs=[WHOLE] * 11,
        out_shape=[
            of((tokens, width), bf16),
            of((tokens, width), f32),
            of((tokens, width), f32),
            of((tokens, width), bf16),
            of((rows, width), f32),
            of((rows, width), bf16),
            of((block, cut), bf16),
            of((block, 3 * units - cut), bf16),
        ]
        + [of((block, 3 * units), bf16)] * 3,
        scratch_shapes=[pltpu.VMEM((width, units), bf16)] * 3
        + quarter_scratch(tokens, width) * 2
        + [pltpu.SemaphoreType.DMA((3,))],
    )(scalars, hidden, own, other, wo, wo_other, gains, target, packed)


def global_back_kernel(
    s_ref, target, middle, partial, came, gains, wo, wo_other, q_ref, k_ref, v_ref, table, w_qkv,
    middle_grad, middle_half, dqkv, out, out_sent, mixed_grad, low,
):
    rows, half = table.shape[1], wo.shape[1]
    m, h = pl.program_id(0), pl.program_id(1)

    @pl.when((m == 0) & (h == 0))
    def _():
        section = s_ref[0]
        v = middle[...]
        grad = partial[...] + came[...].astype(f32)
        grad = target[...].astype(f32) + normalize_back(v, inverse_rms(v), gains[3:4], grad)
        middle_grad[...] = grad
        low[...] = grad.astype(bf16)
        mine, theirs = lanes_of(section, half)
        middle_half[...] = low[:, mine]
        own_rows = pl.ds(pl.multiple_of(section * half, half), half)
        mixed_grad[...] = (
            times_transposed(low[:, mine], wo[own_rows])
            + times_transposed(low[:, theirs], wo_other[own_rows])
        ).astype(bf16)

    here = pl.ds(pl.multiple_of(m * rows, rows), rows)
    at = pl.multiple_of(h * LANES, LANES)
    quad = pl.ds(at, LANES)
    dq, dk, dv = attend_back(
        q_ref[here, quad], k_ref[here, quad], v_ref[here, quad], table[0], mixed_grad[here, quad]
    )
    dqkv[here, quad] = dq
    dqkv[here, pl.ds(at + half, LANES)] = dk
    dqkv[here, pl.ds(at + 2 * half, LANES)] = dv

    @pl.when((m == pl.num_programs(0) - 1) & (h == pl.num_programs(1) - 1))
    def _():
        total = times_transposed(dqkv[...], w_qkv[...])
        out[...] = total
        out_sent[...] = swap_rows(total.astype(bf16))


def global_back(section, target, middle, partial, came, gains, wo, wo_other, q, k, v, table, packed):
    micro, rows, _ = table.shape
    tokens, width = middle.shape
    half = wo.shape[1]

    def fixed(shape):
        return pl.BlockSpec(shape, lambda m, h: (0, 0))

    return kernel_call(
        global_back_kernel,
        "global_back",
        grid=(micro, half // LANES),
        in_specs=[SCALAR]
        + [fixed((tokens, width))] * 4
        + [fixed(gains.shape)]
        + [fixed((width, half))] * 2
        + [fixed((tokens, half))] * 3
        + [pl.BlockSpec((1, rows, rows), lambda m, h: (m, 0, 0)), fixed((width, 3 * half))],
        out_specs=[
            fixed((tokens, width)),
            fixed((tokens, half)),
            fixed((tokens, 3 * half)),
            fixed((tokens, width)),
            fixed((tokens, width)),
        ],
        out_shape=[
            of((tokens, width), f32),
            of((tokens, half), bf16),
            of((tokens, 3 * half), bf16),
            of((tokens, width), f32),
            of((tokens, width), bf16),
        ],
        scratch_shapes=[pltpu.VMEM((tokens, half), bf16), pltpu.VMEM((tokens, width), bf16)],
    )(section, target, middle, partial, came, gains, wo, wo_other, q, k, v, table, packed)


def global_quarters_kernel(axes, s_ref, x_ref, d_ref, y_ref, e_ref, out, *scratch):
    for x, d, at, (turned, rows) in (
        (x_ref, d_ref, 0, scratch[:2]),
        (y_ref, e_ref, d_ref.shape[1], scratch[2:]),
    ):
        fill_quarters(x, turned, rows, s_ref, axes, False)
        for k in range(RING):
            out[k, :, at : at + d.shape[1]] = matmul(rows[k], d[...]).astype(bf16)


def global_quarters(scalars, x, d, y, e, axes):
    tokens, width = x.shape
    return kernel_call(
        functools.partial(global_quarters_kernel, axes),
        "global_quarters",
        in_specs=[SCALAR] + [WHOLE] * 4,
        out_specs=WHOLE,
        out_shape=of((RING, width // RING, d.shape[1] + e.shape[1]), bf16),
        scratch_shapes=quarter_scratch(tokens, width) * 2,
    )(scalars, x, d, y, e)


def encoder_back_kernel(
    s_ref, middle_grad, hidden, partial, came, gains, wo, wo_other, q_ref, k_ref, v_ref, table,
    embed, embed_half, dq_ref, dkv_ref, mixed_grad,
):
    rows, keys = table.shape[1:]
    half = wo.shape[1]
    m, h = pl.program_id(0), pl.program_id(1)

    @pl.when((m == 0) & (h == 0))
    def _():
        section = s_ref[0]
        v = hidden[...]
        grad = partial[...] + came[...].astype(f32)
        grad = middle_grad[...] + normalize_back(v, inverse_rms(v), gains[2:3], grad)
        embed[...] = grad.astype(bf16)
        mine, theirs = lanes_of(section, half)
        embed_half[...] = embed[:, mine]
        own_rows = pl.ds(pl.multiple_of(section * half, half), half)
        mixed_grad[...] = (
            times_transposed(embed[:, mine], wo[own_rows])
            + times_transposed(embed[:, theirs], wo_other[own_rows])
        ).astype(bf16)

    here = pl.ds(pl.multiple_of(m * rows, rows), rows)
    at = pl.multiple_of(h * LANES, LANES)
    dq, dk, dv = attend_back(
        q_ref[...], k_ref[...], v_ref[...], table[0], mixed_grad[here, pl.ds(at, LANES)]
    )
    dq_ref[...] = dq
    there = pl.ds(pl.multiple_of(m * keys, keys), keys)
    dkv_ref[there, pl.ds(at, LANES)] = dk
    dkv_ref[there, pl.ds(at + half, LANES)] = dv


def encoder_back(section, middle_grad, hidden, partial, came, gains, wo, wo_other, q, k, v, table):
    micro, rows, keys = table.shape
    tokens, width = hidden.shape
    half = wo.shape[1]

    def fixed(shape):
        return pl.BlockSpec(shape, lambda m, h: (0, 0))

    per_row = pl.BlockSpec((rows, LANES), lambda m, h: (m, h))
    per_key = pl.BlockSpec((keys, LANES), lambda m, h: (m, h))
    return kernel_call(
        encoder_back_kernel,
        "encoder_back",
        grid=(micro, half // LANES),
        in_specs=[SCALAR]
        + [fixed((tokens, width))] * 4
        + [fixed(gains.shape)]
        + [fixed((width, half))] * 2
        + [per_row, per_key, per_key, pl.BlockSpec((1, rows, keys), lambda m, h: (m, 0, 0))],
        out_specs=[
            fixed((tokens, width)),
            fixed((tokens, half)),
            per_row,
            fixed((micro * keys, 2 * half)),
        ],
        out_shape=[
            of((tokens, width), bf16),
            of((tokens, half), bf16),
            of((tokens, half), bf16),
            of((micro * keys, 2 * half), bf16),
        ],
        scratch_shapes=[pltpu.VMEM((tokens, half), bf16)],
    )(section, middle_grad, hidden, partial, came, gains, wo, wo_other, q, k, v, table)


def encoder_quarters_kernel(axes, s_ref, b_ref, dkv, x_ref, dq, y_ref, e_ref, *refs):
    parts, scratch = refs[:4], refs[4:]
    half = dq.shape[1]
    for x, d, at, (turned, rows) in (
        (x_ref, dq, 0, scratch[:2]),
        (b_ref, dkv, half, scratch[2:4]),
        (y_ref, e_ref, 3 * half, scratch[4:]),
    ):
        fill_quarters(x, turned, rows, s_ref, axes, True)
        for k in (2, 1, 3, 0):
            parts[k][:, at : at + d.shape[1]] = matmul(rows[k], d[...]).astype(bf16)


def encoder_quarters(scalars, b, dkv, x, dq, y, e, axes):
    tokens, width = x.shape
    return kernel_call(
        functools.partial(encoder_quarters_kernel, axes),
        "encoder_quarters",
        in_specs=[SCALAR] + [WHOLE] * 6,
        out_specs=[WHOLE] * 4,
        out_shape=[of((width // RING, 4 * dq.shape[1]), bf16)] * 4,
        scratch_shapes=quarter_scratch(tokens, width)
        + quarter_scratch(b.shape[0], width)
        + quarter_scratch(tokens, width),
    )(scalars, b, dkv, x, dq, y, e)


def byte_partial_kernel(dkv, dq, wk, wv, wq, own, sent, query_own, query_sent):
    half = wk.shape[1]
    count, rows = own.shape[0], query_own.shape[0]
    for at, out in ((0, own), (count, sent)):
        total = times_transposed(dkv[at : at + count, :half], wk[...])
        total = total + times_transposed(dkv[at : at + count, half:], wv[...])
        out[...] = total.astype(out.dtype)
    total = times_transposed(dq[...], wq[...])
    query_own[...] = total[:rows]
    query_sent[...] = total[rows:].astype(bf16)


def byte_partial(dkv, dq, wk, wv, wq):
    width = wk.shape[0]
    count, rows = dkv.shape[0] // 2, dq.shape[0] // 2
    return kernel_call(
        byte_partial_kernel,
        "byte_partial",
        in_specs=[WHOLE] * 5,
        out_specs=[WHOLE] * 4,
        out_shape=[
            of((count, width), f32),
            of((count, width), bf16),
            of((rows, width), f32),
            of((rows, width), bf16),
        ],
    )(dkv, dq, wk, wv, wq)


def byte_grad_kernel(raw, own, came, query_own, query_came, pooled, embed, member, size, gains, out):
    pool = pooled[...]
    grad = query_own[...] + query_came[...].astype(f32)
    share = embed[...].astype(f32) + normalize_back(pool, inverse_rms(pool), gains[0:1], grad)
    share = share / size[...]
    high = share.astype(bf16)
    rest = (share - high.astype(f32)).astype(bf16)
    spread = transposed_times(member[...], high) + transposed_times(member[...], rest)
    v = raw[...].astype(f32)
    grad = own[...] + came[...].astype(f32)
    out[...] = spread + normalize_back(v, inverse_rms(v), gains[1:2], grad)


def byte_gradient(*args):
    return kernel_call(
        byte_grad_kernel,
        "byte_gradient",
        in_specs=[WHOLE] * 10,
        out_specs=WHOLE,
        out_shape=of(args[0].shape, f32),
    )(*args)


def patch_tables(lengths, documents):
    patches, count = lengths.shape[1], documents.shape[1]
    ends = jnp.cumsum(lengths, axis=1, dtype=jnp.int32)
    starts = ends - lengths
    position = lax.broadcasted_iota(jnp.int32, (1, patches, count), 2)
    member = (position >= starts[:, :, None]) & (position < ends[:, :, None])
    first_doc = jnp.sum(
        jnp.where(position == starts[:, :, None], documents[:, None, :], 0), axis=2
    )
    allowed = member & (documents[:, None, :] == first_doc[:, :, None])
    order_rows = lax.broadcasted_iota(jnp.int32, (1, patches, patches), 1)
    order_cols = lax.broadcasted_iota(jnp.int32, (1, patches, patches), 2)
    causal = (order_cols <= order_rows) & (first_doc[:, None, :] == first_doc[:, :, None])
    return member.astype(bf16), allowed.astype(f32), causal.astype(f32)


def own_first(pair, section):
    return jnp.where(section == 0, pair, pair[::-1])


def shards(
    byte_states,
    patch_lengths,
    doc_ids,
    proj_weights,
    out_weights,
    norm_gains,
    in_weights,
    down_weights,
    cotangent,
):
    section = lax.axis_index("section")
    scalars = jnp.stack([section, place("y"), place("x"), place("z")]).astype(jnp.int32)
    width = byte_states.shape[-1]
    half = width // 2
    units = down_weights.shape[1]

    own_w = jnp.concatenate([proj_weights[0], out_weights], axis=0)
    own_w = own_w.transpose(1, 0, 2).reshape(16, 4, 2, half)
    gains_own = jnp.pad(norm_gains[0].T, ((0, 0), (0, 126)))
    keep = jnp.where(section == 0, own_w[:, :, 0], own_w[:, :, 1]).reshape(16, 4 * half)
    give = jnp.where(section == 0, own_w[:, :, 1], own_w[:, :, 0]).reshape(16, 4 * half)
    got = across(jnp.concatenate([give, gains_own], axis=1))
    enc = jnp.where(section == 0, keep, got[:, : 4 * half])
    glob = jnp.where(section == 0, got[:, : 4 * half], keep)
    gains_first = jnp.where(section == 0, gains_own, got[:, 4 * half :])
    gains_last = jnp.where(section == 0, got[:, 4 * half :], gains_own)
    gains = jnp.concatenate([gains_first[:, :2], gains_last[:, :126]], axis=1)
    packed = jnp.concatenate([glob, in_weights[0], in_weights[1], down_weights], axis=1)
    packed = lax.all_gather(packed, "fsdp", axis=0, tiled=True)

    pack = jnp.concatenate(
        [enc[:, half : 3 * half], gains, enc[:, :half], enc[:, 3 * half :]], axis=1
    )
    first = 2 * half + 128
    pack = gather_direct(pack[None], "z", 0).reshape(64, -1)
    on_y = gather_direct(pack[None, :, :first], "x", 0).reshape(256, -1)
    on_x = gather_direct(pack[None, :, first:], "y", 0)
    places = jnp.stack([place("y"), place("x")])
    wk0, wv0, gains, wq0, wo0 = lay(places, ring_pieces(on_y, "y"), ring_pieces(on_x, "x"), half)
    pick = (
        lax.broadcasted_iota(jnp.int32, (8, 128), 0) == lax.broadcasted_iota(jnp.int32, (8, 128), 1)
    ).astype(bf16)
    gains = times_transposed(pick, gains)
    wo0_other = across(wo0)

    own_bytes, own_target = byte_states[0, 0], cotangent[0, 0]
    raw = jnp.concatenate([own_bytes, across(own_bytes)], axis=0)
    target = jnp.concatenate([own_target, across(own_target)], axis=0)
    lengths = own_first(patch_lengths[:, 0], section)
    documents = own_first(doc_ids[:, 0], section)
    patches, count = lengths.shape[1], documents.shape[1]
    member, allowed, causal = patch_tables(lengths, documents)
    size = lengths.astype(f32).reshape(-1, 1)

    raw_f32 = raw.astype(f32)
    pooled = lax.dot_general(
        member,
        raw.reshape(2, count, width),
        (((2,), (1,)), ((0,), (0,))),
        preferred_element_type=f32,
    ).reshape(2 * patches, width)
    pooled = pooled / size
    query_low = (pooled * inverse_rms(pooled) * gains[0]).astype(bf16)
    byte_low = (raw_f32 * inverse_rms(raw_f32) * gains[1]).astype(bf16)
    q0, k0, v0, mixed, mixed_sent = encoder_forward(query_low, byte_low, wq0, wk0, wv0, allowed)
    packed, mixed_came, target, causal, wo0_other = stage(
        packed, across(mixed_sent), target, causal, wo0_other
    )
    wo1 = packed[:, 3 * half : 4 * half]
    wo1_other = across(wo1)
    mixed0, hidden, normed_low, q1, k1, v1, mixed, mixed_sent = global_forward(
        scalars, pooled, mixed, mixed_came, wo0, wo0_other, gains, packed, causal
    )
    (
        mixed1, middle, ffn_partial, ffn_sent, block_out, block_sent, far_a, far_b, up_part, down_part,
        own_part,
    ) = feed_forward(
        scalars, hidden, mixed, across(mixed_sent), wo1, wo1_other, gains, target, packed,
        units, 4 * half, FFN_AXES,
    )
    ffn_came, block_came, far_a, far_b = stage(across(ffn_sent), across(block_sent), far_a, far_b)

    far_a, far_b = shift_by_core(far_a, FFN_AXES, 1), shift_by_core(far_b, FFN_AXES, -1)
    middle_grad, middle_half, dqkv, normed_partial, normed_sent = global_back(
        scalars, target, middle, ffn_partial, ffn_came, gains, wo1, wo1_other,
        q1, k1, v1, causal, packed,
    )
    glob_parts = global_quarters(scalars, normed_low, dqkv, mixed1, middle_half, GLOB_AXES)
    far_a, far_b, normed_sent, glob_parts = stage(far_a, far_b, normed_sent, glob_parts)

    glob_line = line_sum(glob_parts, GLOB_AXES)
    up_part, down_part = near(up_part, down_part, far_a, far_b)
    normed_came, up_part, down_part = stage(across(normed_sent), up_part, down_part)
    up_came, down_came = (
        shift_by_core(up_part, FFN_AXES, 1),
        shift_by_core(down_part, FFN_AXES, -1),
    )
    embed, embed_half, dq, dkv = encoder_back(
        scalars, middle_grad, hidden, normed_partial, normed_came, gains, wo0, wo0_other,
        q0, k0, v0, allowed,
    )
    enc_parts = encoder_quarters(
        scalars, byte_low, dkv, query_low, dq, mixed0, embed_half, ENC_AXES
    )
    up_came, down_came, enc_parts, dq, dkv = stage(up_came, down_came, enc_parts, dq, dkv)

    enc_came = send_quarters(enc_parts, ENC_AXES)
    ffn_sum = plane_sum(line_total(own_part, up_came, down_came), FFN_AXES)
    byte_own, byte_sent, query_own, query_sent = byte_partial(dkv, dq, wk0, wv0, wq0)
    block_out = block_out + block_came.astype(f32)
    enc_came, ffn_sum, byte_sent, query_sent, block_out = stage(
        enc_came, ffn_sum, byte_sent, query_sent, block_out
    )

    byte_came, query_came = across(byte_sent), across(query_sent)
    enc_sum = plane_sum(line_total(enc_parts[0], *enc_came), ENC_AXES)
    glob_sum = plane_sum(glob_line, GLOB_AXES)
    byte_grad = byte_gradient(
        own_bytes, byte_own, byte_came, query_own, query_came,
        pooled[:patches], embed[:patches], member[0], size[:patches], gains,
    )

    gate_sum, up_sum, down_sum = jnp.split(ffn_sum, 3, axis=1)
    mine = jnp.where(section == 0, enc_sum, glob_sum)
    theirs = across(jnp.where(section == 0, glob_sum, enc_sum))
    first = jnp.where(section == 0, mine, theirs)
    last = jnp.where(section == 0, theirs, mine)
    sums = jnp.stack(
        [
            jnp.concatenate([x[:, k * half : (k + 1) * half] for x in (first, last)], axis=1)
            for k in range(4)
        ]
    )

    def against(weight, grad):
        return jnp.sum(weight.astype(f32) * grad, axis=-1)

    own_dots = against(proj_weights[0], sums[:3])
    ffn_dots = against(in_weights[0], gate_sum) + against(in_weights[1], up_sum)
    ffn_dots = ffn_dots + across(ffn_dots)
    gain_sum = jnp.where(
        section == 0,
        jnp.stack([own_dots[0], own_dots[1] + own_dots[2]]),
        jnp.stack([own_dots[0] + own_dots[1] + own_dots[2], ffn_dots]),
    )
    gain_sum = gain_sum / norm_gains[0].astype(f32)
    return (
        block_out[None, None],
        byte_grad[None, None],
        sums[None, :3],
        sums[3:],
        gain_sum[None],
        jnp.stack([gate_sum, up_sum]),
        down_sum,
    )


def solution(mesh):
    in_specs = (
        P("section", "fsdp", None, None),
        P(None, "fsdp", None),
        P(None, "fsdp", None),
        P("section", None, "fsdp", None),
        P("section", "fsdp", None),
        P("section", None, "fsdp"),
        P(None, "fsdp", "section"),
        P("fsdp", "section"),
        P("section", "fsdp", None, None),
    )
    out_specs = (
        P("section", "fsdp", None, None),
        P("section", "fsdp", None, None),
        P("section", None, "fsdp", None),
        P("section", "fsdp", None),
        P("section", None, "fsdp"),
        P(None, "fsdp", "section"),
        P("fsdp", "section"),
    )
    return jax.shard_map(shards, mesh=mesh, in_specs=in_specs, out_specs=out_specs, check_vma=False)
```

```python
import functools

import jax
import jax.numpy as jnp
from jax import lax
from jax.experimental import pallas as pl
from jax.experimental.pallas import tpu as pltpu
from jax.sharding import PartitionSpec as P

HEADS = 16
HEAD_DIM = 64
QUAD = 4
LANES = QUAD * HEAD_DIM
RING = 4
STRIDE = {"y": 16, "x": 4, "z": 1}

FFN_AXES = ("y", "x")
ENC_AXES = ("x", "y")
GLOB_AXES = (("z", "z"), ("y", "x"), ("x", "y"))

epsilon = 1e-05
masked_score = -1e30
bf16 = jnp.bfloat16
f32 = jnp.float32

SCALAR = pl.BlockSpec(memory_space=pltpu.SMEM)
WHOLE = pl.BlockSpec(memory_space=pltpu.VMEM)
IN_HBM = pl.BlockSpec(memory_space=pltpu.HBM)
OUT_HBM = pltpu.HBM
QUICK = pl.CostEstimate(flops=1, bytes_accessed=1, transcendentals=0)


def of(shape, kind):
    return jax.ShapeDtypeStruct(shape, kind)


ROOM = {
    "lay": 6,
    "prepare": 8,
    "encoder_forward": 12,
    "encoder_out": 8,
    "global_forward": 8,
    "feed_forward": 28,
    "global_back": 12,
    "global_quarters": 10,
    "near": 4,
    "split": 4,
    "line_total": 4,
    "encoder_back": 14,
    "encoder_quarters": 10,
    "byte_partial": 8,
    "byte_gradient": 8,
}


def kernel_call(body, name, **options):
    return pl.pallas_call(
        body,
        name=name,
        cost_estimate=QUICK,
        compiler_params=pltpu.CompilerParams(vmem_limit_bytes=ROOM[name] << 20),
        **options,
    )


def across(block):
    return lax.ppermute(block, "section", [(0, 1), (1, 0)])


def moved(i, ax, by):
    step = STRIDE[ax]
    c = (i // step) % RING
    return i + ((c + by) % RING - c) * step


def shift(block, ax, by):
    return lax.ppermute(block, "fsdp", [(i, moved(i, ax, by)) for i in range(64)])


def shift_by_core(block, axes, by):
    route = [(64 * s + i, 64 * s + moved(i, ax, by)) for s, ax in enumerate(axes) for i in range(64)]
    return lax.ppermute(block, ("section", "fsdp"), route)


def place(ax):
    return (lax.axis_index("fsdp") // STRIDE[ax]) % RING


def planes(axes):
    rows = {}
    for s, ax in enumerate(axes):
        for i in range(64):
            rows.setdefault((s, (i // STRIDE[ax]) % RING), []).append(64 * s + i)
    return list(rows.values())


def lines(axes):
    rows = {}
    for s, ax in enumerate(axes):
        for i in range(64):
            c = (i // STRIDE[ax]) % RING
            rows.setdefault((s, i - c * STRIDE[ax]), []).append(64 * s + i)
    return list(rows.values())


def put(whole, piece, at, dim):
    where = [0] * whole.ndim
    where[dim] = at
    return lax.dynamic_update_slice(whole, piece, where)


def gather_direct(block, ax, dim):
    c = place(ax)
    whole = jnp.zeros((*block.shape[:dim], RING, *block.shape[dim + 1 :]), block.dtype)
    arrived = [(shift(block, ax, by), (c - by) % RING) for by in (1, -1, 2)]
    for piece, at in [(block, c)] + arrived:
        whole = put(whole, piece, at, dim)
    return whole


def ring_pieces(block, ax):
    half = block.shape[-1] // 256 * 128
    last = block.ndim - 1
    below, above = shift(block, ax, 1), shift(block, ax, -1)
    first = shift(lax.slice_in_dim(below, 0, half, axis=last), ax, 1)
    second = shift(lax.slice_in_dim(above, half, None, axis=last), ax, -1)
    return block, above, below, first, second


def columns(pieces, k, begin, end):
    if k != 2:
        return pieces[(0, 1, None, 2)[k]][..., begin:end]
    first, second = pieces[3:]
    cut = first.shape[-1]
    if end <= cut:
        return first[..., begin:end]
    if begin >= cut:
        return second[..., begin - cut : end - cut]
    return jnp.concatenate([first[..., begin:], second[..., : end - cut]], axis=-1)


def lay_kernel(c_ref, *refs):
    ins, outs = refs[:10], refs[10:]
    for ax, pieces, targets in (("y", ins[:5], outs[:3]), ("x", ins[5:], outs[3:])):
        c = c_ref[0 if ax == "y" else 1]
        for k in range(RING):
            at = lax.rem(c + k, RING)
            column = 0
            for out in targets:
                value = columns(pieces, k, column, column + out.shape[-1])
                if ax == "y":
                    out[at] = value
                else:
                    out[:, at] = value
                column += out.shape[-1]


def lay(places, on_y, on_x, half):
    rows = on_y[0].shape[0]
    wide = (half, half, on_y[0].shape[1] - 2 * half)
    outs = [of((RING, rows, w), bf16) for w in wide]
    outs += [of((RING, RING, rows // RING, half), bf16)] * 2
    made = kernel_call(
        lay_kernel,
        "lay",
        in_specs=[SCALAR] + [WHOLE] * 10,
        out_specs=[WHOLE] * 5,
        out_shape=outs,
    )(places, *on_y, *on_x)
    return [m.reshape(RING * rows, m.shape[-1]) for m in made]


def send_near(parts, axes):
    return [shift_by_core(parts[1], axes, 1), shift_by_core(parts[3], axes, -1)]


def send_far(parts, axes):
    return shift_by_core(parts[2], axes, 2)


def send_quarters(parts, axes):
    return [*send_near(parts, axes), send_far(parts, axes)]


def total_kernel(*refs):
    total = refs[0][...].astype(f32)
    for part in refs[1:-1]:
        total = total + part[...].astype(f32)
    refs[-1][...] = total.astype(bf16)


def line_total(*parts):
    return kernel_call(
        total_kernel,
        "line_total",
        in_specs=[WHOLE] * len(parts),
        out_specs=WHOLE,
        out_shape=of(parts[0].shape, bf16),
    )(*parts)


def split_kernel(axes, names, s_ref, *refs):
    n = len(refs) - RING
    total = refs[0][...].astype(f32)
    for part in refs[1:n]:
        total = total + part[...].astype(f32)
    total = total.astype(bf16)
    outs = refs[n:]
    for s, ax in enumerate(axes):

        @pl.when(s_ref[0] == s)
        def _():
            c = s_ref[1 + "yxz".index(ax)]
            dim = names[s].index(ax)
            blocks = total.reshape(*[RING] * len(names[s]), -1, total.shape[1])
            for at in range(RING):
                block = lax.index_in_dim(blocks, at, dim, keepdims=False)
                k = lax.rem(at + RING - c, RING)
                for j in range(RING):

                    @pl.when(k == j)
                    def _():
                        outs[j][...] = block.reshape(outs[j].shape)


def split(scalars, parts, axes, names):
    rows, wide = parts[0].shape
    return kernel_call(
        functools.partial(split_kernel, axes, names),
        "split",
        in_specs=[SCALAR] + [WHOLE] * len(parts),
        out_specs=[WHOLE] * RING,
        out_shape=[of((rows // RING, wide), bf16)] * RING,
    )(scalars, *parts)


def near_kernel(up, down, a, b, up_out, down_out):
    cut = a.shape[1]
    up_out[:, :cut] = (up[:, :cut].astype(f32) + a[...].astype(f32)).astype(bf16)
    up_out[:, cut:] = up[:, cut:]
    down_out[:, cut:] = (down[:, cut:].astype(f32) + b[...].astype(f32)).astype(bf16)
    down_out[:, :cut] = down[:, :cut]


def near(up, down, a, b):
    return kernel_call(
        near_kernel,
        "near",
        in_specs=[WHOLE] * 4,
        out_specs=[WHOLE] * 2,
        out_shape=[of(up.shape, bf16)] * 2,
    )(up, down, a, b)


def line_sum(parts, axes):
    return lax.psum_scatter(
        parts,
        ("section", "fsdp"),
        scatter_dimension=0,
        axis_index_groups=lines(axes),
        tiled=False,
    )


def plane_sum(part, axes):
    blocks = part.reshape(16, part.shape[0] // 16, part.shape[1])
    blocks = lax.all_to_all(
        blocks, ("section", "fsdp"), 0, 0, axis_index_groups=planes(axes), tiled=True
    )
    return jnp.sum(blocks.astype(f32), axis=0)


def stage(*values):
    return lax.optimization_barrier(values)


def inverse_rms(values):
    return lax.rsqrt(jnp.mean(values * values, axis=-1, keepdims=True) + epsilon)


def normalize_back(values, inverse, scales, gradient):
    unit_rows = values * inverse
    scaled = gradient * scales
    inner_mean = jnp.mean(scaled * unit_rows, axis=-1, keepdims=True)
    return inverse * (scaled - unit_rows * inner_mean)


def matmul(left, right):
    return jnp.dot(left, right, preferred_element_type=f32)


def times_transposed(left, right):
    return lax.dot_general(left, right, (((1,), (1,)), ((), ())), preferred_element_type=f32)


def transposed_times(left, right):
    return lax.dot_general(left, right, (((0,), (0,)), ((), ())), preferred_element_type=f32)


def of_head(value, h):
    head = lax.broadcasted_iota(jnp.int32, value.shape, 1) // HEAD_DIM
    return jnp.where(head == h, value, jnp.zeros_like(value))


def stacked(value):
    return jnp.concatenate([of_head(value, h) for h in range(QUAD)], axis=0)


def unstacked(value, rows):
    total = of_head(value[:rows], 0)
    for h in range(1, QUAD):
        total = total + of_head(value[h * rows : (h + 1) * rows], h)
    return total


def probabilities(q4, keys, table):
    raw = times_transposed(q4, keys)
    allowed = jnp.concatenate([table] * QUAD, axis=0) > 0
    scores = jnp.where(allowed, raw * HEAD_DIM ** (-0.5), masked_score)
    weights = jnp.exp(scores - jnp.max(scores, axis=-1, keepdims=True))
    return weights / jnp.sum(weights, axis=-1, keepdims=True)


def attend(q, k, v, table):
    p = probabilities(stacked(q), k, table).astype(bf16)
    return unstacked(matmul(p, v), q.shape[0]).astype(bf16)


def attend_back(q, k, v, table, d):
    rows = q.shape[0]
    q4, d4 = stacked(q), stacked(d)
    p = probabilities(q4, k, table)
    dp = times_transposed(d4, v)
    ds = p * (dp - jnp.sum(p * dp, axis=-1, keepdims=True)) * HEAD_DIM ** (-0.5)
    ds = ds.astype(bf16)
    dq = unstacked(matmul(ds, k), rows).astype(bf16)
    dk = transposed_times(ds, q4).astype(bf16)
    dv = transposed_times(p.astype(bf16), d4).astype(bf16)
    return dq, dk, dv


def lanes_of(section, half):
    mine = pl.ds(pl.multiple_of(section * half, half), half)
    theirs = pl.ds(pl.multiple_of((1 - section) * half, half), half)
    return mine, theirs


def merge(scratch, section, own, other):
    mine, theirs = lanes_of(section, own.shape[1])
    scratch[:, mine] = own
    scratch[:, theirs] = other


def swap_rows(x):
    half = x.shape[0] // 2
    return jnp.concatenate([x[half:], x[:half]], axis=0)


def quarter(turned, ax, at):
    if ax == "y":
        rows = turned[at]
    elif ax == "x":
        rows = turned[:, at]
    else:
        rows = turned[:, :, at]
    return rows.reshape(turned.shape[0] ** 2 * turned.shape[3], turned.shape[4])


def fill_quarters(x_ref, turned, rows, s_ref, axes, first):
    turned[...] = x_ref[...].T.reshape(turned.shape)
    for s, ax in enumerate(axes):

        @pl.when(s_ref[0] == s)
        def _():
            c = s_ref[1 + "yxz".index(ax)] if first else 0
            for k in range(RING):
                rows[k] = quarter(turned, ax, lax.rem(c + k, RING))


def turned_scratch(tokens, features):
    return pltpu.VMEM((RING, RING, RING, features // RING**3, tokens), bf16)


def quarter_scratch(tokens, features):
    return [
        turned_scratch(tokens, features),
        pltpu.VMEM((RING, features // RING, tokens), bf16),
    ]


def rows_of(x):
    return of((RING, x.shape[1] // RING, x.shape[0]), bf16)


def prepare_kernel(enc_axes, ffn_axes, s_ref, b_ref, x_ref, t_ref, b_rows, x_rows, t_rows, *turned):
    fill_quarters(b_ref, turned[0], b_rows, s_ref, enc_axes, True)
    fill_quarters(x_ref, turned[1], x_rows, s_ref, enc_axes, True)
    fill_quarters(t_ref, turned[2], t_rows, s_ref, ffn_axes, True)


def prepare(scalars, b, x, t, enc_axes, ffn_axes):
    return kernel_call(
        functools.partial(prepare_kernel, enc_axes, ffn_axes),
        "prepare",
        in_specs=[SCALAR] + [WHOLE] * 3,
        out_specs=[WHOLE] * 3,
        out_shape=[rows_of(a) for a in (b, x, t)],
        scratch_shapes=[turned_scratch(*a.shape) for a in (b, x, t)],
    )(scalars, b, x, t)


def encoder_kernel(x_ref, b_ref, wq, wk, wv, table, q_ref, k_ref, v_ref, mixed, mixed_swapped):
    q = matmul(x_ref[...], wq[...]).astype(bf16)
    k = matmul(b_ref[...], wk[...]).astype(bf16)
    v = matmul(b_ref[...], wv[...]).astype(bf16)
    q_ref[...], k_ref[...], v_ref[...] = q, k, v
    out = attend(q, k, v, table[0])
    mixed[...] = out
    mixed_swapped[...] = out


def encoder_forward(query_low, byte_low, wq, wk, wv, table):
    micro, rows, keys = table.shape
    width, half = wq.shape
    weight = pl.BlockSpec((width, LANES), lambda h, m: (0, h))
    per_row = pl.BlockSpec((rows, LANES), lambda h, m: (m, h))
    per_key = pl.BlockSpec((keys, LANES), lambda h, m: (m, h))
    return kernel_call(
        encoder_kernel,
        "encoder_forward",
        grid=(half // LANES, micro),
        in_specs=[
            pl.BlockSpec((rows, width), lambda h, m: (m, 0)),
            pl.BlockSpec((keys, width), lambda h, m: (m, 0)),
            weight,
            weight,
            weight,
            pl.BlockSpec((1, rows, keys), lambda h, m: (m, 0, 0)),
        ],
        out_specs=[
            per_row,
            per_key,
            per_key,
            per_row,
            pl.BlockSpec((rows, LANES), lambda h, m: (1 - m, h)),
        ],
        out_shape=[
            of((micro * rows, half), bf16),
            of((micro * keys, half), bf16),
            of((micro * keys, half), bf16),
            of((micro * rows, half), bf16),
            of((micro * rows, half), bf16),
        ],
    )(query_low, byte_low, wq, wk, wv, table)


def encoder_out_kernel(
    enc_axes, glob_axes, s_ref, pooled, own, other, wo, wo_other, gains,
    hidden_ref, low_ref, mixed_rows, low_rows, whole_ref, sum_ref, turned_mixed, turned_low,
):
    section = s_ref[0]
    merge(whole_ref, section, own[...], other[...])
    whole = whole_ref[...]
    merge(sum_ref, section, matmul(whole, wo[...]), matmul(whole, wo_other[...]))
    low_hidden = (pooled[...] + sum_ref[...]).astype(bf16)
    hidden_ref[...] = low_hidden
    hidden = low_hidden.astype(f32)
    low = (hidden * inverse_rms(hidden) * gains[2:3]).astype(bf16)
    low_ref[...] = low
    fill_quarters(whole, turned_mixed, mixed_rows, s_ref, enc_axes, True)
    fill_quarters(low, turned_low, low_rows, s_ref, glob_axes, True)


def encoder_out(scalars, pooled, own, other, wo, wo_other, gains, enc_axes, glob_axes):
    tokens, width = pooled.shape
    rows = of((RING, width // RING, tokens), bf16)
    return kernel_call(
        functools.partial(encoder_out_kernel, enc_axes, glob_axes),
        "encoder_out",
        in_specs=[SCALAR] + [WHOLE] * 6,
        out_specs=[WHOLE] * 4,
        out_shape=[of((tokens, width), bf16), of((tokens, width), bf16), rows, rows],
        scratch_shapes=[pltpu.VMEM((tokens, width), bf16), pltpu.VMEM((tokens, width), f32)]
        + [turned_scratch(tokens, width)] * 2,
    )(scalars, pooled, own, other, wo, wo_other, gains)


def global_kernel(x_ref, packed, table, q_ref, k_ref, v_ref, mixed, mixed_swapped, weights, sems):
    h, m = pl.program_id(0), pl.program_id(1)
    count = pl.num_programs(0)

    def copy(j, at):
        source = packed.at[:, pl.ds(pl.multiple_of((j * count + at) * LANES, LANES), LANES)]
        return pltpu.make_async_copy(source, weights.at[at, j], sems.at[at, j])

    @pl.when((h == 0) & (m == 0))
    def _():
        for at in range(weights.shape[0]):
            for j in range(3):
                copy(j, at).start()

    @pl.when(m == 0)
    def _():
        for j in range(3):
            copy(j, h).wait()

    x = x_ref[...]
    q, k, v = (matmul(x, weights[h, j]).astype(bf16) for j in range(3))
    q_ref[...], k_ref[...], v_ref[...] = q, k, v
    out = attend(q, k, v, table[0])
    mixed[...] = out
    mixed_swapped[...] = out


def global_forward(x, packed, table, half):
    micro, rows, _ = table.shape
    width = x.shape[1]
    count = half // LANES
    per_row = pl.BlockSpec((rows, LANES), lambda h, m: (m, h))
    return kernel_call(
        global_kernel,
        "global_forward",
        grid=(count, micro),
        in_specs=[
            pl.BlockSpec((rows, width), lambda h, m: (m, 0)),
            IN_HBM,
            pl.BlockSpec((1, rows, rows), lambda h, m: (m, 0, 0)),
        ],
        out_specs=[per_row] * 4 + [pl.BlockSpec((rows, LANES), lambda h, m: (1 - m, h))],
        out_shape=[of((micro * rows, half), bf16)] * 5,
        scratch_shapes=[
            pltpu.VMEM((count, 3, width, LANES), bf16),
            pltpu.SemaphoreType.DMA((count, 3)),
        ],
    )(x, packed, table)


class Outgoing:
    def __init__(self, buffers, targets, sems):
        self.copies = [
            pltpu.make_async_copy(b, t, sems.at[k]) for k, (b, t) in enumerate(zip(buffers, targets))
        ]

    def send(self, k):
        self.copies[k].start()

    def finish(self):
        for copy in self.copies:
            copy.wait()


def ffn_kernel(
    units, at, axes, s_ref, hidden, own, other, wo, wo_other, gains, target, rows_target, packed,
    mixed_whole, middle_ref, partial, partial_sent, result, result_sent, far_a, far_b, up_part,
    down_part, own_part, w_gate, w_up, w_down, turned, rows, up_made, down_made, own_made, sems, sent,
):
    outgoing = Outgoing((up_made, down_made, own_made), (up_part, down_part, own_part), sent)
    copies = [
        pltpu.make_async_copy(packed.at[:, pl.ds(at + k * units, units)], w, sems.at[k])
        for k, w in enumerate((w_gate, w_up, w_down))
    ]
    for copy in copies:
        copy.start()
    section = s_ref[0]
    merge(mixed_whole, section, own[...], other[...])
    whole = mixed_whole[...]
    merge(middle_ref, section, matmul(whole, wo[...]), matmul(whole, wo_other[...]))
    middle = hidden[...].astype(f32) + middle_ref[...]
    middle_ref[...] = middle
    low = (middle * inverse_rms(middle) * gains[3:4]).astype(bf16)
    copies[0].wait()
    gate = matmul(low, w_gate[...])
    copies[1].wait()
    up = matmul(low, w_up[...])
    sigma = jax.nn.sigmoid(gate)
    inner = (gate * sigma * up).astype(bf16)
    copies[2].wait()
    inner_grad = matmul(target[...], w_down[...])
    up_grad = (inner_grad * gate * sigma).astype(bf16)
    gate_grad = (inner_grad * up * sigma * (1.0 + gate * (1.0 - sigma))).astype(bf16)
    half = partial.shape[0] // 2
    total = times_transposed(gate_grad, w_gate[...]) + times_transposed(up_grad, w_up[...])
    partial[...] = total
    partial_sent[...] = swap_rows(total.astype(bf16))
    out = times_transposed(inner, w_down[...])
    result[...] = middle[:half] + out[:half]
    result_sent[...] = out[half:].astype(bf16)
    fill_quarters(low, turned, rows, s_ref, axes, True)
    cut = far_a.shape[1]
    for k, part in ((1, up_made), (3, down_made), (0, own_made), (2, None)):
        for j, (x, d) in enumerate(((rows, gate_grad), (rows, up_grad), (rows_target, inner))):
            value = matmul(x[k], d).astype(bf16)
            begin, end = j * units, (j + 1) * units
            if part is not None:
                part[:, begin:end] = value
            elif end <= cut:
                far_a[:, begin:end] = value
            elif begin >= cut:
                far_b[:, begin - cut : end - cut] = value
            else:
                far_a[:, begin:] = value[:, : cut - begin]
                far_b[:, : end - cut] = value[:, cut - begin :]
        if part is not None:
            outgoing.send({1: 0, 3: 1, 0: 2}[k])
    outgoing.finish()


def feed_forward(
    scalars, hidden, own, other, wo, wo_other, gains, target, rows, packed, units, at, axes
):
    tokens, width = hidden.shape
    part = tokens // 2
    block = width // RING
    cut = 3 * units // 256 * 128
    return kernel_call(
        functools.partial(ffn_kernel, units, at, axes),
        "feed_forward",
        in_specs=[SCALAR] + [WHOLE] * 8 + [IN_HBM],
        out_specs=[WHOLE] * 8 + [IN_HBM] * 3,
        out_shape=[
            of((tokens, width), bf16),
            of((tokens, width), f32),
            of((tokens, width), f32),
            of((tokens, width), bf16),
            of((part, width), f32),
            of((part, width), bf16),
            of((block, cut), bf16),
            of((block, 3 * units - cut), bf16),
        ]
        + [OUT_HBM((block, 3 * units), bf16)] * 3,
        scratch_shapes=[pltpu.VMEM((width, units), bf16)] * 3
        + quarter_scratch(tokens, width)
        + [pltpu.VMEM((block, 3 * units), bf16)] * 3
        + [pltpu.SemaphoreType.DMA((3,))] * 2,
    )(scalars, hidden, own, other, wo, wo_other, gains, target, rows, packed)


def global_back_kernel(
    s_ref, target, middle, partial, came, gains, wo, wo_other, q_ref, k_ref, v_ref, table, packed,
    middle_grad, middle_half, dqkv, out, out_sent, mixed_grad, low, w_qkv, sem,
):
    rows, half = table.shape[1], wo.shape[1]
    m, h = pl.program_id(0), pl.program_id(1)
    copy = pltpu.make_async_copy(packed.at[:, pl.ds(0, 3 * half)], w_qkv, sem)

    @pl.when((m == 0) & (h == 0))
    def _():
        copy.start()
        section = s_ref[0]
        v = middle[...]
        grad = partial[...] + came[...].astype(f32)
        grad = target[...].astype(f32) + normalize_back(v, inverse_rms(v), gains[3:4], grad)
        middle_grad[...] = grad
        low[...] = grad.astype(bf16)
        mine, theirs = lanes_of(section, half)
        middle_half[...] = low[:, mine]
        own_rows = pl.ds(pl.multiple_of(section * half, half), half)
        mixed_grad[...] = (
            times_transposed(low[:, mine], wo[own_rows])
            + times_transposed(low[:, theirs], wo_other[own_rows])
        ).astype(bf16)

    here = pl.ds(pl.multiple_of(m * rows, rows), rows)
    at = pl.multiple_of(h * LANES, LANES)
    quad = pl.ds(at, LANES)
    dq, dk, dv = attend_back(
        q_ref[here, quad], k_ref[here, quad], v_ref[here, quad], table[0], mixed_grad[here, quad]
    )
    dqkv[here, quad] = dq
    dqkv[here, pl.ds(at + half, LANES)] = dk
    dqkv[here, pl.ds(at + 2 * half, LANES)] = dv

    @pl.when((m == pl.num_programs(0) - 1) & (h == pl.num_programs(1) - 1))
    def _():
        copy.wait()
        total = times_transposed(dqkv[...], w_qkv[...])
        out[...] = total
        out_sent[...] = swap_rows(total.astype(bf16))


def global_back(section, target, middle, partial, came, gains, wo, wo_other, q, k, v, table, packed):
    micro, rows, _ = table.shape
    tokens, width = middle.shape
    half = wo.shape[1]

    def fixed(shape):
        return pl.BlockSpec(shape, lambda m, h: (0, 0))

    return kernel_call(
        global_back_kernel,
        "global_back",
        grid=(micro, half // LANES),
        in_specs=[SCALAR]
        + [fixed((tokens, width))] * 4
        + [fixed(gains.shape)]
        + [fixed((width, half))] * 2
        + [fixed((tokens, half))] * 3
        + [pl.BlockSpec((1, rows, rows), lambda m, h: (m, 0, 0)), IN_HBM],
        out_specs=[
            fixed((tokens, width)),
            fixed((tokens, half)),
            fixed((tokens, 3 * half)),
            fixed((tokens, width)),
            fixed((tokens, width)),
        ],
        out_shape=[
            of((tokens, width), f32),
            of((tokens, half), bf16),
            of((tokens, 3 * half), bf16),
            of((tokens, width), f32),
            of((tokens, width), bf16),
        ],
        scratch_shapes=[
            pltpu.VMEM((tokens, half), bf16),
            pltpu.VMEM((tokens, width), bf16),
            pltpu.VMEM((width, 3 * half), bf16),
            pltpu.SemaphoreType.DMA,
        ],
    )(section, target, middle, partial, came, gains, wo, wo_other, q, k, v, table, packed)


def global_quarters_kernel(axes, s_ref, x_rows, d_ref, y_ref, e_ref, *refs):
    outs, made, (turned, y_rows, sent) = refs[:4], refs[4:8], refs[8:]
    outgoing = Outgoing(made, outs, sent)
    fill_quarters(y_ref, turned, y_rows, s_ref, axes, True)
    for k in (1, 3, 2, 0):
        made[k][:, : d_ref.shape[1]] = matmul(x_rows[k], d_ref[...]).astype(bf16)
        made[k][:, d_ref.shape[1] :] = matmul(y_rows[k], e_ref[...]).astype(bf16)
        outgoing.send(k)
    outgoing.finish()


def global_quarters(scalars, x_rows, d, y, e, axes):
    tokens, width = y.shape
    shape = (width // RING, d.shape[1] + e.shape[1])
    return kernel_call(
        functools.partial(global_quarters_kernel, axes),
        "global_quarters",
        in_specs=[SCALAR] + [WHOLE] * 4,
        out_specs=[IN_HBM] * 4,
        out_shape=[OUT_HBM(shape, bf16)] * 4,
        scratch_shapes=[pltpu.VMEM(shape, bf16)] * 4
        + quarter_scratch(tokens, width)
        + [pltpu.SemaphoreType.DMA((4,))],
    )(scalars, x_rows, d, y, e)


def encoder_back_kernel(
    s_ref, middle_grad, hidden, partial, came, gains, wo, wo_other, q_ref, k_ref, v_ref, table,
    embed, embed_half, dq_ref, dkv_ref, mixed_grad,
):
    rows, keys = table.shape[1:]
    half = wo.shape[1]
    m, h = pl.program_id(0), pl.program_id(1)

    @pl.when((m == 0) & (h == 0))
    def _():
        section = s_ref[0]
        v = hidden[...].astype(f32)
        grad = partial[...] + came[...].astype(f32)
        grad = middle_grad[...] + normalize_back(v, inverse_rms(v), gains[2:3], grad)
        embed[...] = grad.astype(bf16)
        mine, theirs = lanes_of(section, half)
        embed_half[...] = embed[:, mine]
        own_rows = pl.ds(pl.multiple_of(section * half, half), half)
        mixed_grad[...] = (
            times_transposed(embed[:, mine], wo[own_rows])
            + times_transposed(embed[:, theirs], wo_other[own_rows])
        ).astype(bf16)

    here = pl.ds(pl.multiple_of(m * rows, rows), rows)
    at = pl.multiple_of(h * LANES, LANES)
    dq, dk, dv = attend_back(
        q_ref[...], k_ref[...], v_ref[...], table[0], mixed_grad[here, pl.ds(at, LANES)]
    )
    dq_ref[...] = dq
    there = pl.ds(pl.multiple_of(m * keys, keys), keys)
    dkv_ref[there, pl.ds(at, LANES)] = dk
    dkv_ref[there, pl.ds(at + half, LANES)] = dv


def encoder_back(section, middle_grad, hidden, partial, came, gains, wo, wo_other, q, k, v, table):
    micro, rows, keys = table.shape
    tokens, width = hidden.shape
    half = wo.shape[1]

    def fixed(shape):
        return pl.BlockSpec(shape, lambda m, h: (0, 0))

    per_row = pl.BlockSpec((rows, LANES), lambda m, h: (m, h))
    per_key = pl.BlockSpec((keys, LANES), lambda m, h: (m, h))
    return kernel_call(
        encoder_back_kernel,
        "encoder_back",
        grid=(micro, half // LANES),
        in_specs=[SCALAR]
        + [fixed((tokens, width))] * 4
        + [fixed(gains.shape)]
        + [fixed((width, half))] * 2
        + [per_row, per_key, per_key, pl.BlockSpec((1, rows, keys), lambda m, h: (m, 0, 0))],
        out_specs=[
            fixed((tokens, width)),
            fixed((tokens, half)),
            per_row,
            fixed((micro * keys, 2 * half)),
        ],
        out_shape=[
            of((tokens, width), bf16),
            of((tokens, half), bf16),
            of((tokens, half), bf16),
            of((micro * keys, 2 * half), bf16),
        ],
        scratch_shapes=[pltpu.VMEM((tokens, half), bf16)],
    )(section, middle_grad, hidden, partial, came, gains, wo, wo_other, q, k, v, table)


def encoder_quarters_kernel(b_rows, dkv, x_rows, dq, y_rows, e_ref, *refs):
    outs, made, sent = refs[:4], refs[4:8], refs[8]
    half = dq.shape[1]
    outgoing = Outgoing(made, outs, sent)
    for k in (1, 3, 2, 0):
        for rows, d, at in ((x_rows, dq, 0), (b_rows, dkv, half), (y_rows, e_ref, 3 * half)):
            made[k][:, at : at + d.shape[1]] = matmul(rows[k], d[...]).astype(bf16)
        outgoing.send(k)
    outgoing.finish()


def encoder_quarters(b_rows, dkv, x_rows, dq, y_rows, e):
    shape = (x_rows.shape[1], 4 * dq.shape[1])
    return kernel_call(
        encoder_quarters_kernel,
        "encoder_quarters",
        in_specs=[WHOLE] * 6,
        out_specs=[IN_HBM] * 4,
        out_shape=[OUT_HBM(shape, bf16)] * 4,
        scratch_shapes=[pltpu.VMEM(shape, bf16)] * 4 + [pltpu.SemaphoreType.DMA((4,))],
    )(b_rows, dkv, x_rows, dq, y_rows, e)


def byte_partial_kernel(dkv, dq, wk, wv, wq, own, sent, query_own, query_sent):
    half = wk.shape[1]
    count, rows = own.shape[0], query_own.shape[0]
    for at, out in ((0, own), (count, sent)):
        total = times_transposed(dkv[at : at + count, :half], wk[...])
        total = total + times_transposed(dkv[at : at + count, half:], wv[...])
        out[...] = total.astype(out.dtype)
    total = times_transposed(dq[...], wq[...])
    query_own[...] = total[:rows]
    query_sent[...] = total[rows:].astype(bf16)


def byte_partial(dkv, dq, wk, wv, wq):
    width = wk.shape[0]
    count, rows = dkv.shape[0] // 2, dq.shape[0] // 2
    return kernel_call(
        byte_partial_kernel,
        "byte_partial",
        in_specs=[WHOLE] * 5,
        out_specs=[WHOLE] * 4,
        out_shape=[
            of((count, width), f32),
            of((count, width), bf16),
            of((rows, width), f32),
            of((rows, width), bf16),
        ],
    )(dkv, dq, wk, wv, wq)


def byte_grad_kernel(raw, own, came, query_own, query_came, pooled, embed, member, size, gains, out):
    pool = pooled[...]
    grad = query_own[...] + query_came[...].astype(f32)
    share = embed[...].astype(f32) + normalize_back(pool, inverse_rms(pool), gains[0:1], grad)
    share = share / size[...]
    high = share.astype(bf16)
    rest = (share - high.astype(f32)).astype(bf16)
    spread = transposed_times(member[...], high) + transposed_times(member[...], rest)
    v = raw[...].astype(f32)
    grad = own[...] + came[...].astype(f32)
    out[...] = spread + normalize_back(v, inverse_rms(v), gains[1:2], grad)


def byte_gradient(*args):
    return kernel_call(
        byte_grad_kernel,
        "byte_gradient",
        in_specs=[WHOLE] * 10,
        out_specs=WHOLE,
        out_shape=of(args[0].shape, f32),
    )(*args)


def patch_tables(lengths, documents):
    patches, count = lengths.shape[1], documents.shape[1]
    ends = jnp.cumsum(lengths, axis=1, dtype=jnp.int32)
    starts = ends - lengths
    position = lax.broadcasted_iota(jnp.int32, (1, patches, count), 2)
    member = (position >= starts[:, :, None]) & (position < ends[:, :, None])
    first_doc = jnp.sum(
        jnp.where(position == starts[:, :, None], documents[:, None, :], 0), axis=2
    )
    allowed = member & (documents[:, None, :] == first_doc[:, :, None])
    order_rows = lax.broadcasted_iota(jnp.int32, (1, patches, patches), 1)
    order_cols = lax.broadcasted_iota(jnp.int32, (1, patches, patches), 2)
    causal = (order_cols <= order_rows) & (first_doc[:, None, :] == first_doc[:, :, None])
    return member.astype(bf16), allowed.astype(f32), causal.astype(f32)


def own_first(pair, section):
    return jnp.where(section == 0, pair, pair[::-1])


def shards(
    byte_states,
    patch_lengths,
    doc_ids,
    proj_weights,
    out_weights,
    norm_gains,
    in_weights,
    down_weights,
    cotangent,
):
    section = lax.axis_index("section")
    scalars = jnp.stack([section, place("y"), place("x"), place("z")]).astype(jnp.int32)
    scalars, section = stage(scalars, section)
    width = byte_states.shape[-1]
    half = width // 2
    units = down_weights.shape[1]

    own_w = jnp.concatenate([proj_weights[0], out_weights], axis=0)
    own_w = own_w.transpose(1, 0, 2).reshape(16, 4, 2, half)
    gains_own = jnp.pad(norm_gains[0].T, ((0, 0), (0, 126)))
    keep = jnp.where(section == 0, own_w[:, :, 0], own_w[:, :, 1]).reshape(16, 4 * half)
    give = jnp.where(section == 0, own_w[:, :, 1], own_w[:, :, 0]).reshape(16, 4 * half)
    got = across(jnp.concatenate([give, gains_own], axis=1))
    enc = jnp.where(section == 0, keep, got[:, : 4 * half])
    glob = jnp.where(section == 0, got[:, : 4 * half], keep)
    gains_first = jnp.where(section == 0, gains_own, got[:, 4 * half :])
    gains_last = jnp.where(section == 0, got[:, 4 * half :], gains_own)
    gains = jnp.concatenate([gains_first[:, :2], gains_last[:, :126]], axis=1)
    packed = jnp.concatenate(
        [glob, in_weights[0], in_weights[1], down_weights], axis=1
    )
    packed = lax.all_gather(packed, "fsdp", axis=0, tiled=True)

    pack = jnp.concatenate(
        [enc[:, half : 3 * half], gains, enc[:, :half], enc[:, 3 * half :]], axis=1
    )
    first = 2 * half + 128
    pack = gather_direct(pack[None], "z", 0).reshape(64, -1)
    on_y = gather_direct(pack[None, :, :first], "x", 0).reshape(256, -1)
    on_x = gather_direct(pack[None, :, first:], "y", 0)
    places = jnp.stack([place("y"), place("x")])
    wk0, wv0, gains, wq0, wo0 = lay(places, ring_pieces(on_y, "y"), ring_pieces(on_x, "x"), half)
    pick = (
        lax.broadcasted_iota(jnp.int32, (8, 128), 0) == lax.broadcasted_iota(jnp.int32, (8, 128), 1)
    ).astype(bf16)
    gains = times_transposed(pick, gains)
    wo0_other = across(wo0)

    own_bytes, own_target = byte_states[0, 0], cotangent[0, 0]
    raw = jnp.concatenate([own_bytes, across(own_bytes)], axis=0)
    target = jnp.concatenate([own_target, across(own_target)], axis=0)
    lengths = own_first(patch_lengths[:, 0], section)
    documents = own_first(doc_ids[:, 0], section)
    patches, count = lengths.shape[1], documents.shape[1]
    member, allowed, causal = patch_tables(lengths, documents)
    size = lengths.astype(f32).reshape(-1, 1)

    raw_f32 = raw.astype(f32)
    pooled = lax.dot_general(
        member,
        raw.reshape(2, count, width),
        (((2,), (1,)), ((0,), (0,))),
        preferred_element_type=f32,
    ).reshape(2 * patches, width)
    pooled = pooled / size
    query_low = (pooled * inverse_rms(pooled) * gains[0]).astype(bf16)
    byte_low = (raw_f32 * inverse_rms(raw_f32) * gains[1]).astype(bf16)
    q0, k0, v0, mixed, mixed_sent = encoder_forward(query_low, byte_low, wq0, wk0, wv0, allowed)
    byte_rows, query_rows, target_rows = prepare(
        scalars, byte_low, query_low, target, ENC_AXES, FFN_AXES
    )
    hidden, normed_low, mixed_rows, normed_rows = encoder_out(
        scalars, pooled, mixed, across(mixed_sent), wo0, wo0_other, gains, ENC_AXES, GLOB_AXES[0]
    )
    (
        packed, hidden, normed_low, mixed_rows, normed_rows, byte_rows, query_rows, target_rows, causal,
    ) = stage(
        packed, hidden, normed_low, mixed_rows, normed_rows, byte_rows, query_rows, target_rows, causal,
    )
    wo1 = packed[:, 3 * half : 4 * half]
    wo1_other = across(wo1)
    packed = pltpu.with_memory_space_constraint(packed, pltpu.HBM)
    q1, k1, v1, mixed, mixed_sent = global_forward(normed_low, packed, causal, half)
    (
        mixed1, middle, ffn_partial, ffn_sent, block_out, block_sent, far_a, far_b, up_part, down_part,
        own_part,
    ) = feed_forward(
        scalars, hidden, mixed, across(mixed_sent), wo1, wo1_other, gains, target, target_rows,
        packed, units, 4 * half, FFN_AXES,
    )
    ffn_came, far_a, far_b = stage(across(ffn_sent), far_a, far_b)

    far_a, far_b = shift_by_core(far_a, FFN_AXES, 1), shift_by_core(far_b, FFN_AXES, -1)
    middle_grad, middle_half, dqkv, normed_partial, normed_sent = global_back(
        scalars, target, middle, ffn_partial, ffn_came, gains, wo1, wo1_other,
        q1, k1, v1, causal, packed,
    )
    glob_parts = global_quarters(
        scalars, normed_rows, dqkv, mixed1, middle_half, GLOB_AXES[0]
    )
    far_a, far_b, normed_sent, glob_parts = stage(far_a, far_b, normed_sent, glob_parts)

    up_part, down_part = near(up_part, down_part, far_a, far_b)
    normed_came, up_part, down_part = stage(across(normed_sent), up_part, down_part)
    up_came, down_came = (
        shift_by_core(up_part, FFN_AXES, 1),
        shift_by_core(down_part, FFN_AXES, -1),
    )
    glob_came = send_near(glob_parts, GLOB_AXES[0])
    embed, embed_half, dq, dkv = encoder_back(
        scalars, middle_grad, hidden, normed_partial, normed_came, gains, wo0, wo0_other,
        q0, k0, v0, allowed,
    )
    enc_parts = encoder_quarters(byte_rows, dkv, query_rows, dq, mixed_rows, embed_half)
    up_came, down_came, glob_came, glob_parts, enc_parts, dq, dkv = stage(
        up_came, down_came, glob_came, glob_parts, enc_parts, dq, dkv
    )

    enc_came = send_near(enc_parts, ENC_AXES)
    glob_came.append(send_far(glob_parts, GLOB_AXES[0]))
    byte_own, byte_sent, query_own, query_sent = byte_partial(dkv, dq, wk0, wv0, wq0)
    ffn_line = line_total(own_part, up_came, down_came)
    ffn_line, enc_came, enc_parts, glob_came, byte_sent, query_sent = stage(
        ffn_line, enc_came, enc_parts, glob_came, byte_sent, query_sent
    )

    enc_line = line_total(enc_parts[0], *enc_came)
    glob_parts = split(scalars, [glob_parts[0], *glob_came], GLOB_AXES[1], ("yx", "yx"))
    ffn_line, enc_line, glob_parts = stage(ffn_line, enc_line, glob_parts)
    enc_far = send_far(enc_parts, ENC_AXES)
    ffn_sum = plane_sum(ffn_line, FFN_AXES)
    glob_came = send_quarters(glob_parts, GLOB_AXES[1])
    byte_grad = byte_gradient(
        own_bytes, byte_own, across(byte_sent), query_own, across(query_sent),
        pooled[:patches], embed[:patches], member[0], size[:patches], gains,
    )
    block_out = block_out + across(block_sent).astype(f32)
    enc_far, ffn_sum, glob_came, block_out, byte_grad = stage(
        enc_far, ffn_sum, glob_came, block_out, byte_grad
    )

    enc_line = line_total(enc_line, enc_far)
    glob_parts = split(scalars, [glob_parts[0], *glob_came], GLOB_AXES[2], ("x", "y"))
    enc_line, glob_parts = stage(enc_line, glob_parts)
    enc_sum = plane_sum(enc_line, ENC_AXES)
    glob_sum = sum(p.astype(f32) for p in [glob_parts[0], *send_quarters(glob_parts, GLOB_AXES[2])])

    gate_sum, up_sum, down_sum = jnp.split(ffn_sum, 3, axis=1)
    mine = jnp.where(section == 0, enc_sum, glob_sum)
    theirs = across(jnp.where(section == 0, glob_sum, enc_sum))
    first = jnp.where(section == 0, mine, theirs)
    last = jnp.where(section == 0, theirs, mine)
    sums = jnp.stack(
        [
            jnp.concatenate([x[:, k * half : (k + 1) * half] for x in (first, last)], axis=1)
            for k in range(4)
        ]
    )

    def against(weight, grad):
        return jnp.sum(weight.astype(f32) * grad, axis=-1)

    own_dots = against(proj_weights[0], sums[:3])
    ffn_dots = against(in_weights[0], gate_sum) + against(in_weights[1], up_sum)
    ffn_dots = ffn_dots + across(ffn_dots)
    gain_sum = jnp.where(
        section == 0,
        jnp.stack([own_dots[0], own_dots[1] + own_dots[2]]),
        jnp.stack([own_dots[0] + own_dots[1] + own_dots[2], ffn_dots]),
    )
    gain_sum = gain_sum / norm_gains[0].astype(f32)
    return (
        block_out[None, None],
        byte_grad[None, None],
        sums[None, :3],
        sums[3:],
        gain_sum[None],
        jnp.stack([gate_sum, up_sum]),
        down_sum,
    )


def solution(mesh):
    in_specs = (
        P("section", "fsdp", None, None),
        P(None, "fsdp", None),
        P(None, "fsdp", None),
        P("section", None, "fsdp", None),
        P("section", "fsdp", None),
        P("section", None, "fsdp"),
        P(None, "fsdp", "section"),
        P("fsdp", "section"),
        P("section", "fsdp", None, None),
    )
    out_specs = (
        P("section", "fsdp", None, None),
        P("section", "fsdp", None, None),
        P("section", None, "fsdp", None),
        P("section", "fsdp", None),
        P("section", None, "fsdp"),
        P(None, "fsdp", "section"),
        P("fsdp", "section"),
    )
    return jax.shard_map(shards, mesh=mesh, in_specs=in_specs, out_specs=out_specs, check_vma=False)
```

```python
import functools

import jax
import jax.numpy as jnp
from jax import lax
from jax.experimental import pallas as pl
from jax.experimental.pallas import tpu as pltpu
from jax.sharding import PartitionSpec as P

HEADS = 16
HEAD_DIM = 64
QUAD = 4
LANES = QUAD * HEAD_DIM
RING = 4
STRIDE = {"y": 16, "x": 4, "z": 1}

FFN_AXES = ("y", "x")
ENC_AXES = ("x", "y")
GLOB_AXES = (("z", "z"), ("y", "x"), ("x", "y"))

epsilon = 1e-05
masked_score = -1e30
bf16 = jnp.bfloat16
f32 = jnp.float32

SCALAR = pl.BlockSpec(memory_space=pltpu.SMEM)
WHOLE = pl.BlockSpec(memory_space=pltpu.VMEM)
IN_HBM = pl.BlockSpec(memory_space=pltpu.HBM)
OUT_HBM = pltpu.HBM
QUICK = pl.CostEstimate(flops=1, bytes_accessed=1, transcendentals=0)


def of(shape, kind):
    return jax.ShapeDtypeStruct(shape, kind)


ROOM = {
    "lay": 6,
    "prepare": 8,
    "encoder_forward": 12,
    "encoder_out": 8,
    "global_forward": 8,
    "feed_forward": 28,
    "global_back": 12,
    "global_quarters": 10,
    "near": 10,
    "split": 10,
    "line_total": 10,
    "encoder_back": 14,
    "encoder_quarters": 10,
    "byte_partial": 12,
    "byte_gradient": 8,
}


def kernel_call(body, name, **options):
    return pl.pallas_call(
        body,
        name=name,
        cost_estimate=QUICK,
        compiler_params=pltpu.CompilerParams(vmem_limit_bytes=ROOM[name] << 20),
        **options,
    )


def across(block):
    return lax.ppermute(block, "section", [(0, 1), (1, 0)])


def moved(i, ax, by):
    step = STRIDE[ax]
    c = (i // step) % RING
    return i + ((c + by) % RING - c) * step


def shift(block, ax, by):
    return lax.ppermute(block, "fsdp", [(i, moved(i, ax, by)) for i in range(64)])


def shift_by_core(block, axes, by):
    route = [(64 * s + i, 64 * s + moved(i, ax, by)) for s, ax in enumerate(axes) for i in range(64)]
    return lax.ppermute(block, ("section", "fsdp"), route)


def place(ax):
    return (lax.axis_index("fsdp") // STRIDE[ax]) % RING


def planes(axes):
    rows = {}
    for s, ax in enumerate(axes):
        for i in range(64):
            rows.setdefault((s, (i // STRIDE[ax]) % RING), []).append(64 * s + i)
    return list(rows.values())


def lines(axes):
    rows = {}
    for s, ax in enumerate(axes):
        for i in range(64):
            c = (i // STRIDE[ax]) % RING
            rows.setdefault((s, i - c * STRIDE[ax]), []).append(64 * s + i)
    return list(rows.values())


def put(whole, piece, at, dim):
    where = [0] * whole.ndim
    where[dim] = at
    return lax.dynamic_update_slice(whole, piece, where)


def gather_direct(block, ax, dim):
    c = place(ax)
    whole = jnp.zeros((*block.shape[:dim], RING, *block.shape[dim + 1 :]), block.dtype)
    arrived = [(shift(block, ax, by), (c - by) % RING) for by in (1, -1, 2)]
    for piece, at in [(block, c)] + arrived:
        whole = put(whole, piece, at, dim)
    return whole


def ring_pieces(block, ax):
    half = block.shape[-1] // 256 * 128
    last = block.ndim - 1
    below, above = shift(block, ax, 1), shift(block, ax, -1)
    first = shift(lax.slice_in_dim(below, 0, half, axis=last), ax, 1)
    second = shift(lax.slice_in_dim(above, half, None, axis=last), ax, -1)
    return block, above, below, first, second


def columns(pieces, k, begin, end):
    if k != 2:
        return pieces[(0, 1, None, 2)[k]][..., begin:end]
    first, second = pieces[3:]
    cut = first.shape[-1]
    if end <= cut:
        return first[..., begin:end]
    if begin >= cut:
        return second[..., begin - cut : end - cut]
    return jnp.concatenate([first[..., begin:], second[..., : end - cut]], axis=-1)


def lay_kernel(c_ref, *refs):
    ins, outs = refs[:10], refs[10:]
    for ax, pieces, targets in (("y", ins[:5], outs[:3]), ("x", ins[5:], outs[3:])):
        c = c_ref[0 if ax == "y" else 1]
        for k in range(RING):
            at = lax.rem(c + k, RING)
            column = 0
            for out in targets:
                value = columns(pieces, k, column, column + out.shape[-1])
                if ax == "y":
                    out[at] = value
                else:
                    out[:, at] = value
                column += out.shape[-1]


def lay(places, on_y, on_x, half):
    rows = on_y[0].shape[0]
    wide = (half, half, on_y[0].shape[1] - 2 * half)
    outs = [of((RING, rows, w), bf16) for w in wide]
    outs += [of((RING, RING, rows // RING, half), bf16)] * 2
    made = kernel_call(
        lay_kernel,
        "lay",
        in_specs=[SCALAR] + [WHOLE] * 10,
        out_specs=[WHOLE] * 5,
        out_shape=outs,
    )(places, *on_y, *on_x)
    return [m.reshape(RING * rows, m.shape[-1]) for m in made]


def send_near(parts, axes):
    return [shift_by_core(parts[1], axes, 1), shift_by_core(parts[3], axes, -1)]


def send_far(parts, axes):
    return shift_by_core(parts[2], axes, 2)


def send_quarters(parts, axes):
    return [*send_near(parts, axes), send_far(parts, axes)]


def total_kernel(*refs):
    total = refs[0][...].astype(f32)
    for part in refs[1:-1]:
        total = total + part[...].astype(f32)
    refs[-1][...] = total.astype(bf16)


def line_total(*parts):
    return kernel_call(
        total_kernel,
        "line_total",
        in_specs=[WHOLE] * len(parts),
        out_specs=WHOLE,
        out_shape=of(parts[0].shape, bf16),
    )(*parts)


def split_kernel(axes, names, s_ref, *refs):
    n = len(refs) - 2 * RING - 1
    targets, refs, sent = refs[n : n + RING], refs[:n] + refs[n + RING : -1], refs[-1]
    total = refs[0][...].astype(f32)
    for part in refs[1:n]:
        total = total + part[...].astype(f32)
    total = total.astype(bf16)
    outs = refs[n:]
    for s, ax in enumerate(axes):

        @pl.when(s_ref[0] == s)
        def _():
            c = s_ref[1 + "yxz".index(ax)]
            dim = names[s].index(ax)
            blocks = total.reshape(*[RING] * len(names[s]), -1, total.shape[1])
            for at in range(RING):
                block = lax.index_in_dim(blocks, at, dim, keepdims=False)
                k = lax.rem(at + RING - c, RING)
                for j in range(RING):

                    @pl.when(k == j)
                    def _():
                        outs[j][...] = block.reshape(outs[j].shape)

    outgoing = Outgoing(outs, targets, sent)
    for k in range(RING):
        outgoing.send(k)
    outgoing.finish()


def split(scalars, parts, axes, names):
    rows, wide = parts[0].shape
    return kernel_call(
        functools.partial(split_kernel, axes, names),
        "split",
        in_specs=[SCALAR] + [WHOLE] * len(parts),
        out_specs=[IN_HBM] * RING,
        out_shape=[OUT_HBM((rows // RING, wide), bf16)] * RING,
        scratch_shapes=[pltpu.VMEM((rows // RING, wide), bf16)] * RING
        + [pltpu.SemaphoreType.DMA((RING,))],
    )(scalars, *parts)


def near_kernel(up, down, a, b, up_out, down_out):
    cut = a.shape[1]
    up_out[:, :cut] = (up[:, :cut].astype(f32) + a[...].astype(f32)).astype(bf16)
    up_out[:, cut:] = up[:, cut:]
    down_out[:, cut:] = (down[:, cut:].astype(f32) + b[...].astype(f32)).astype(bf16)
    down_out[:, :cut] = down[:, :cut]


def near(up, down, a, b):
    return kernel_call(
        near_kernel,
        "near",
        in_specs=[WHOLE] * 4,
        out_specs=[WHOLE] * 2,
        out_shape=[of(up.shape, bf16)] * 2,
    )(up, down, a, b)


def line_sum(parts, axes):
    return lax.psum_scatter(
        parts,
        ("section", "fsdp"),
        scatter_dimension=0,
        axis_index_groups=lines(axes),
        tiled=False,
    )


def plane_sum(part, axes):
    blocks = part.reshape(16, part.shape[0] // 16, part.shape[1])
    blocks = lax.all_to_all(
        blocks, ("section", "fsdp"), 0, 0, axis_index_groups=planes(axes), tiled=True
    )
    return jnp.sum(blocks.astype(f32), axis=0)


def stage(*values):
    return lax.optimization_barrier(values)


def inverse_rms(values):
    return lax.rsqrt(jnp.mean(values * values, axis=-1, keepdims=True) + epsilon)


def normalize_back(values, inverse, scales, gradient):
    unit_rows = values * inverse
    scaled = gradient * scales
    inner_mean = jnp.mean(scaled * unit_rows, axis=-1, keepdims=True)
    return inverse * (scaled - unit_rows * inner_mean)


def matmul(left, right):
    return jnp.dot(left, right, preferred_element_type=f32)


def times_transposed(left, right):
    return lax.dot_general(left, right, (((1,), (1,)), ((), ())), preferred_element_type=f32)


def transposed_times(left, right):
    return lax.dot_general(left, right, (((0,), (0,)), ((), ())), preferred_element_type=f32)


def of_head(value, h):
    head = lax.broadcasted_iota(jnp.int32, value.shape, 1) // HEAD_DIM
    return jnp.where(head == h, value, jnp.zeros_like(value))


def stacked(value):
    return jnp.concatenate([of_head(value, h) for h in range(QUAD)], axis=0)


def unstacked(value, rows):
    total = of_head(value[:rows], 0)
    for h in range(1, QUAD):
        total = total + of_head(value[h * rows : (h + 1) * rows], h)
    return total


def probabilities(q4, keys, table):
    raw = times_transposed(q4, keys)
    allowed = jnp.concatenate([table] * QUAD, axis=0) > 0
    scores = jnp.where(allowed, raw * HEAD_DIM ** (-0.5), masked_score)
    weights = jnp.exp(scores - jnp.max(scores, axis=-1, keepdims=True))
    return weights / jnp.sum(weights, axis=-1, keepdims=True)


def attend(q, k, v, table):
    p = probabilities(stacked(q), k, table).astype(bf16)
    return unstacked(matmul(p, v), q.shape[0]).astype(bf16)


def attend_back(q, k, v, table, d):
    rows = q.shape[0]
    q4, d4 = stacked(q), stacked(d)
    p = probabilities(q4, k, table)
    dp = times_transposed(d4, v)
    ds = p * (dp - jnp.sum(p * dp, axis=-1, keepdims=True)) * HEAD_DIM ** (-0.5)
    ds = ds.astype(bf16)
    dq = unstacked(matmul(ds, k), rows).astype(bf16)
    dk = transposed_times(ds, q4).astype(bf16)
    dv = transposed_times(p.astype(bf16), d4).astype(bf16)
    return dq, dk, dv


def lanes_of(section, half):
    mine = pl.ds(pl.multiple_of(section * half, half), half)
    theirs = pl.ds(pl.multiple_of((1 - section) * half, half), half)
    return mine, theirs


def merge(scratch, section, own, other):
    mine, theirs = lanes_of(section, own.shape[1])
    scratch[:, mine] = own
    scratch[:, theirs] = other


def swap_rows(x):
    half = x.shape[0] // 2
    return jnp.concatenate([x[half:], x[:half]], axis=0)


def quarter(turned, ax, at):
    if ax == "y":
        rows = turned[at]
    elif ax == "x":
        rows = turned[:, at]
    else:
        rows = turned[:, :, at]
    return rows.reshape(turned.shape[0] ** 2 * turned.shape[3], turned.shape[4])


def fill_quarters(x_ref, turned, rows, s_ref, axes, first):
    turned[...] = x_ref[...].T.reshape(turned.shape)
    for s, ax in enumerate(axes):

        @pl.when(s_ref[0] == s)
        def _():
            c = s_ref[1 + "yxz".index(ax)] if first else 0
            for k in range(RING):
                rows[k] = quarter(turned, ax, lax.rem(c + k, RING))


def turned_scratch(tokens, features):
    return pltpu.VMEM((RING, RING, RING, features // RING**3, tokens), bf16)


def quarter_scratch(tokens, features):
    return [
        turned_scratch(tokens, features),
        pltpu.VMEM((RING, features // RING, tokens), bf16),
    ]


def rows_of(x):
    return of((RING, x.shape[1] // RING, x.shape[0]), bf16)


def prepare_kernel(enc_axes, ffn_axes, s_ref, b_ref, x_ref, t_ref, b_rows, x_rows, t_rows, *turned):
    fill_quarters(b_ref, turned[0], b_rows, s_ref, enc_axes, True)
    fill_quarters(x_ref, turned[1], x_rows, s_ref, enc_axes, True)
    fill_quarters(t_ref, turned[2], t_rows, s_ref, ffn_axes, True)


def prepare(scalars, b, x, t, enc_axes, ffn_axes):
    return kernel_call(
        functools.partial(prepare_kernel, enc_axes, ffn_axes),
        "prepare",
        in_specs=[SCALAR] + [WHOLE] * 3,
        out_specs=[WHOLE] * 3,
        out_shape=[rows_of(a) for a in (b, x, t)],
        scratch_shapes=[turned_scratch(*a.shape) for a in (b, x, t)],
    )(scalars, b, x, t)


def encoder_kernel(x_ref, b_ref, wq, wk, wv, table, q_ref, k_ref, v_ref, mixed, mixed_swapped):
    q = matmul(x_ref[...], wq[...]).astype(bf16)
    k = matmul(b_ref[...], wk[...]).astype(bf16)
    v = matmul(b_ref[...], wv[...]).astype(bf16)
    q_ref[...], k_ref[...], v_ref[...] = q, k, v
    out = attend(q, k, v, table[0])
    mixed[...] = out
    mixed_swapped[...] = out


def encoder_forward(query_low, byte_low, wq, wk, wv, table):
    micro, rows, keys = table.shape
    width, half = wq.shape
    weight = pl.BlockSpec((width, LANES), lambda h, m: (0, h))
    per_row = pl.BlockSpec((rows, LANES), lambda h, m: (m, h))
    per_key = pl.BlockSpec((keys, LANES), lambda h, m: (m, h))
    return kernel_call(
        encoder_kernel,
        "encoder_forward",
        grid=(half // LANES, micro),
        in_specs=[
            pl.BlockSpec((rows, width), lambda h, m: (m, 0)),
            pl.BlockSpec((keys, width), lambda h, m: (m, 0)),
            weight,
            weight,
            weight,
            pl.BlockSpec((1, rows, keys), lambda h, m: (m, 0, 0)),
        ],
        out_specs=[
            per_row,
            per_key,
            per_key,
            per_row,
            pl.BlockSpec((rows, LANES), lambda h, m: (1 - m, h)),
        ],
        out_shape=[
            of((micro * rows, half), bf16),
            of((micro * keys, half), bf16),
            of((micro * keys, half), bf16),
            of((micro * rows, half), bf16),
            of((micro * rows, half), bf16),
        ],
    )(query_low, byte_low, wq, wk, wv, table)


def encoder_out_kernel(
    enc_axes, glob_axes, s_ref, pooled, own, other, wo, wo_other, gains,
    hidden_ref, low_ref, mixed_rows, low_rows, whole_ref, sum_ref, turned_mixed, turned_low,
):
    section = s_ref[0]
    merge(whole_ref, section, own[...], other[...])
    whole = whole_ref[...]
    merge(sum_ref, section, matmul(whole, wo[...]), matmul(whole, wo_other[...]))
    low_hidden = (pooled[...] + sum_ref[...]).astype(bf16)
    hidden_ref[...] = low_hidden
    hidden = low_hidden.astype(f32)
    low = (hidden * inverse_rms(hidden) * gains[2:3]).astype(bf16)
    low_ref[...] = low
    fill_quarters(whole, turned_mixed, mixed_rows, s_ref, enc_axes, True)
    fill_quarters(low, turned_low, low_rows, s_ref, glob_axes, True)


def encoder_out(scalars, pooled, own, other, wo, wo_other, gains, enc_axes, glob_axes):
    tokens, width = pooled.shape
    rows = of((RING, width // RING, tokens), bf16)
    return kernel_call(
        functools.partial(encoder_out_kernel, enc_axes, glob_axes),
        "encoder_out",
        in_specs=[SCALAR] + [WHOLE] * 6,
        out_specs=[WHOLE] * 4,
        out_shape=[of((tokens, width), bf16), of((tokens, width), bf16), rows, rows],
        scratch_shapes=[pltpu.VMEM((tokens, width), bf16), pltpu.VMEM((tokens, width), f32)]
        + [turned_scratch(tokens, width)] * 2,
    )(scalars, pooled, own, other, wo, wo_other, gains)


def global_kernel(x_ref, packed, table, q_ref, k_ref, v_ref, mixed, mixed_swapped, weights, sems):
    h, m = pl.program_id(0), pl.program_id(1)
    count = pl.num_programs(0)

    def copy(j, at):
        source = packed.at[:, pl.ds(pl.multiple_of((j * count + at) * LANES, LANES), LANES)]
        return pltpu.make_async_copy(source, weights.at[at, j], sems.at[at, j])

    @pl.when((h == 0) & (m == 0))
    def _():
        for at in range(weights.shape[0]):
            for j in range(3):
                copy(j, at).start()

    @pl.when(m == 0)
    def _():
        for j in range(3):
            copy(j, h).wait()

    x = x_ref[...]
    q, k, v = (matmul(x, weights[h, j]).astype(bf16) for j in range(3))
    q_ref[...], k_ref[...], v_ref[...] = q, k, v
    out = attend(q, k, v, table[0])
    mixed[...] = out
    mixed_swapped[...] = out


def global_forward(x, packed, table, half):
    micro, rows, _ = table.shape
    width = x.shape[1]
    count = half // LANES
    per_row = pl.BlockSpec((rows, LANES), lambda h, m: (m, h))
    return kernel_call(
        global_kernel,
        "global_forward",
        grid=(count, micro),
        in_specs=[
            pl.BlockSpec((rows, width), lambda h, m: (m, 0)),
            IN_HBM,
            pl.BlockSpec((1, rows, rows), lambda h, m: (m, 0, 0)),
        ],
        out_specs=[per_row] * 4 + [pl.BlockSpec((rows, LANES), lambda h, m: (1 - m, h))],
        out_shape=[of((micro * rows, half), bf16)] * 5,
        scratch_shapes=[
            pltpu.VMEM((count, 3, width, LANES), bf16),
            pltpu.SemaphoreType.DMA((count, 3)),
        ],
    )(x, packed, table)


class Outgoing:
    def __init__(self, buffers, targets, sems):
        self.copies = [
            pltpu.make_async_copy(b, t, sems.at[k]) for k, (b, t) in enumerate(zip(buffers, targets))
        ]

    def send(self, k):
        self.copies[k].start()

    def finish(self):
        for copy in self.copies:
            copy.wait()


def ffn_kernel(
    units, at, axes, s_ref, hidden, own, other, wo, wo_other, gains, target, rows_target, packed,
    mixed_whole, middle_ref, partial, partial_sent, result, result_sent, far_a, far_b, up_part,
    down_part, own_part, w_gate, w_up, w_down, turned, rows, up_made, down_made, own_made, sems, sent,
):
    outgoing = Outgoing((up_made, down_made, own_made), (up_part, down_part, own_part), sent)
    copies = [
        pltpu.make_async_copy(packed.at[:, pl.ds(at + k * units, units)], w, sems.at[k])
        for k, w in enumerate((w_gate, w_up, w_down))
    ]
    for copy in copies:
        copy.start()
    section = s_ref[0]
    merge(mixed_whole, section, own[...], other[...])
    whole = mixed_whole[...]
    merge(middle_ref, section, matmul(whole, wo[...]), matmul(whole, wo_other[...]))
    middle = hidden[...].astype(f32) + middle_ref[...]
    middle_ref[...] = middle
    low = (middle * inverse_rms(middle) * gains[3:4]).astype(bf16)
    copies[0].wait()
    gate = matmul(low, w_gate[...])
    copies[1].wait()
    up = matmul(low, w_up[...])
    sigma = jax.nn.sigmoid(gate)
    inner = (gate * sigma * up).astype(bf16)
    copies[2].wait()
    inner_grad = matmul(target[...], w_down[...])
    up_grad = (inner_grad * gate * sigma).astype(bf16)
    gate_grad = (inner_grad * up * sigma * (1.0 + gate * (1.0 - sigma))).astype(bf16)
    half = partial.shape[0] // 2
    total = times_transposed(gate_grad, w_gate[...]) + times_transposed(up_grad, w_up[...])
    partial[...] = total
    partial_sent[...] = swap_rows(total.astype(bf16))
    out = times_transposed(inner, w_down[...])
    result[...] = middle[:half] + out[:half]
    result_sent[...] = out[half:].astype(bf16)
    fill_quarters(low, turned, rows, s_ref, axes, True)
    cut = far_a.shape[1]
    for k, part in ((1, up_made), (3, down_made), (0, own_made), (2, None)):
        for j, (x, d) in enumerate(((rows, gate_grad), (rows, up_grad), (rows_target, inner))):
            value = matmul(x[k], d).astype(bf16)
            begin, end = j * units, (j + 1) * units
            if part is not None:
                part[:, begin:end] = value
            elif end <= cut:
                far_a[:, begin:end] = value
            elif begin >= cut:
                far_b[:, begin - cut : end - cut] = value
            else:
                far_a[:, begin:] = value[:, : cut - begin]
                far_b[:, : end - cut] = value[:, cut - begin :]
        if part is not None:
            outgoing.send({1: 0, 3: 1, 0: 2}[k])
    outgoing.finish()


def feed_forward(
    scalars, hidden, own, other, wo, wo_other, gains, target, rows, packed, units, at, axes
):
    tokens, width = hidden.shape
    part = tokens // 2
    block = width // RING
    cut = 3 * units // 256 * 128
    return kernel_call(
        functools.partial(ffn_kernel, units, at, axes),
        "feed_forward",
        in_specs=[SCALAR] + [WHOLE] * 8 + [IN_HBM],
        out_specs=[WHOLE] * 8 + [IN_HBM] * 3,
        out_shape=[
            of((tokens, width), bf16),
            of((tokens, width), f32),
            of((tokens, width), f32),
            of((tokens, width), bf16),
            of((part, width), f32),
            of((part, width), bf16),
            of((block, cut), bf16),
            of((block, 3 * units - cut), bf16),
        ]
        + [OUT_HBM((block, 3 * units), bf16)] * 3,
        scratch_shapes=[pltpu.VMEM((width, units), bf16)] * 3
        + quarter_scratch(tokens, width)
        + [pltpu.VMEM((block, 3 * units), bf16)] * 3
        + [pltpu.SemaphoreType.DMA((3,))] * 2,
    )(scalars, hidden, own, other, wo, wo_other, gains, target, rows, packed)


def global_back_kernel(
    s_ref, target, middle, partial, came, gains, wo, wo_other, q_ref, k_ref, v_ref, table, packed,
    middle_grad, middle_half, dqkv, out, out_sent, mixed_grad, low, w_qkv, sem,
):
    rows, half = table.shape[1], wo.shape[1]
    m, h = pl.program_id(0), pl.program_id(1)
    copy = pltpu.make_async_copy(packed.at[:, pl.ds(0, 3 * half)], w_qkv, sem)

    @pl.when((m == 0) & (h == 0))
    def _():
        copy.start()
        section = s_ref[0]
        v = middle[...]
        grad = partial[...] + came[...].astype(f32)
        grad = target[...].astype(f32) + normalize_back(v, inverse_rms(v), gains[3:4], grad)
        middle_grad[...] = grad
        low[...] = grad.astype(bf16)
        mine, theirs = lanes_of(section, half)
        middle_half[...] = low[:, mine]
        own_rows = pl.ds(pl.multiple_of(section * half, half), half)
        mixed_grad[...] = (
            times_transposed(low[:, mine], wo[own_rows])
            + times_transposed(low[:, theirs], wo_other[own_rows])
        ).astype(bf16)

    here = pl.ds(pl.multiple_of(m * rows, rows), rows)
    at = pl.multiple_of(h * LANES, LANES)
    quad = pl.ds(at, LANES)
    dq, dk, dv = attend_back(
        q_ref[here, quad], k_ref[here, quad], v_ref[here, quad], table[0], mixed_grad[here, quad]
    )
    dqkv[here, quad] = dq
    dqkv[here, pl.ds(at + half, LANES)] = dk
    dqkv[here, pl.ds(at + 2 * half, LANES)] = dv

    @pl.when((m == pl.num_programs(0) - 1) & (h == pl.num_programs(1) - 1))
    def _():
        copy.wait()
        total = times_transposed(dqkv[...], w_qkv[...])
        out[...] = total
        out_sent[...] = swap_rows(total.astype(bf16))


def global_back(section, target, middle, partial, came, gains, wo, wo_other, q, k, v, table, packed):
    micro, rows, _ = table.shape
    tokens, width = middle.shape
    half = wo.shape[1]

    def fixed(shape):
        return pl.BlockSpec(shape, lambda m, h: (0, 0))

    return kernel_call(
        global_back_kernel,
        "global_back",
        grid=(micro, half // LANES),
        in_specs=[SCALAR]
        + [fixed((tokens, width))] * 4
        + [fixed(gains.shape)]
        + [fixed((width, half))] * 2
        + [fixed((tokens, half))] * 3
        + [pl.BlockSpec((1, rows, rows), lambda m, h: (m, 0, 0)), IN_HBM],
        out_specs=[
            fixed((tokens, width)),
            fixed((tokens, half)),
            fixed((tokens, 3 * half)),
            fixed((tokens, width)),
            fixed((tokens, width)),
        ],
        out_shape=[
            of((tokens, width), f32),
            of((tokens, half), bf16),
            of((tokens, 3 * half), bf16),
            of((tokens, width), f32),
            of((tokens, width), bf16),
        ],
        scratch_shapes=[
            pltpu.VMEM((tokens, half), bf16),
            pltpu.VMEM((tokens, width), bf16),
            pltpu.VMEM((width, 3 * half), bf16),
            pltpu.SemaphoreType.DMA,
        ],
    )(section, target, middle, partial, came, gains, wo, wo_other, q, k, v, table, packed)


def global_quarters_kernel(axes, s_ref, x_rows, d_ref, y_ref, e_ref, *refs):
    outs, made, (turned, y_rows, sent) = refs[:4], refs[4:8], refs[8:]
    outgoing = Outgoing(made, outs, sent)
    fill_quarters(y_ref, turned, y_rows, s_ref, axes, True)
    for k in (1, 3, 2, 0):
        made[k][:, : d_ref.shape[1]] = matmul(x_rows[k], d_ref[...]).astype(bf16)
        made[k][:, d_ref.shape[1] :] = matmul(y_rows[k], e_ref[...]).astype(bf16)
        outgoing.send(k)
    outgoing.finish()


def global_quarters(scalars, x_rows, d, y, e, axes):
    tokens, width = y.shape
    shape = (width // RING, d.shape[1] + e.shape[1])
    return kernel_call(
        functools.partial(global_quarters_kernel, axes),
        "global_quarters",
        in_specs=[SCALAR] + [WHOLE] * 4,
        out_specs=[IN_HBM] * 4,
        out_shape=[OUT_HBM(shape, bf16)] * 4,
        scratch_shapes=[pltpu.VMEM(shape, bf16)] * 4
        + quarter_scratch(tokens, width)
        + [pltpu.SemaphoreType.DMA((4,))],
    )(scalars, x_rows, d, y, e)


def encoder_back_kernel(
    s_ref, middle_grad, hidden, partial, came, gains, wo, wo_other, q_ref, k_ref, v_ref, table,
    embed, embed_half, dq_ref, dkv_ref, mixed_grad,
):
    rows, keys = table.shape[1:]
    half = wo.shape[1]
    m, h = pl.program_id(0), pl.program_id(1)

    @pl.when((m == 0) & (h == 0))
    def _():
        section = s_ref[0]
        v = hidden[...].astype(f32)
        grad = partial[...] + came[...].astype(f32)
        grad = middle_grad[...] + normalize_back(v, inverse_rms(v), gains[2:3], grad)
        embed[...] = grad.astype(bf16)
        mine, theirs = lanes_of(section, half)
        embed_half[...] = embed[:, mine]
        own_rows = pl.ds(pl.multiple_of(section * half, half), half)
        mixed_grad[...] = (
            times_transposed(embed[:, mine], wo[own_rows])
            + times_transposed(embed[:, theirs], wo_other[own_rows])
        ).astype(bf16)

    here = pl.ds(pl.multiple_of(m * rows, rows), rows)
    at = pl.multiple_of(h * LANES, LANES)
    dq, dk, dv = attend_back(
        q_ref[...], k_ref[...], v_ref[...], table[0], mixed_grad[here, pl.ds(at, LANES)]
    )
    dq_ref[...] = dq
    there = pl.ds(pl.multiple_of(m * keys, keys), keys)
    dkv_ref[there, pl.ds(at, LANES)] = dk
    dkv_ref[there, pl.ds(at + half, LANES)] = dv


def encoder_back(section, middle_grad, hidden, partial, came, gains, wo, wo_other, q, k, v, table):
    micro, rows, keys = table.shape
    tokens, width = hidden.shape
    half = wo.shape[1]

    def fixed(shape):
        return pl.BlockSpec(shape, lambda m, h: (0, 0))

    per_row = pl.BlockSpec((rows, LANES), lambda m, h: (m, h))
    per_key = pl.BlockSpec((keys, LANES), lambda m, h: (m, h))
    return kernel_call(
        encoder_back_kernel,
        "encoder_back",
        grid=(micro, half // LANES),
        in_specs=[SCALAR]
        + [fixed((tokens, width))] * 4
        + [fixed(gains.shape)]
        + [fixed((width, half))] * 2
        + [per_row, per_key, per_key, pl.BlockSpec((1, rows, keys), lambda m, h: (m, 0, 0))],
        out_specs=[
            fixed((tokens, width)),
            fixed((tokens, half)),
            per_row,
            fixed((micro * keys, 2 * half)),
        ],
        out_shape=[
            of((tokens, width), bf16),
            of((tokens, half), bf16),
            of((tokens, half), bf16),
            of((micro * keys, 2 * half), bf16),
        ],
        scratch_shapes=[pltpu.VMEM((tokens, half), bf16)],
    )(section, middle_grad, hidden, partial, came, gains, wo, wo_other, q, k, v, table)


def encoder_quarters_kernel(b_rows, dkv, x_rows, dq, y_rows, e_ref, *refs):
    outs, made, sent = refs[:4], refs[4:8], refs[8]
    half = dq.shape[1]
    outgoing = Outgoing(made, outs, sent)
    for k in (1, 3, 2, 0):
        for rows, d, at in ((x_rows, dq, 0), (b_rows, dkv, half), (y_rows, e_ref, 3 * half)):
            made[k][:, at : at + d.shape[1]] = matmul(rows[k], d[...]).astype(bf16)
        outgoing.send(k)
    outgoing.finish()


def encoder_quarters(b_rows, dkv, x_rows, dq, y_rows, e):
    shape = (x_rows.shape[1], 4 * dq.shape[1])
    return kernel_call(
        encoder_quarters_kernel,
        "encoder_quarters",
        in_specs=[WHOLE] * 6,
        out_specs=[IN_HBM] * 4,
        out_shape=[OUT_HBM(shape, bf16)] * 4,
        scratch_shapes=[pltpu.VMEM(shape, bf16)] * 4 + [pltpu.SemaphoreType.DMA((4,))],
    )(b_rows, dkv, x_rows, dq, y_rows, e)


def byte_partial_kernel(dkv, dq, wk, wv, wq, own, query_own, sent):
    half = wk.shape[1]
    count, rows = own.shape[0], query_own.shape[0]
    for at, out in ((0, own), (count, sent.at[:count])):
        total = times_transposed(dkv[at : at + count, :half], wk[...])
        total = total + times_transposed(dkv[at : at + count, half:], wv[...])
        out[...] = total.astype(out.dtype)
    total = times_transposed(dq[...], wq[...])
    query_own[...] = total[:rows]
    sent[count:] = total[rows:].astype(bf16)


def byte_partial(dkv, dq, wk, wv, wq):
    width = wk.shape[0]
    count, rows = dkv.shape[0] // 2, dq.shape[0] // 2
    return kernel_call(
        byte_partial_kernel,
        "byte_partial",
        in_specs=[WHOLE] * 5,
        out_specs=[WHOLE] * 3,
        out_shape=[
            of((count, width), f32),
            of((rows, width), f32),
            of((count + rows, width), bf16),
        ],
    )(dkv, dq, wk, wv, wq)


def byte_grad_kernel(raw, own, query_own, came, pooled, embed, member, size, gains, out):
    count = raw.shape[0]
    pool = pooled[...]
    grad = query_own[...] + came[count:].astype(f32)
    share = embed[...].astype(f32) + normalize_back(pool, inverse_rms(pool), gains[0:1], grad)
    share = share / size[...]
    high = share.astype(bf16)
    rest = (share - high.astype(f32)).astype(bf16)
    spread = transposed_times(member[...], high) + transposed_times(member[...], rest)
    v = raw[...].astype(f32)
    grad = own[...] + came[:count].astype(f32)
    out[...] = spread + normalize_back(v, inverse_rms(v), gains[1:2], grad)


def byte_gradient(*args):
    return kernel_call(
        byte_grad_kernel,
        "byte_gradient",
        in_specs=[WHOLE] * 9,
        out_specs=WHOLE,
        out_shape=of(args[0].shape, f32),
    )(*args)


def patch_tables(lengths, documents):
    patches, count = lengths.shape[1], documents.shape[1]
    ends = jnp.cumsum(lengths, axis=1, dtype=jnp.int32)
    starts = ends - lengths
    position = lax.broadcasted_iota(jnp.int32, (1, patches, count), 2)
    member = (position >= starts[:, :, None]) & (position < ends[:, :, None])
    first_doc = jnp.sum(
        jnp.where(position == starts[:, :, None], documents[:, None, :], 0), axis=2
    )
    allowed = member & (documents[:, None, :] == first_doc[:, :, None])
    order_rows = lax.broadcasted_iota(jnp.int32, (1, patches, patches), 1)
    order_cols = lax.broadcasted_iota(jnp.int32, (1, patches, patches), 2)
    causal = (order_cols <= order_rows) & (first_doc[:, None, :] == first_doc[:, :, None])
    return member.astype(bf16), allowed.astype(f32), causal.astype(f32)


def own_first(pair, section):
    return jnp.where(section == 0, pair, pair[::-1])


def shards(
    byte_states,
    patch_lengths,
    doc_ids,
    proj_weights,
    out_weights,
    norm_gains,
    in_weights,
    down_weights,
    cotangent,
):
    section = lax.axis_index("section")
    scalars = jnp.stack([section, place("y"), place("x"), place("z")]).astype(jnp.int32)
    scalars, section = stage(scalars, section)
    width = byte_states.shape[-1]
    half = width // 2
    units = down_weights.shape[1]

    own_w = jnp.concatenate([proj_weights[0], out_weights], axis=0)
    own_w = own_w.transpose(1, 0, 2).reshape(16, 4, 2, half)
    gains_own = jnp.pad(norm_gains[0].T, ((0, 0), (0, 126)))
    keep = jnp.where(section == 0, own_w[:, :, 0], own_w[:, :, 1]).reshape(16, 4 * half)
    give = jnp.where(section == 0, own_w[:, :, 1], own_w[:, :, 0]).reshape(16, 4 * half)
    got = across(jnp.concatenate([give, gains_own], axis=1))
    enc = jnp.where(section == 0, keep, got[:, : 4 * half])
    glob = jnp.where(section == 0, got[:, : 4 * half], keep)
    gains_first = jnp.where(section == 0, gains_own, got[:, 4 * half :])
    gains_last = jnp.where(section == 0, got[:, 4 * half :], gains_own)
    gains = jnp.concatenate([gains_first[:, :2], gains_last[:, :126]], axis=1)
    packed = jnp.concatenate(
        [glob, in_weights[0], in_weights[1], down_weights], axis=1
    )
    packed = lax.all_gather(packed, "fsdp", axis=0, tiled=True)

    pack = jnp.concatenate(
        [enc[:, half : 3 * half], gains, enc[:, :half], enc[:, 3 * half :]], axis=1
    )
    first = 2 * half + 128
    pack = gather_direct(pack[None], "z", 0).reshape(64, -1)
    on_y = gather_direct(pack[None, :, :first], "x", 0).reshape(256, -1)
    on_x = gather_direct(pack[None, :, first:], "y", 0)
    places = jnp.stack([place("y"), place("x")])
    wk0, wv0, gains, wq0, wo0 = lay(places, ring_pieces(on_y, "y"), ring_pieces(on_x, "x"), half)
    pick = (
        lax.broadcasted_iota(jnp.int32, (8, 128), 0) == lax.broadcasted_iota(jnp.int32, (8, 128), 1)
    ).astype(bf16)
    gains = times_transposed(pick, gains)
    wo0_other = across(wo0)

    own_bytes, own_target = byte_states[0, 0], cotangent[0, 0]
    raw = jnp.concatenate([own_bytes, across(own_bytes)], axis=0)
    target = jnp.concatenate([own_target, across(own_target)], axis=0)
    lengths = own_first(patch_lengths[:, 0], section)
    documents = own_first(doc_ids[:, 0], section)
    patches, count = lengths.shape[1], documents.shape[1]
    member, allowed, causal = patch_tables(lengths, documents)
    size = lengths.astype(f32).reshape(-1, 1)

    raw_f32 = raw.astype(f32)
    pooled = lax.dot_general(
        member,
        raw.reshape(2, count, width),
        (((2,), (1,)), ((0,), (0,))),
        preferred_element_type=f32,
    ).reshape(2 * patches, width)
    pooled = pooled / size
    query_low = (pooled * inverse_rms(pooled) * gains[0]).astype(bf16)
    byte_low = (raw_f32 * inverse_rms(raw_f32) * gains[1]).astype(bf16)
    q0, k0, v0, mixed, mixed_sent = encoder_forward(query_low, byte_low, wq0, wk0, wv0, allowed)
    byte_rows, query_rows, target_rows = prepare(
        scalars, byte_low, query_low, target, ENC_AXES, FFN_AXES
    )
    hidden, normed_low, mixed_rows, normed_rows = encoder_out(
        scalars, pooled, mixed, across(mixed_sent), wo0, wo0_other, gains, ENC_AXES, GLOB_AXES[0]
    )
    (
        packed, hidden, normed_low, mixed_rows, normed_rows, byte_rows, query_rows, target_rows, causal,
    ) = stage(
        packed, hidden, normed_low, mixed_rows, normed_rows, byte_rows, query_rows, target_rows, causal,
    )
    wo1 = packed[:, 3 * half : 4 * half]
    wo1_other = across(wo1)
    packed = pltpu.with_memory_space_constraint(packed, pltpu.HBM)
    q1, k1, v1, mixed, mixed_sent = global_forward(normed_low, packed, causal, half)
    (
        mixed1, middle, ffn_partial, ffn_sent, block_out, block_sent, far_a, far_b, up_part, down_part,
        own_part,
    ) = feed_forward(
        scalars, hidden, mixed, across(mixed_sent), wo1, wo1_other, gains, target, target_rows,
        packed, units, 4 * half, FFN_AXES,
    )
    ffn_came, far_a, far_b = stage(across(ffn_sent), far_a, far_b)

    far_a, far_b = shift_by_core(far_a, FFN_AXES, 1), shift_by_core(far_b, FFN_AXES, -1)
    middle_grad, middle_half, dqkv, normed_partial, normed_sent = global_back(
        scalars, target, middle, ffn_partial, ffn_came, gains, wo1, wo1_other,
        q1, k1, v1, causal, packed,
    )
    glob_parts = global_quarters(
        scalars, normed_rows, dqkv, mixed1, middle_half, GLOB_AXES[0]
    )
    far_a, far_b, normed_sent, glob_parts, block_came = stage(
        far_a, far_b, normed_sent, glob_parts, across(block_sent)
    )

    up_part, down_part = near(up_part, down_part, far_a, far_b)
    normed_came, up_part, down_part = stage(across(normed_sent), up_part, down_part)
    up_came, down_came = (
        shift_by_core(up_part, FFN_AXES, 1),
        shift_by_core(down_part, FFN_AXES, -1),
    )
    glob_came = send_near(glob_parts, GLOB_AXES[0])
    embed, embed_half, dq, dkv = encoder_back(
        scalars, middle_grad, hidden, normed_partial, normed_came, gains, wo0, wo0_other,
        q0, k0, v0, allowed,
    )
    enc_parts = encoder_quarters(byte_rows, dkv, query_rows, dq, mixed_rows, embed_half)
    block_out = block_out + block_came.astype(f32)
    up_came, down_came, glob_came, glob_parts, enc_parts, dq, dkv, block_out = stage(
        up_came, down_came, glob_came, glob_parts, enc_parts, dq, dkv, block_out
    )

    enc_came = send_quarters(enc_parts, ENC_AXES)
    glob_came.append(send_far(glob_parts, GLOB_AXES[0]))
    byte_own, query_own, byte_sent = byte_partial(dkv, dq, wk0, wv0, wq0)
    ffn_line = line_total(own_part, up_came, down_came)
    ffn_line, enc_came, enc_parts, glob_came, byte_sent = stage(
        ffn_line, enc_came, enc_parts, glob_came, byte_sent
    )

    glob_parts = split(scalars, [glob_parts[0], *glob_came], GLOB_AXES[1], ("yx", "yx"))
    enc_line = line_total(enc_parts[0], *enc_came)
    ffn_line, glob_parts, enc_line = stage(ffn_line, glob_parts, enc_line)
    ffn_sum = plane_sum(ffn_line, FFN_AXES)
    glob_came = send_quarters(glob_parts, GLOB_AXES[1])
    byte_grad = byte_gradient(
        own_bytes, byte_own, query_own, across(byte_sent), pooled[:patches], embed[:patches],
        member[0], size[:patches], gains,
    )
    glob_came, byte_grad = stage(glob_came, byte_grad)
    glob_parts = split(scalars, [glob_parts[0], *glob_came], GLOB_AXES[2], ("x", "y"))
    ffn_sum, enc_line, glob_parts = stage(ffn_sum, enc_line, glob_parts)
    glob_came = send_quarters(glob_parts, GLOB_AXES[2])

    enc_sum = plane_sum(enc_line, ENC_AXES)
    glob_sum = sum(p.astype(f32) for p in [glob_parts[0], *glob_came])

    gate_sum, up_sum, down_sum = jnp.split(ffn_sum, 3, axis=1)
    mine = jnp.where(section == 0, enc_sum, glob_sum)
    theirs = across(jnp.where(section == 0, glob_sum, enc_sum))
    first = jnp.where(section == 0, mine, theirs)
    last = jnp.where(section == 0, theirs, mine)
    sums = jnp.stack(
        [
            jnp.concatenate([x[:, k * half : (k + 1) * half] for x in (first, last)], axis=1)
            for k in range(4)
        ]
    )

    def against(weight, grad):
        return jnp.sum(weight.astype(f32) * grad, axis=-1)

    own_dots = against(proj_weights[0], sums[:3])
    ffn_dots = against(in_weights[0], gate_sum) + against(in_weights[1], up_sum)
    ffn_dots = ffn_dots + across(ffn_dots)
    gain_sum = jnp.where(
        section == 0,
        jnp.stack([own_dots[0], own_dots[1] + own_dots[2]]),
        jnp.stack([own_dots[0] + own_dots[1] + own_dots[2], ffn_dots]),
    )
    gain_sum = gain_sum / norm_gains[0].astype(f32)
    return (
        block_out[None, None],
        byte_grad[None, None],
        sums[None, :3],
        sums[3:],
        gain_sum[None],
        jnp.stack([gate_sum, up_sum]),
        down_sum,
    )


def solution(mesh):
    in_specs = (
        P("section", "fsdp", None, None),
        P(None, "fsdp", None),
        P(None, "fsdp", None),
        P("section", None, "fsdp", None),
        P("section", "fsdp", None),
        P("section", None, "fsdp"),
        P(None, "fsdp", "section"),
        P("fsdp", "section"),
        P("section", "fsdp", None, None),
    )
    out_specs = (
        P("section", "fsdp", None, None),
        P("section", "fsdp", None, None),
        P("section", None, "fsdp", None),
        P("section", "fsdp", None),
        P("section", None, "fsdp"),
        P(None, "fsdp", "section"),
        P("fsdp", "section"),
    )
    return jax.shard_map(shards, mesh=mesh, in_specs=in_specs, out_specs=out_specs, check_vma=False)
```

```python
import functools

import jax
import jax.numpy as jnp
from jax import lax
from jax.experimental import pallas as pl
from jax.experimental.pallas import tpu as pltpu
from jax.sharding import PartitionSpec as P

HEADS = 16
HEAD_DIM = 64
QUAD = 4
LANES = QUAD * HEAD_DIM
RING = 4
STRIDE = {"y": 16, "x": 4, "z": 1}

FFN_AXES = ("y", "x")
ENC_AXES = ("x", "y")
GLOB_AXES = (("z", "z"), ("y", "x"), ("x", "y"))

epsilon = 1e-05
masked_score = -1e30
bf16 = jnp.bfloat16
f32 = jnp.float32

SCALAR = pl.BlockSpec(memory_space=pltpu.SMEM)
WHOLE = pl.BlockSpec(memory_space=pltpu.VMEM)
IN_HBM = pl.BlockSpec(memory_space=pltpu.HBM)
OUT_HBM = pltpu.HBM
QUICK = pl.CostEstimate(flops=1, bytes_accessed=1, transcendentals=0)


def of(shape, kind):
    return jax.ShapeDtypeStruct(shape, kind)


ROOM = {
    "lay": 6,
    "prepare": 8,
    "encoder_forward": 12,
    "encoder_out": 8,
    "global_forward": 8,
    "feed_forward": 26,
    "ffn_quarters": 18,
    "global_back": 12,
    "global_quarters": 10,
    "near": 10,
    "split": 10,
    "line_total": 10,
    "encoder_back": 14,
    "encoder_quarters": 10,
    "byte_partial": 12,
    "byte_gradient": 8,
}


def kernel_call(body, name, **options):
    return pl.pallas_call(
        body,
        name=name,
        cost_estimate=QUICK,
        compiler_params=pltpu.CompilerParams(vmem_limit_bytes=ROOM[name] << 20),
        **options,
    )


def across(block):
    return lax.ppermute(block, "section", [(0, 1), (1, 0)])


def moved(i, ax, by):
    step = STRIDE[ax]
    c = (i // step) % RING
    return i + ((c + by) % RING - c) * step


def shift(block, ax, by):
    return lax.ppermute(block, "fsdp", [(i, moved(i, ax, by)) for i in range(64)])


def shift_by_core(block, axes, by):
    route = [(64 * s + i, 64 * s + moved(i, ax, by)) for s, ax in enumerate(axes) for i in range(64)]
    return lax.ppermute(block, ("section", "fsdp"), route)


def place(ax):
    return (lax.axis_index("fsdp") // STRIDE[ax]) % RING


def planes(axes):
    rows = {}
    for s, ax in enumerate(axes):
        for i in range(64):
            rows.setdefault((s, (i // STRIDE[ax]) % RING), []).append(64 * s + i)
    return list(rows.values())


def lines(axes):
    rows = {}
    for s, ax in enumerate(axes):
        for i in range(64):
            c = (i // STRIDE[ax]) % RING
            rows.setdefault((s, i - c * STRIDE[ax]), []).append(64 * s + i)
    return list(rows.values())


def put(whole, piece, at, dim):
    where = [0] * whole.ndim
    where[dim] = at
    return lax.dynamic_update_slice(whole, piece, where)


def gather_direct(block, ax, dim):
    c = place(ax)
    whole = jnp.zeros((*block.shape[:dim], RING, *block.shape[dim + 1 :]), block.dtype)
    arrived = [(shift(block, ax, by), (c - by) % RING) for by in (1, -1, 2)]
    for piece, at in [(block, c)] + arrived:
        whole = put(whole, piece, at, dim)
    return whole


def ring_pieces(block, ax):
    half = block.shape[-1] // 256 * 128
    last = block.ndim - 1
    below, above = shift(block, ax, 1), shift(block, ax, -1)
    first = shift(lax.slice_in_dim(below, 0, half, axis=last), ax, 1)
    second = shift(lax.slice_in_dim(above, half, None, axis=last), ax, -1)
    return block, above, below, first, second


def columns(pieces, k, begin, end):
    if k != 2:
        return pieces[(0, 1, None, 2)[k]][..., begin:end]
    first, second = pieces[3:]
    cut = first.shape[-1]
    if end <= cut:
        return first[..., begin:end]
    if begin >= cut:
        return second[..., begin - cut : end - cut]
    return jnp.concatenate([first[..., begin:], second[..., : end - cut]], axis=-1)


def lay_kernel(c_ref, *refs):
    ins, outs = refs[:10], refs[10:]
    for ax, pieces, targets in (("y", ins[:5], outs[:3]), ("x", ins[5:], outs[3:])):
        c = c_ref[0 if ax == "y" else 1]
        for k in range(RING):
            at = lax.rem(c + k, RING)
            column = 0
            for out in targets:
                value = columns(pieces, k, column, column + out.shape[-1])
                if ax == "y":
                    out[at] = value
                else:
                    out[:, at] = value
                column += out.shape[-1]


def lay(places, on_y, on_x, half):
    rows = on_y[0].shape[0]
    wide = (half, half, on_y[0].shape[1] - 2 * half)
    outs = [of((RING, rows, w), bf16) for w in wide]
    outs += [of((RING, RING, rows // RING, half), bf16)] * 2
    made = kernel_call(
        lay_kernel,
        "lay",
        in_specs=[SCALAR] + [WHOLE] * 10,
        out_specs=[WHOLE] * 5,
        out_shape=outs,
    )(places, *on_y, *on_x)
    return [m.reshape(RING * rows, m.shape[-1]) for m in made]


def send_near(parts, axes):
    return [shift_by_core(parts[1], axes, 1), shift_by_core(parts[3], axes, -1)]


def send_far(parts, axes):
    return shift_by_core(parts[2], axes, 2)


def send_quarters(parts, axes):
    return [*send_near(parts, axes), send_far(parts, axes)]


def total_kernel(*refs):
    total = refs[0][...].astype(f32)
    for part in refs[1:-1]:
        total = total + part[...].astype(f32)
    refs[-1][...] = total.astype(bf16)


def line_total(*parts):
    return kernel_call(
        total_kernel,
        "line_total",
        in_specs=[WHOLE] * len(parts),
        out_specs=WHOLE,
        out_shape=of(parts[0].shape, bf16),
    )(*parts)


def split_kernel(axes, names, s_ref, *refs):
    n = len(refs) - 2 * RING - 1
    targets, refs, sent = refs[n : n + RING], refs[:n] + refs[n + RING : -1], refs[-1]
    total = refs[0][...].astype(f32)
    for part in refs[1:n]:
        total = total + part[...].astype(f32)
    total = total.astype(bf16)
    outs = refs[n:]
    for s, ax in enumerate(axes):

        @pl.when(s_ref[0] == s)
        def _():
            c = s_ref[1 + "yxz".index(ax)]
            dim = names[s].index(ax)
            blocks = total.reshape(*[RING] * len(names[s]), -1, total.shape[1])
            for at in range(RING):
                block = lax.index_in_dim(blocks, at, dim, keepdims=False)
                k = lax.rem(at + RING - c, RING)
                for j in range(RING):

                    @pl.when(k == j)
                    def _():
                        outs[j][...] = block.reshape(outs[j].shape)

    outgoing = Outgoing(outs, targets, sent)
    for k in range(RING):
        outgoing.send(k)
    outgoing.finish()


def split(scalars, parts, axes, names):
    rows, wide = parts[0].shape
    return kernel_call(
        functools.partial(split_kernel, axes, names),
        "split",
        in_specs=[SCALAR] + [WHOLE] * len(parts),
        out_specs=[IN_HBM] * RING,
        out_shape=[OUT_HBM((rows // RING, wide), bf16)] * RING,
        scratch_shapes=[pltpu.VMEM((rows // RING, wide), bf16)] * RING
        + [pltpu.SemaphoreType.DMA((RING,))],
    )(scalars, *parts)


def near_kernel(up, down, a, b, up_out, down_out):
    cut = a.shape[1]
    up_out[:, :cut] = (up[:, :cut].astype(f32) + a[...].astype(f32)).astype(bf16)
    up_out[:, cut:] = up[:, cut:]
    down_out[:, cut:] = (down[:, cut:].astype(f32) + b[...].astype(f32)).astype(bf16)
    down_out[:, :cut] = down[:, :cut]


def near(up, down, a, b):
    return kernel_call(
        near_kernel,
        "near",
        in_specs=[WHOLE] * 4,
        out_specs=[WHOLE] * 2,
        out_shape=[of(up.shape, bf16)] * 2,
    )(up, down, a, b)


def line_sum(parts, axes):
    return lax.psum_scatter(
        parts,
        ("section", "fsdp"),
        scatter_dimension=0,
        axis_index_groups=lines(axes),
        tiled=False,
    )


def plane_sum(part, axes):
    blocks = part.reshape(16, part.shape[0] // 16, part.shape[1])
    blocks = lax.all_to_all(
        blocks, ("section", "fsdp"), 0, 0, axis_index_groups=planes(axes), tiled=True
    )
    return jnp.sum(blocks.astype(f32), axis=0)


def stage(*values):
    return lax.optimization_barrier(values)


def inverse_rms(values):
    return lax.rsqrt(jnp.mean(values * values, axis=-1, keepdims=True) + epsilon)


def normalize_back(values, inverse, scales, gradient):
    unit_rows = values * inverse
    scaled = gradient * scales
    inner_mean = jnp.mean(scaled * unit_rows, axis=-1, keepdims=True)
    return inverse * (scaled - unit_rows * inner_mean)


def matmul(left, right):
    return jnp.dot(left, right, preferred_element_type=f32)


def times_transposed(left, right):
    return lax.dot_general(left, right, (((1,), (1,)), ((), ())), preferred_element_type=f32)


def transposed_times(left, right):
    return lax.dot_general(left, right, (((0,), (0,)), ((), ())), preferred_element_type=f32)


def of_head(value, h):
    head = lax.broadcasted_iota(jnp.int32, value.shape, 1) // HEAD_DIM
    return jnp.where(head == h, value, jnp.zeros_like(value))


def stacked(value):
    return jnp.concatenate([of_head(value, h) for h in range(QUAD)], axis=0)


def unstacked(value, rows):
    total = of_head(value[:rows], 0)
    for h in range(1, QUAD):
        total = total + of_head(value[h * rows : (h + 1) * rows], h)
    return total


def probabilities(q4, keys, table):
    raw = times_transposed(q4, keys)
    allowed = jnp.concatenate([table] * QUAD, axis=0) > 0
    scores = jnp.where(allowed, raw * HEAD_DIM ** (-0.5), masked_score)
    weights = jnp.exp(scores - jnp.max(scores, axis=-1, keepdims=True))
    return weights / jnp.sum(weights, axis=-1, keepdims=True)


def attend(q, k, v, table):
    p = probabilities(stacked(q), k, table).astype(bf16)
    return unstacked(matmul(p, v), q.shape[0]).astype(bf16)


def attend_back(q, k, v, table, d):
    rows = q.shape[0]
    q4, d4 = stacked(q), stacked(d)
    p = probabilities(q4, k, table)
    dp = times_transposed(d4, v)
    ds = p * (dp - jnp.sum(p * dp, axis=-1, keepdims=True)) * HEAD_DIM ** (-0.5)
    ds = ds.astype(bf16)
    dq = unstacked(matmul(ds, k), rows).astype(bf16)
    dk = transposed_times(ds, q4).astype(bf16)
    dv = transposed_times(p.astype(bf16), d4).astype(bf16)
    return dq, dk, dv


def lanes_of(section, half):
    mine = pl.ds(pl.multiple_of(section * half, half), half)
    theirs = pl.ds(pl.multiple_of((1 - section) * half, half), half)
    return mine, theirs


def merge(scratch, section, own, other):
    mine, theirs = lanes_of(section, own.shape[1])
    scratch[:, mine] = own
    scratch[:, theirs] = other


def swap_rows(x):
    half = x.shape[0] // 2
    return jnp.concatenate([x[half:], x[:half]], axis=0)


def quarter(turned, ax, at):
    if ax == "y":
        rows = turned[at]
    elif ax == "x":
        rows = turned[:, at]
    else:
        rows = turned[:, :, at]
    return rows.reshape(turned.shape[0] ** 2 * turned.shape[3], turned.shape[4])


def fill_quarters(x_ref, turned, rows, s_ref, axes, first):
    turned[...] = x_ref[...].T.reshape(turned.shape)
    for s, ax in enumerate(axes):

        @pl.when(s_ref[0] == s)
        def _():
            c = s_ref[1 + "yxz".index(ax)] if first else 0
            for k in range(RING):
                rows[k] = quarter(turned, ax, lax.rem(c + k, RING))


def turned_scratch(tokens, features):
    return pltpu.VMEM((RING, RING, RING, features // RING**3, tokens), bf16)


def quarter_scratch(tokens, features):
    return [
        turned_scratch(tokens, features),
        pltpu.VMEM((RING, features // RING, tokens), bf16),
    ]


def rows_of(x):
    return of((RING, x.shape[1] // RING, x.shape[0]), bf16)


def prepare_kernel(enc_axes, ffn_axes, s_ref, b_ref, x_ref, t_ref, b_rows, x_rows, t_rows, *turned):
    fill_quarters(b_ref, turned[0], b_rows, s_ref, enc_axes, True)
    fill_quarters(x_ref, turned[1], x_rows, s_ref, enc_axes, True)
    fill_quarters(t_ref, turned[2], t_rows, s_ref, ffn_axes, True)


def prepare(scalars, b, x, t, enc_axes, ffn_axes):
    return kernel_call(
        functools.partial(prepare_kernel, enc_axes, ffn_axes),
        "prepare",
        in_specs=[SCALAR] + [WHOLE] * 3,
        out_specs=[WHOLE] * 3,
        out_shape=[rows_of(a) for a in (b, x, t)],
        scratch_shapes=[turned_scratch(*a.shape) for a in (b, x, t)],
    )(scalars, b, x, t)


def encoder_kernel(x_ref, b_ref, wq, wk, wv, table, q_ref, k_ref, v_ref, mixed, mixed_swapped):
    q = matmul(x_ref[...], wq[...]).astype(bf16)
    k = matmul(b_ref[...], wk[...]).astype(bf16)
    v = matmul(b_ref[...], wv[...]).astype(bf16)
    q_ref[...], k_ref[...], v_ref[...] = q, k, v
    out = attend(q, k, v, table[0])
    mixed[...] = out
    mixed_swapped[...] = out


def encoder_forward(query_low, byte_low, wq, wk, wv, table):
    micro, rows, keys = table.shape
    width, half = wq.shape
    weight = pl.BlockSpec((width, LANES), lambda h, m: (0, h))
    per_row = pl.BlockSpec((rows, LANES), lambda h, m: (m, h))
    per_key = pl.BlockSpec((keys, LANES), lambda h, m: (m, h))
    return kernel_call(
        encoder_kernel,
        "encoder_forward",
        grid=(half // LANES, micro),
        in_specs=[
            pl.BlockSpec((rows, width), lambda h, m: (m, 0)),
            pl.BlockSpec((keys, width), lambda h, m: (m, 0)),
            weight,
            weight,
            weight,
            pl.BlockSpec((1, rows, keys), lambda h, m: (m, 0, 0)),
        ],
        out_specs=[
            per_row,
            per_key,
            per_key,
            per_row,
            pl.BlockSpec((rows, LANES), lambda h, m: (1 - m, h)),
        ],
        out_shape=[
            of((micro * rows, half), bf16),
            of((micro * keys, half), bf16),
            of((micro * keys, half), bf16),
            of((micro * rows, half), bf16),
            of((micro * rows, half), bf16),
        ],
    )(query_low, byte_low, wq, wk, wv, table)


def encoder_out_kernel(
    enc_axes, glob_axes, s_ref, pooled, own, other, wo, wo_other, gains,
    hidden_ref, low_ref, mixed_rows, low_rows, whole_ref, sum_ref, turned_mixed, turned_low,
):
    section = s_ref[0]
    merge(whole_ref, section, own[...], other[...])
    whole = whole_ref[...]
    merge(sum_ref, section, matmul(whole, wo[...]), matmul(whole, wo_other[...]))
    low_hidden = (pooled[...] + sum_ref[...]).astype(bf16)
    hidden_ref[...] = low_hidden
    hidden = low_hidden.astype(f32)
    low = (hidden * inverse_rms(hidden) * gains[2:3]).astype(bf16)
    low_ref[...] = low
    fill_quarters(whole, turned_mixed, mixed_rows, s_ref, enc_axes, True)
    fill_quarters(low, turned_low, low_rows, s_ref, glob_axes, True)


def encoder_out(scalars, pooled, own, other, wo, wo_other, gains, enc_axes, glob_axes):
    tokens, width = pooled.shape
    rows = of((RING, width // RING, tokens), bf16)
    return kernel_call(
        functools.partial(encoder_out_kernel, enc_axes, glob_axes),
        "encoder_out",
        in_specs=[SCALAR] + [WHOLE] * 6,
        out_specs=[WHOLE] * 4,
        out_shape=[of((tokens, width), bf16), of((tokens, width), bf16), rows, rows],
        scratch_shapes=[pltpu.VMEM((tokens, width), bf16), pltpu.VMEM((tokens, width), f32)]
        + [turned_scratch(tokens, width)] * 2,
    )(scalars, pooled, own, other, wo, wo_other, gains)


def global_kernel(x_ref, packed, table, q_ref, k_ref, v_ref, mixed, mixed_swapped, weights, sems):
    h, m = pl.program_id(0), pl.program_id(1)
    count = pl.num_programs(0)

    def copy(j, at):
        source = packed.at[:, pl.ds(pl.multiple_of((j * count + at) * LANES, LANES), LANES)]
        return pltpu.make_async_copy(source, weights.at[at, j], sems.at[at, j])

    @pl.when((h == 0) & (m == 0))
    def _():
        for at in range(weights.shape[0]):
            for j in range(3):
                copy(j, at).start()

    @pl.when(m == 0)
    def _():
        for j in range(3):
            copy(j, h).wait()

    x = x_ref[...]
    q, k, v = (matmul(x, weights[h, j]).astype(bf16) for j in range(3))
    q_ref[...], k_ref[...], v_ref[...] = q, k, v
    out = attend(q, k, v, table[0])
    mixed[...] = out
    mixed_swapped[...] = out


def global_forward(x, packed, table, half):
    micro, rows, _ = table.shape
    width = x.shape[1]
    count = half // LANES
    per_row = pl.BlockSpec((rows, LANES), lambda h, m: (m, h))
    return kernel_call(
        global_kernel,
        "global_forward",
        grid=(count, micro),
        in_specs=[
            pl.BlockSpec((rows, width), lambda h, m: (m, 0)),
            IN_HBM,
            pl.BlockSpec((1, rows, rows), lambda h, m: (m, 0, 0)),
        ],
        out_specs=[per_row] * 4 + [pl.BlockSpec((rows, LANES), lambda h, m: (1 - m, h))],
        out_shape=[of((micro * rows, half), bf16)] * 5,
        scratch_shapes=[
            pltpu.VMEM((count, 3, width, LANES), bf16),
            pltpu.SemaphoreType.DMA((count, 3)),
        ],
    )(x, packed, table)


class Outgoing:
    def __init__(self, buffers, targets, sems):
        self.copies = [
            pltpu.make_async_copy(b, t, sems.at[k]) for k, (b, t) in enumerate(zip(buffers, targets))
        ]

    def send(self, k):
        self.copies[k].start()

    def finish(self):
        for copy in self.copies:
            copy.wait()


def ffn_kernel(
    units, at, axes, s_ref, hidden, own, other, wo, wo_other, gains, target, rows_target, packed,
    mixed_whole, middle_ref, partial, partial_sent, far_a, far_b, gate_out, up_out, inner_out, rows,
    w_gate, w_up, w_down, turned, sems,
):
    copies = [
        pltpu.make_async_copy(packed.at[:, pl.ds(at + k * units, units)], w, sems.at[k])
        for k, w in enumerate((w_gate, w_up, w_down))
    ]
    for copy in copies:
        copy.start()
    section = s_ref[0]
    merge(mixed_whole, section, own[...], other[...])
    whole = mixed_whole[...]
    merge(middle_ref, section, matmul(whole, wo[...]), matmul(whole, wo_other[...]))
    middle = hidden[...].astype(f32) + middle_ref[...]
    middle_ref[...] = middle
    low = (middle * inverse_rms(middle) * gains[3:4]).astype(bf16)
    copies[0].wait()
    gate = matmul(low, w_gate[...])
    copies[1].wait()
    up = matmul(low, w_up[...])
    sigma = jax.nn.sigmoid(gate)
    inner = (gate * sigma * up).astype(bf16)
    copies[2].wait()
    inner_grad = matmul(target[...], w_down[...])
    up_grad = (inner_grad * gate * sigma).astype(bf16)
    gate_grad = (inner_grad * up * sigma * (1.0 + gate * (1.0 - sigma))).astype(bf16)
    gate_out[...], up_out[...], inner_out[...] = gate_grad, up_grad, inner
    total = times_transposed(gate_grad, w_gate[...]) + times_transposed(up_grad, w_up[...])
    partial[...] = total
    partial_sent[...] = swap_rows(total.astype(bf16))
    fill_quarters(low, turned, rows, s_ref, axes, True)
    cut = far_a.shape[1]
    for j, (x, d) in enumerate(((rows, gate_grad), (rows, up_grad), (rows_target, inner))):
        value = matmul(x[2], d).astype(bf16)
        begin, end = j * units, (j + 1) * units
        if end <= cut:
            far_a[:, begin:end] = value
        elif begin >= cut:
            far_b[:, begin - cut : end - cut] = value
        else:
            far_a[:, begin:] = value[:, : cut - begin]
            far_b[:, : end - cut] = value[:, cut - begin :]


def feed_forward(
    scalars, hidden, own, other, wo, wo_other, gains, target, rows, packed, units, at, axes
):
    tokens, width = hidden.shape
    block = width // RING
    cut = 3 * units // 256 * 128
    return kernel_call(
        functools.partial(ffn_kernel, units, at, axes),
        "feed_forward",
        in_specs=[SCALAR] + [WHOLE] * 8 + [IN_HBM],
        out_specs=[WHOLE] * 10,
        out_shape=[
            of((tokens, width), bf16),
            of((tokens, width), f32),
            of((tokens, width), f32),
            of((tokens, width), bf16),
            of((block, cut), bf16),
            of((block, 3 * units - cut), bf16),
        ]
        + [of((tokens, units), bf16)] * 3
        + [of((RING, block, tokens), bf16)],
        scratch_shapes=[pltpu.VMEM((width, units), bf16)] * 3
        + [turned_scratch(tokens, width), pltpu.SemaphoreType.DMA((3,))],
    )(scalars, hidden, own, other, wo, wo_other, gains, target, rows, packed)


def ffn_quarters_kernel(
    at, rows, rows_target, gate_grad, up_grad, inner, middle, packed,
    result, result_sent, up_part, down_part, own_part, up_made, down_made, own_made, w_down, sent, sem,
):
    units = inner.shape[1]
    copy = pltpu.make_async_copy(packed.at[:, pl.ds(at + 2 * units, units)], w_down, sem)
    copy.start()
    outgoing = Outgoing((up_made, down_made, own_made), (up_part, down_part, own_part), sent)
    for n, (k, part) in enumerate(((1, up_made), (3, down_made), (0, own_made))):
        for j, (x, d) in enumerate(((rows, gate_grad), (rows, up_grad), (rows_target, inner))):
            part[:, j * units : (j + 1) * units] = matmul(x[k], d[...]).astype(bf16)
        outgoing.send(n)
    copy.wait()
    half = result.shape[0]
    out = times_transposed(inner[...], w_down[...])
    result[...] = middle[:half] + out[:half]
    result_sent[...] = out[half:].astype(bf16)
    outgoing.finish()


def ffn_quarters(rows, rows_target, gate_grad, up_grad, inner, middle, packed, at):
    tokens, width = middle.shape
    units = inner.shape[1]
    shape = (width // RING, 3 * units)
    return kernel_call(
        functools.partial(ffn_quarters_kernel, at),
        "ffn_quarters",
        in_specs=[WHOLE] * 6 + [IN_HBM],
        out_specs=[WHOLE] * 2 + [IN_HBM] * 3,
        out_shape=[of((tokens // 2, width), f32), of((tokens // 2, width), bf16)]
        + [OUT_HBM(shape, bf16)] * 3,
        scratch_shapes=[pltpu.VMEM(shape, bf16)] * 3
        + [pltpu.VMEM((width, units), bf16)]
        + [pltpu.SemaphoreType.DMA((3,)), pltpu.SemaphoreType.DMA],
    )(rows, rows_target, gate_grad, up_grad, inner, middle, packed)


def global_back_kernel(
    s_ref, target, middle, partial, came, gains, wo, wo_other, q_ref, k_ref, v_ref, table, packed,
    middle_grad, middle_half, dqkv, out, out_sent, mixed_grad, low, w_qkv, sem,
):
    rows, half = table.shape[1], wo.shape[1]
    m, h = pl.program_id(0), pl.program_id(1)
    copy = pltpu.make_async_copy(packed.at[:, pl.ds(0, 3 * half)], w_qkv, sem)

    @pl.when((m == 0) & (h == 0))
    def _():
        copy.start()
        section = s_ref[0]
        v = middle[...]
        grad = partial[...] + came[...].astype(f32)
        grad = target[...].astype(f32) + normalize_back(v, inverse_rms(v), gains[3:4], grad)
        middle_grad[...] = grad
        low[...] = grad.astype(bf16)
        mine, theirs = lanes_of(section, half)
        middle_half[...] = low[:, mine]
        own_rows = pl.ds(pl.multiple_of(section * half, half), half)
        mixed_grad[...] = (
            times_transposed(low[:, mine], wo[own_rows])
            + times_transposed(low[:, theirs], wo_other[own_rows])
        ).astype(bf16)

    here = pl.ds(pl.multiple_of(m * rows, rows), rows)
    at = pl.multiple_of(h * LANES, LANES)
    quad = pl.ds(at, LANES)
    dq, dk, dv = attend_back(
        q_ref[here, quad], k_ref[here, quad], v_ref[here, quad], table[0], mixed_grad[here, quad]
    )
    dqkv[here, quad] = dq
    dqkv[here, pl.ds(at + half, LANES)] = dk
    dqkv[here, pl.ds(at + 2 * half, LANES)] = dv

    @pl.when((m == pl.num_programs(0) - 1) & (h == pl.num_programs(1) - 1))
    def _():
        copy.wait()
        total = times_transposed(dqkv[...], w_qkv[...])
        out[...] = total
        out_sent[...] = swap_rows(total.astype(bf16))


def global_back(section, target, middle, partial, came, gains, wo, wo_other, q, k, v, table, packed):
    micro, rows, _ = table.shape
    tokens, width = middle.shape
    half = wo.shape[1]

    def fixed(shape):
        return pl.BlockSpec(shape, lambda m, h: (0, 0))

    return kernel_call(
        global_back_kernel,
        "global_back",
        grid=(micro, half // LANES),
        in_specs=[SCALAR]
        + [fixed((tokens, width))] * 4
        + [fixed(gains.shape)]
        + [fixed((width, half))] * 2
        + [fixed((tokens, half))] * 3
        + [pl.BlockSpec((1, rows, rows), lambda m, h: (m, 0, 0)), IN_HBM],
        out_specs=[
            fixed((tokens, width)),
            fixed((tokens, half)),
            fixed((tokens, 3 * half)),
            fixed((tokens, width)),
            fixed((tokens, width)),
        ],
        out_shape=[
            of((tokens, width), f32),
            of((tokens, half), bf16),
            of((tokens, 3 * half), bf16),
            of((tokens, width), f32),
            of((tokens, width), bf16),
        ],
        scratch_shapes=[
            pltpu.VMEM((tokens, half), bf16),
            pltpu.VMEM((tokens, width), bf16),
            pltpu.VMEM((width, 3 * half), bf16),
            pltpu.SemaphoreType.DMA,
        ],
    )(section, target, middle, partial, came, gains, wo, wo_other, q, k, v, table, packed)


def global_quarters_kernel(axes, s_ref, x_rows, d_ref, y_ref, e_ref, *refs):
    outs, made, (turned, y_rows, sent) = refs[:4], refs[4:8], refs[8:]
    outgoing = Outgoing(made, outs, sent)
    fill_quarters(y_ref, turned, y_rows, s_ref, axes, True)
    for k in (1, 3, 2, 0):
        made[k][:, : d_ref.shape[1]] = matmul(x_rows[k], d_ref[...]).astype(bf16)
        made[k][:, d_ref.shape[1] :] = matmul(y_rows[k], e_ref[...]).astype(bf16)
        outgoing.send(k)
    outgoing.finish()


def global_quarters(scalars, x_rows, d, y, e, axes):
    tokens, width = y.shape
    shape = (width // RING, d.shape[1] + e.shape[1])
    return kernel_call(
        functools.partial(global_quarters_kernel, axes),
        "global_quarters",
        in_specs=[SCALAR] + [WHOLE] * 4,
        out_specs=[IN_HBM] * 4,
        out_shape=[OUT_HBM(shape, bf16)] * 4,
        scratch_shapes=[pltpu.VMEM(shape, bf16)] * 4
        + quarter_scratch(tokens, width)
        + [pltpu.SemaphoreType.DMA((4,))],
    )(scalars, x_rows, d, y, e)


def encoder_back_kernel(
    s_ref, middle_grad, hidden, partial, came, gains, wo, wo_other, q_ref, k_ref, v_ref, table,
    embed, embed_half, dq_ref, dkv_ref, mixed_grad,
):
    rows, keys = table.shape[1:]
    half = wo.shape[1]
    m, h = pl.program_id(0), pl.program_id(1)

    @pl.when((m == 0) & (h == 0))
    def _():
        section = s_ref[0]
        v = hidden[...].astype(f32)
        grad = partial[...] + came[...].astype(f32)
        grad = middle_grad[...] + normalize_back(v, inverse_rms(v), gains[2:3], grad)
        embed[...] = grad.astype(bf16)
        mine, theirs = lanes_of(section, half)
        embed_half[...] = embed[:, mine]
        own_rows = pl.ds(pl.multiple_of(section * half, half), half)
        mixed_grad[...] = (
            times_transposed(embed[:, mine], wo[own_rows])
            + times_transposed(embed[:, theirs], wo_other[own_rows])
        ).astype(bf16)

    here = pl.ds(pl.multiple_of(m * rows, rows), rows)
    at = pl.multiple_of(h * LANES, LANES)
    dq, dk, dv = attend_back(
        q_ref[...], k_ref[...], v_ref[...], table[0], mixed_grad[here, pl.ds(at, LANES)]
    )
    dq_ref[...] = dq
    there = pl.ds(pl.multiple_of(m * keys, keys), keys)
    dkv_ref[there, pl.ds(at, LANES)] = dk
    dkv_ref[there, pl.ds(at + half, LANES)] = dv


def encoder_back(section, middle_grad, hidden, partial, came, gains, wo, wo_other, q, k, v, table):
    micro, rows, keys = table.shape
    tokens, width = hidden.shape
    half = wo.shape[1]

    def fixed(shape):
        return pl.BlockSpec(shape, lambda m, h: (0, 0))

    per_row = pl.BlockSpec((rows, LANES), lambda m, h: (m, h))
    per_key = pl.BlockSpec((keys, LANES), lambda m, h: (m, h))
    return kernel_call(
        encoder_back_kernel,
        "encoder_back",
        grid=(micro, half // LANES),
        in_specs=[SCALAR]
        + [fixed((tokens, width))] * 4
        + [fixed(gains.shape)]
        + [fixed((width, half))] * 2
        + [per_row, per_key, per_key, pl.BlockSpec((1, rows, keys), lambda m, h: (m, 0, 0))],
        out_specs=[
            fixed((tokens, width)),
            fixed((tokens, half)),
            per_row,
            fixed((micro * keys, 2 * half)),
        ],
        out_shape=[
            of((tokens, width), bf16),
            of((tokens, half), bf16),
            of((tokens, half), bf16),
            of((micro * keys, 2 * half), bf16),
        ],
        scratch_shapes=[pltpu.VMEM((tokens, half), bf16)],
    )(section, middle_grad, hidden, partial, came, gains, wo, wo_other, q, k, v, table)


def encoder_quarters_kernel(b_rows, dkv, x_rows, dq, y_rows, e_ref, *refs):
    outs, made, sent = refs[:4], refs[4:8], refs[8]
    half = dq.shape[1]
    outgoing = Outgoing(made, outs, sent)
    for k in (1, 3, 2, 0):
        for rows, d, at in ((x_rows, dq, 0), (b_rows, dkv, half), (y_rows, e_ref, 3 * half)):
            made[k][:, at : at + d.shape[1]] = matmul(rows[k], d[...]).astype(bf16)
        outgoing.send(k)
    outgoing.finish()


def encoder_quarters(b_rows, dkv, x_rows, dq, y_rows, e):
    shape = (x_rows.shape[1], 4 * dq.shape[1])
    return kernel_call(
        encoder_quarters_kernel,
        "encoder_quarters",
        in_specs=[WHOLE] * 6,
        out_specs=[IN_HBM] * 4,
        out_shape=[OUT_HBM(shape, bf16)] * 4,
        scratch_shapes=[pltpu.VMEM(shape, bf16)] * 4 + [pltpu.SemaphoreType.DMA((4,))],
    )(b_rows, dkv, x_rows, dq, y_rows, e)


def byte_partial_kernel(dkv, dq, wk, wv, wq, own, query_own, sent):
    half = wk.shape[1]
    count, rows = own.shape[0], query_own.shape[0]
    for at, out in ((0, own), (count, sent.at[:count])):
        total = times_transposed(dkv[at : at + count, :half], wk[...])
        total = total + times_transposed(dkv[at : at + count, half:], wv[...])
        out[...] = total.astype(out.dtype)
    total = times_transposed(dq[...], wq[...])
    query_own[...] = total[:rows]
    sent[count:] = total[rows:].astype(bf16)


def byte_partial(dkv, dq, wk, wv, wq):
    width = wk.shape[0]
    count, rows = dkv.shape[0] // 2, dq.shape[0] // 2
    return kernel_call(
        byte_partial_kernel,
        "byte_partial",
        in_specs=[WHOLE] * 5,
        out_specs=[WHOLE] * 3,
        out_shape=[
            of((count, width), f32),
            of((rows, width), f32),
            of((count + rows, width), bf16),
        ],
    )(dkv, dq, wk, wv, wq)


def byte_grad_kernel(raw, own, query_own, came, pooled, embed, member, size, gains, out):
    count = raw.shape[0]
    pool = pooled[...]
    grad = query_own[...] + came[count:].astype(f32)
    share = embed[...].astype(f32) + normalize_back(pool, inverse_rms(pool), gains[0:1], grad)
    share = share / size[...]
    high = share.astype(bf16)
    rest = (share - high.astype(f32)).astype(bf16)
    spread = transposed_times(member[...], high) + transposed_times(member[...], rest)
    v = raw[...].astype(f32)
    grad = own[...] + came[:count].astype(f32)
    out[...] = spread + normalize_back(v, inverse_rms(v), gains[1:2], grad)


def byte_gradient(*args):
    return kernel_call(
        byte_grad_kernel,
        "byte_gradient",
        in_specs=[WHOLE] * 9,
        out_specs=WHOLE,
        out_shape=of(args[0].shape, f32),
    )(*args)


def patch_tables(lengths, documents):
    patches, count = lengths.shape[1], documents.shape[1]
    ends = jnp.cumsum(lengths, axis=1, dtype=jnp.int32)
    starts = ends - lengths
    position = lax.broadcasted_iota(jnp.int32, (1, patches, count), 2)
    member = (position >= starts[:, :, None]) & (position < ends[:, :, None])
    first_doc = jnp.sum(
        jnp.where(position == starts[:, :, None], documents[:, None, :], 0), axis=2
    )
    allowed = member & (documents[:, None, :] == first_doc[:, :, None])
    order_rows = lax.broadcasted_iota(jnp.int32, (1, patches, patches), 1)
    order_cols = lax.broadcasted_iota(jnp.int32, (1, patches, patches), 2)
    causal = (order_cols <= order_rows) & (first_doc[:, None, :] == first_doc[:, :, None])
    return member.astype(bf16), allowed.astype(f32), causal.astype(f32)


def own_first(pair, section):
    return jnp.where(section == 0, pair, pair[::-1])


def shards(
    byte_states,
    patch_lengths,
    doc_ids,
    proj_weights,
    out_weights,
    norm_gains,
    in_weights,
    down_weights,
    cotangent,
):
    section = lax.axis_index("section")
    scalars = jnp.stack([section, place("y"), place("x"), place("z")]).astype(jnp.int32)
    scalars, section = stage(scalars, section)
    width = byte_states.shape[-1]
    half = width // 2
    units = down_weights.shape[1]

    own_w = jnp.concatenate([proj_weights[0], out_weights], axis=0)
    own_w = own_w.transpose(1, 0, 2).reshape(16, 4, 2, half)
    gains_own = jnp.pad(norm_gains[0].T, ((0, 0), (0, 126)))
    keep = jnp.where(section == 0, own_w[:, :, 0], own_w[:, :, 1]).reshape(16, 4 * half)
    give = jnp.where(section == 0, own_w[:, :, 1], own_w[:, :, 0]).reshape(16, 4 * half)
    got = across(jnp.concatenate([give, gains_own], axis=1))
    enc = jnp.where(section == 0, keep, got[:, : 4 * half])
    glob = jnp.where(section == 0, got[:, : 4 * half], keep)
    gains_first = jnp.where(section == 0, gains_own, got[:, 4 * half :])
    gains_last = jnp.where(section == 0, got[:, 4 * half :], gains_own)
    gains = jnp.concatenate([gains_first[:, :2], gains_last[:, :126]], axis=1)
    packed = jnp.concatenate(
        [glob, in_weights[0], in_weights[1], down_weights], axis=1
    )
    packed = lax.all_gather(packed, "fsdp", axis=0, tiled=True)

    pack = jnp.concatenate(
        [enc[:, half : 3 * half], gains, enc[:, :half], enc[:, 3 * half :]], axis=1
    )
    first = 2 * half + 128
    pack = gather_direct(pack[None], "z", 0).reshape(64, -1)
    on_y = gather_direct(pack[None, :, :first], "x", 0).reshape(256, -1)
    on_x = gather_direct(pack[None, :, first:], "y", 0)
    places = jnp.stack([place("y"), place("x")])
    wk0, wv0, gains, wq0, wo0 = lay(places, ring_pieces(on_y, "y"), ring_pieces(on_x, "x"), half)
    pick = (
        lax.broadcasted_iota(jnp.int32, (8, 128), 0) == lax.broadcasted_iota(jnp.int32, (8, 128), 1)
    ).astype(bf16)
    gains = times_transposed(pick, gains)
    wo0_other = across(wo0)

    own_bytes, own_target = byte_states[0, 0], cotangent[0, 0]
    raw = jnp.concatenate([own_bytes, across(own_bytes)], axis=0)
    target = jnp.concatenate([own_target, across(own_target)], axis=0)
    lengths = own_first(patch_lengths[:, 0], section)
    documents = own_first(doc_ids[:, 0], section)
    patches, count = lengths.shape[1], documents.shape[1]
    member, allowed, causal = patch_tables(lengths, documents)
    size = lengths.astype(f32).reshape(-1, 1)

    raw_f32 = raw.astype(f32)
    pooled = lax.dot_general(
        member,
        raw.reshape(2, count, width),
        (((2,), (1,)), ((0,), (0,))),
        preferred_element_type=f32,
    ).reshape(2 * patches, width)
    pooled = pooled / size
    query_low = (pooled * inverse_rms(pooled) * gains[0]).astype(bf16)
    byte_low = (raw_f32 * inverse_rms(raw_f32) * gains[1]).astype(bf16)
    q0, k0, v0, mixed, mixed_sent = encoder_forward(query_low, byte_low, wq0, wk0, wv0, allowed)
    byte_rows, query_rows, target_rows = prepare(
        scalars, byte_low, query_low, target, ENC_AXES, FFN_AXES
    )
    hidden, normed_low, mixed_rows, normed_rows = encoder_out(
        scalars, pooled, mixed, across(mixed_sent), wo0, wo0_other, gains, ENC_AXES, GLOB_AXES[0]
    )
    (
        packed, hidden, normed_low, mixed_rows, normed_rows, byte_rows, query_rows, target_rows, causal,
    ) = stage(
        packed, hidden, normed_low, mixed_rows, normed_rows, byte_rows, query_rows, target_rows, causal,
    )
    wo1 = packed[:, 3 * half : 4 * half]
    wo1_other = across(wo1)
    packed = pltpu.with_memory_space_constraint(packed, pltpu.HBM)
    q1, k1, v1, mixed, mixed_sent = global_forward(normed_low, packed, causal, half)
    (
        mixed1, middle, ffn_partial, ffn_sent, far_a, far_b, gate_grad, up_grad, inner, low_rows,
    ) = feed_forward(
        scalars, hidden, mixed, across(mixed_sent), wo1, wo1_other, gains, target, target_rows,
        packed, units, 4 * half, FFN_AXES,
    )
    ffn_came, far_a, far_b, inner = stage(across(ffn_sent), far_a, far_b, inner)

    far_a, far_b = shift_by_core(far_a, FFN_AXES, 1), shift_by_core(far_b, FFN_AXES, -1)
    middle_grad, middle_half, dqkv, normed_partial, normed_sent = global_back(
        scalars, target, middle, ffn_partial, ffn_came, gains, wo1, wo1_other,
        q1, k1, v1, causal, packed,
    )
    block_out, block_sent, up_part, down_part, own_part = ffn_quarters(
        low_rows, target_rows, gate_grad, up_grad, inner, middle, packed, 4 * half
    )
    glob_parts = global_quarters(
        scalars, normed_rows, dqkv, mixed1, middle_half, GLOB_AXES[0]
    )
    far_a, far_b, normed_sent, glob_parts, up_part, down_part, own_part, block_sent = stage(
        far_a, far_b, normed_sent, glob_parts, up_part, down_part, own_part, block_sent
    )
    block_came = across(block_sent)

    up_part, down_part = near(up_part, down_part, far_a, far_b)
    normed_came, up_part, down_part = stage(across(normed_sent), up_part, down_part)
    up_came, down_came = (
        shift_by_core(up_part, FFN_AXES, 1),
        shift_by_core(down_part, FFN_AXES, -1),
    )
    glob_came = send_near(glob_parts, GLOB_AXES[0])
    embed, embed_half, dq, dkv = encoder_back(
        scalars, middle_grad, hidden, normed_partial, normed_came, gains, wo0, wo0_other,
        q0, k0, v0, allowed,
    )
    enc_parts = encoder_quarters(byte_rows, dkv, query_rows, dq, mixed_rows, embed_half)
    block_out = block_out + block_came.astype(f32)
    up_came, down_came, glob_came, glob_parts, enc_parts, dq, dkv, block_out = stage(
        up_came, down_came, glob_came, glob_parts, enc_parts, dq, dkv, block_out
    )

    enc_came = send_quarters(enc_parts, ENC_AXES)
    glob_came.append(send_far(glob_parts, GLOB_AXES[0]))
    byte_own, query_own, byte_sent = byte_partial(dkv, dq, wk0, wv0, wq0)
    ffn_line = line_total(own_part, up_came, down_came)
    ffn_line, enc_came, enc_parts, glob_came, byte_sent = stage(
        ffn_line, enc_came, enc_parts, glob_came, byte_sent
    )

    glob_parts = split(scalars, [glob_parts[0], *glob_came], GLOB_AXES[1], ("yx", "yx"))
    enc_line = line_total(enc_parts[0], *enc_came)
    ffn_line, glob_parts, enc_line = stage(ffn_line, glob_parts, enc_line)
    ffn_sum = plane_sum(ffn_line, FFN_AXES)
    glob_came = send_quarters(glob_parts, GLOB_AXES[1])
    byte_grad = byte_gradient(
        own_bytes, byte_own, query_own, across(byte_sent), pooled[:patches], embed[:patches],
        member[0], size[:patches], gains,
    )
    glob_came, byte_grad = stage(glob_came, byte_grad)
    glob_parts = split(scalars, [glob_parts[0], *glob_came], GLOB_AXES[2], ("x", "y"))
    ffn_sum, enc_line, glob_parts = stage(ffn_sum, enc_line, glob_parts)
    glob_came = send_quarters(glob_parts, GLOB_AXES[2])

    enc_sum = plane_sum(enc_line, ENC_AXES)
    glob_sum = sum(p.astype(f32) for p in [glob_parts[0], *glob_came])

    gate_sum, up_sum, down_sum = jnp.split(ffn_sum, 3, axis=1)
    mine = jnp.where(section == 0, enc_sum, glob_sum)
    theirs = across(jnp.where(section == 0, glob_sum, enc_sum))
    first = jnp.where(section == 0, mine, theirs)
    last = jnp.where(section == 0, theirs, mine)
    sums = jnp.stack(
        [
            jnp.concatenate([x[:, k * half : (k + 1) * half] for x in (first, last)], axis=1)
            for k in range(4)
        ]
    )

    def against(weight, grad):
        return jnp.sum(weight.astype(f32) * grad, axis=-1)

    own_dots = against(proj_weights[0], sums[:3])
    ffn_dots = against(in_weights[0], gate_sum) + against(in_weights[1], up_sum)
    ffn_dots = ffn_dots + across(ffn_dots)
    gain_sum = jnp.where(
        section == 0,
        jnp.stack([own_dots[0], own_dots[1] + own_dots[2]]),
        jnp.stack([own_dots[0] + own_dots[1] + own_dots[2], ffn_dots]),
    )
    gain_sum = gain_sum / norm_gains[0].astype(f32)
    return (
        block_out[None, None],
        byte_grad[None, None],
        sums[None, :3],
        sums[3:],
        gain_sum[None],
        jnp.stack([gate_sum, up_sum]),
        down_sum,
    )


def solution(mesh):
    in_specs = (
        P("section", "fsdp", None, None),
        P(None, "fsdp", None),
        P(None, "fsdp", None),
        P("section", None, "fsdp", None),
        P("section", "fsdp", None),
        P("section", None, "fsdp"),
        P(None, "fsdp", "section"),
        P("fsdp", "section"),
        P("section", "fsdp", None, None),
    )
    out_specs = (
        P("section", "fsdp", None, None),
        P("section", "fsdp", None, None),
        P("section", None, "fsdp", None),
        P("section", "fsdp", None),
        P("section", None, "fsdp"),
        P(None, "fsdp", "section"),
        P("fsdp", "section"),
    )
    return jax.shard_map(shards, mesh=mesh, in_specs=in_specs, out_specs=out_specs, check_vma=False)
```

```python
import functools

import jax
import jax.numpy as jnp
from jax import lax
from jax.experimental import pallas as pl
from jax.experimental.pallas import tpu as pltpu
from jax.sharding import PartitionSpec as P

HEADS = 16
HEAD_DIM = 64
QUAD = 4
LANES = QUAD * HEAD_DIM
RING = 4
STRIDE = {"y": 16, "x": 4, "z": 1}

FFN_AXES = ("y", "x")
ENC_AXES = ("x", "y")
GLOB_AXES = (("z", "z"), ("y", "x"), ("x", "y"))

epsilon = 1e-05
masked_score = -1e30
bf16 = jnp.bfloat16
f32 = jnp.float32

SCALAR = pl.BlockSpec(memory_space=pltpu.SMEM)
WHOLE = pl.BlockSpec(memory_space=pltpu.VMEM)
IN_HBM = pl.BlockSpec(memory_space=pltpu.HBM)
OUT_HBM = pltpu.HBM
QUICK = pl.CostEstimate(flops=1, bytes_accessed=1, transcendentals=0)


def of(shape, kind):
    return jax.ShapeDtypeStruct(shape, kind)


ROOM = {
    "lay": 6,
    "prepare": 8,
    "encoder_forward": 12,
    "encoder_out": 8,
    "global_forward": 8,
    "feed_forward": 26,
    "ffn_quarters": 18,
    "global_back": 12,
    "global_quarters": 10,
    "near": 10,
    "split": 10,
    "line_total": 10,
    "encoder_back": 14,
    "encoder_quarters": 10,
    "byte_partial": 12,
    "byte_gradient": 8,
}


def kernel_call(body, name, **options):
    return pl.pallas_call(
        body,
        name=name,
        cost_estimate=QUICK,
        compiler_params=pltpu.CompilerParams(vmem_limit_bytes=ROOM[name] << 20),
        **options,
    )


def across(block):
    return lax.ppermute(block, "section", [(0, 1), (1, 0)])


def moved(i, ax, by):
    step = STRIDE[ax]
    c = (i // step) % RING
    return i + ((c + by) % RING - c) * step


def shift(block, ax, by):
    return lax.ppermute(block, "fsdp", [(i, moved(i, ax, by)) for i in range(64)])


def shift_by_core(block, axes, by):
    route = [(64 * s + i, 64 * s + moved(i, ax, by)) for s, ax in enumerate(axes) for i in range(64)]
    return lax.ppermute(block, ("section", "fsdp"), route)


def place(ax):
    return (lax.axis_index("fsdp") // STRIDE[ax]) % RING


def planes(axes):
    rows = {}
    for s, ax in enumerate(axes):
        for i in range(64):
            rows.setdefault((s, (i // STRIDE[ax]) % RING), []).append(64 * s + i)
    return list(rows.values())


def lines(axes):
    rows = {}
    for s, ax in enumerate(axes):
        for i in range(64):
            c = (i // STRIDE[ax]) % RING
            rows.setdefault((s, i - c * STRIDE[ax]), []).append(64 * s + i)
    return list(rows.values())


def put(whole, piece, at, dim):
    where = [0] * whole.ndim
    where[dim] = at
    return lax.dynamic_update_slice(whole, piece, where)


def gather_direct(block, ax, dim):
    c = place(ax)
    whole = jnp.zeros((*block.shape[:dim], RING, *block.shape[dim + 1 :]), block.dtype)
    arrived = [(shift(block, ax, by), (c - by) % RING) for by in (1, -1, 2)]
    for piece, at in [(block, c)] + arrived:
        whole = put(whole, piece, at, dim)
    return whole


def ring_pieces(block, ax):
    half = block.shape[-1] // 256 * 128
    last = block.ndim - 1
    below, above = shift(block, ax, 1), shift(block, ax, -1)
    first = shift(lax.slice_in_dim(below, 0, half, axis=last), ax, 1)
    second = shift(lax.slice_in_dim(above, half, None, axis=last), ax, -1)
    return block, above, below, first, second


def columns(pieces, k, begin, end):
    if k != 2:
        return pieces[(0, 1, None, 2)[k]][..., begin:end]
    first, second = pieces[3:]
    cut = first.shape[-1]
    if end <= cut:
        return first[..., begin:end]
    if begin >= cut:
        return second[..., begin - cut : end - cut]
    return jnp.concatenate([first[..., begin:], second[..., : end - cut]], axis=-1)


def lay_kernel(c_ref, *refs):
    ins, outs = refs[:10], refs[10:]
    for ax, pieces, targets in (("y", ins[:5], outs[:3]), ("x", ins[5:], outs[3:])):
        c = c_ref[0 if ax == "y" else 1]
        for k in range(RING):
            at = lax.rem(c + k, RING)
            column = 0
            for out in targets:
                value = columns(pieces, k, column, column + out.shape[-1])
                if ax == "y":
                    out[at] = value
                else:
                    out[:, at] = value
                column += out.shape[-1]


def lay(places, on_y, on_x, half):
    rows = on_y[0].shape[0]
    wide = (half, half, on_y[0].shape[1] - 2 * half)
    outs = [of((RING, rows, w), bf16) for w in wide]
    outs += [of((RING, RING, rows // RING, half), bf16)] * 2
    made = kernel_call(
        lay_kernel,
        "lay",
        in_specs=[SCALAR] + [WHOLE] * 10,
        out_specs=[WHOLE] * 5,
        out_shape=outs,
    )(places, *on_y, *on_x)
    return [m.reshape(RING * rows, m.shape[-1]) for m in made]


def send_near(parts, axes):
    return [shift_by_core(parts[1], axes, 1), shift_by_core(parts[3], axes, -1)]


def send_far(parts, axes):
    return shift_by_core(parts[2], axes, 2)


def send_quarters(parts, axes):
    return [*send_near(parts, axes), send_far(parts, axes)]


def total_kernel(*refs):
    total = refs[0][...].astype(f32)
    for part in refs[1:-1]:
        total = total + part[...].astype(f32)
    refs[-1][...] = total.astype(bf16)


def line_total(*parts):
    return kernel_call(
        total_kernel,
        "line_total",
        in_specs=[WHOLE] * len(parts),
        out_specs=WHOLE,
        out_shape=of(parts[0].shape, bf16),
    )(*parts)


def split_kernel(axes, names, s_ref, *refs):
    n = len(refs) - 2 * RING - 1
    targets, refs, sent = refs[n : n + RING], refs[:n] + refs[n + RING : -1], refs[-1]
    total = refs[0][...].astype(f32)
    for part in refs[1:n]:
        total = total + part[...].astype(f32)
    total = total.astype(bf16)
    outs = refs[n:]
    for s, ax in enumerate(axes):

        @pl.when(s_ref[0] == s)
        def _():
            c = s_ref[1 + "yxz".index(ax)]
            dim = names[s].index(ax)
            blocks = total.reshape(*[RING] * len(names[s]), -1, total.shape[1])
            for at in range(RING):
                block = lax.index_in_dim(blocks, at, dim, keepdims=False)
                k = lax.rem(at + RING - c, RING)
                for j in range(RING):

                    @pl.when(k == j)
                    def _():
                        outs[j][...] = block.reshape(outs[j].shape)

    outgoing = Outgoing(outs, targets, sent)
    for k in range(RING):
        outgoing.send(k)
    outgoing.finish()


def split(scalars, parts, axes, names):
    rows, wide = parts[0].shape
    return kernel_call(
        functools.partial(split_kernel, axes, names),
        "split",
        in_specs=[SCALAR] + [WHOLE] * len(parts),
        out_specs=[IN_HBM] * RING,
        out_shape=[OUT_HBM((rows // RING, wide), bf16)] * RING,
        scratch_shapes=[pltpu.VMEM((rows // RING, wide), bf16)] * RING
        + [pltpu.SemaphoreType.DMA((RING,))],
    )(scalars, *parts)


def near_kernel(up, down, a, b, up_out, down_out):
    cut = a.shape[1]
    up_out[:, :cut] = (up[:, :cut].astype(f32) + a[...].astype(f32)).astype(bf16)
    up_out[:, cut:] = up[:, cut:]
    down_out[:, cut:] = (down[:, cut:].astype(f32) + b[...].astype(f32)).astype(bf16)
    down_out[:, :cut] = down[:, :cut]


def near(up, down, a, b):
    return kernel_call(
        near_kernel,
        "near",
        in_specs=[WHOLE] * 4,
        out_specs=[WHOLE] * 2,
        out_shape=[of(up.shape, bf16)] * 2,
    )(up, down, a, b)


def line_sum(parts, axes):
    return lax.psum_scatter(
        parts,
        ("section", "fsdp"),
        scatter_dimension=0,
        axis_index_groups=lines(axes),
        tiled=False,
    )


def plane_sum(part, axes):
    blocks = part.reshape(16, part.shape[0] // 16, part.shape[1])
    blocks = lax.all_to_all(
        blocks, ("section", "fsdp"), 0, 0, axis_index_groups=planes(axes), tiled=True
    )
    return jnp.sum(blocks.astype(f32), axis=0)


def stage(*values):
    return lax.optimization_barrier(values)


def inverse_rms(values):
    return lax.rsqrt(jnp.mean(values * values, axis=-1, keepdims=True) + epsilon)


def normalize_back(values, inverse, scales, gradient):
    unit_rows = values * inverse
    scaled = gradient * scales
    inner_mean = jnp.mean(scaled * unit_rows, axis=-1, keepdims=True)
    return inverse * (scaled - unit_rows * inner_mean)


def matmul(left, right):
    return jnp.dot(left, right, preferred_element_type=f32)


def times_transposed(left, right):
    return lax.dot_general(left, right, (((1,), (1,)), ((), ())), preferred_element_type=f32)


def transposed_times(left, right):
    return lax.dot_general(left, right, (((0,), (0,)), ((), ())), preferred_element_type=f32)


def of_head(value, h):
    head = lax.broadcasted_iota(jnp.int32, value.shape, 1) // HEAD_DIM
    return jnp.where(head == h, value, jnp.zeros_like(value))


def stacked(value):
    return jnp.concatenate([of_head(value, h) for h in range(QUAD)], axis=0)


def unstacked(value, rows):
    total = of_head(value[:rows], 0)
    for h in range(1, QUAD):
        total = total + of_head(value[h * rows : (h + 1) * rows], h)
    return total


def probabilities(q4, keys, table):
    raw = times_transposed(q4, keys)
    allowed = jnp.concatenate([table] * QUAD, axis=0) > 0
    scores = jnp.where(allowed, raw * HEAD_DIM ** (-0.5), masked_score)
    weights = jnp.exp(scores - jnp.max(scores, axis=-1, keepdims=True))
    return weights / jnp.sum(weights, axis=-1, keepdims=True)


def attend(q, k, v, table):
    p = probabilities(stacked(q), k, table).astype(bf16)
    return unstacked(matmul(p, v), q.shape[0]).astype(bf16)


def attend_back(q, k, v, table, d):
    rows = q.shape[0]
    q4, d4 = stacked(q), stacked(d)
    p = probabilities(q4, k, table)
    dp = times_transposed(d4, v)
    ds = p * (dp - jnp.sum(p * dp, axis=-1, keepdims=True)) * HEAD_DIM ** (-0.5)
    ds = ds.astype(bf16)
    dq = unstacked(matmul(ds, k), rows).astype(bf16)
    dk = transposed_times(ds, q4).astype(bf16)
    dv = transposed_times(p.astype(bf16), d4).astype(bf16)
    return dq, dk, dv


def lanes_of(section, half):
    mine = pl.ds(pl.multiple_of(section * half, half), half)
    theirs = pl.ds(pl.multiple_of((1 - section) * half, half), half)
    return mine, theirs


def merge(scratch, section, own, other):
    mine, theirs = lanes_of(section, own.shape[1])
    scratch[:, mine] = own
    scratch[:, theirs] = other


def swap_rows(x):
    half = x.shape[0] // 2
    return jnp.concatenate([x[half:], x[:half]], axis=0)


def quarter(turned, ax, at):
    if ax == "y":
        rows = turned[at]
    elif ax == "x":
        rows = turned[:, at]
    else:
        rows = turned[:, :, at]
    return rows.reshape(turned.shape[0] ** 2 * turned.shape[3], turned.shape[4])


def fill_quarters(x_ref, turned, rows, s_ref, axes, first):
    turned[...] = x_ref[...].T.reshape(turned.shape)
    for s, ax in enumerate(axes):

        @pl.when(s_ref[0] == s)
        def _():
            c = s_ref[1 + "yxz".index(ax)] if first else 0
            for k in range(RING):
                rows[k] = quarter(turned, ax, lax.rem(c + k, RING))


def turned_scratch(tokens, features):
    return pltpu.VMEM((RING, RING, RING, features // RING**3, tokens), bf16)


def quarter_scratch(tokens, features):
    return [
        turned_scratch(tokens, features),
        pltpu.VMEM((RING, features // RING, tokens), bf16),
    ]


def rows_of(x):
    return of((RING, x.shape[1] // RING, x.shape[0]), bf16)


def prepare_kernel(enc_axes, ffn_axes, s_ref, b_ref, x_ref, t_ref, b_rows, x_rows, t_rows, *turned):
    fill_quarters(b_ref, turned[0], b_rows, s_ref, enc_axes, True)
    fill_quarters(x_ref, turned[1], x_rows, s_ref, enc_axes, True)
    fill_quarters(t_ref, turned[2], t_rows, s_ref, ffn_axes, True)


def prepare(scalars, b, x, t, enc_axes, ffn_axes):
    return kernel_call(
        functools.partial(prepare_kernel, enc_axes, ffn_axes),
        "prepare",
        in_specs=[SCALAR] + [WHOLE] * 3,
        out_specs=[WHOLE] * 3,
        out_shape=[rows_of(a) for a in (b, x, t)],
        scratch_shapes=[turned_scratch(*a.shape) for a in (b, x, t)],
    )(scalars, b, x, t)


def encoder_kernel(x_ref, b_ref, wq, wk, wv, table, q_ref, k_ref, v_ref, mixed, mixed_swapped):
    q = matmul(x_ref[...], wq[...]).astype(bf16)
    k = matmul(b_ref[...], wk[...]).astype(bf16)
    v = matmul(b_ref[...], wv[...]).astype(bf16)
    q_ref[...], k_ref[...], v_ref[...] = q, k, v
    out = attend(q, k, v, table[0])
    mixed[...] = out
    mixed_swapped[...] = out


def encoder_forward(query_low, byte_low, wq, wk, wv, table):
    micro, rows, keys = table.shape
    width, half = wq.shape
    weight = pl.BlockSpec((width, LANES), lambda h, m: (0, h))
    per_row = pl.BlockSpec((rows, LANES), lambda h, m: (m, h))
    per_key = pl.BlockSpec((keys, LANES), lambda h, m: (m, h))
    return kernel_call(
        encoder_kernel,
        "encoder_forward",
        grid=(half // LANES, micro),
        in_specs=[
            pl.BlockSpec((rows, width), lambda h, m: (m, 0)),
            pl.BlockSpec((keys, width), lambda h, m: (m, 0)),
            weight,
            weight,
            weight,
            pl.BlockSpec((1, rows, keys), lambda h, m: (m, 0, 0)),
        ],
        out_specs=[
            per_row,
            per_key,
            per_key,
            per_row,
            pl.BlockSpec((rows, LANES), lambda h, m: (1 - m, h)),
        ],
        out_shape=[
            of((micro * rows, half), bf16),
            of((micro * keys, half), bf16),
            of((micro * keys, half), bf16),
            of((micro * rows, half), bf16),
            of((micro * rows, half), bf16),
        ],
    )(query_low, byte_low, wq, wk, wv, table)


def encoder_out_kernel(
    enc_axes, glob_axes, s_ref, pooled, own, other, wo, wo_other, gains,
    hidden_ref, low_ref, mixed_rows, low_rows, whole_ref, sum_ref, turned_mixed, turned_low,
):
    section = s_ref[0]
    merge(whole_ref, section, own[...], other[...])
    whole = whole_ref[...]
    merge(sum_ref, section, matmul(whole, wo[...]), matmul(whole, wo_other[...]))
    low_hidden = (pooled[...] + sum_ref[...]).astype(bf16)
    hidden_ref[...] = low_hidden
    hidden = low_hidden.astype(f32)
    low = (hidden * inverse_rms(hidden) * gains[2:3]).astype(bf16)
    low_ref[...] = low
    fill_quarters(whole, turned_mixed, mixed_rows, s_ref, enc_axes, True)
    fill_quarters(low, turned_low, low_rows, s_ref, glob_axes, True)


def encoder_out(scalars, pooled, own, other, wo, wo_other, gains, enc_axes, glob_axes):
    tokens, width = pooled.shape
    rows = of((RING, width // RING, tokens), bf16)
    return kernel_call(
        functools.partial(encoder_out_kernel, enc_axes, glob_axes),
        "encoder_out",
        in_specs=[SCALAR] + [WHOLE] * 6,
        out_specs=[WHOLE] * 4,
        out_shape=[of((tokens, width), bf16), of((tokens, width), bf16), rows, rows],
        scratch_shapes=[pltpu.VMEM((tokens, width), bf16), pltpu.VMEM((tokens, width), f32)]
        + [turned_scratch(tokens, width)] * 2,
    )(scalars, pooled, own, other, wo, wo_other, gains)


def global_kernel(x_ref, packed, table, q_ref, k_ref, v_ref, mixed, mixed_swapped, weights, sems):
    h, m = pl.program_id(0), pl.program_id(1)
    count = pl.num_programs(0)

    def copy(j, at):
        source = packed.at[:, pl.ds(pl.multiple_of((j * count + at) * LANES, LANES), LANES)]
        return pltpu.make_async_copy(source, weights.at[at, j], sems.at[at, j])

    @pl.when((h == 0) & (m == 0))
    def _():
        for at in range(weights.shape[0]):
            for j in range(3):
                copy(j, at).start()

    @pl.when(m == 0)
    def _():
        for j in range(3):
            copy(j, h).wait()

    x = x_ref[...]
    q, k, v = (matmul(x, weights[h, j]).astype(bf16) for j in range(3))
    q_ref[...], k_ref[...], v_ref[...] = q, k, v
    out = attend(q, k, v, table[0])
    mixed[...] = out
    mixed_swapped[...] = out


def global_forward(x, packed, table, half):
    micro, rows, _ = table.shape
    width = x.shape[1]
    count = half // LANES
    per_row = pl.BlockSpec((rows, LANES), lambda h, m: (m, h))
    return kernel_call(
        global_kernel,
        "global_forward",
        grid=(count, micro),
        in_specs=[
            pl.BlockSpec((rows, width), lambda h, m: (m, 0)),
            IN_HBM,
            pl.BlockSpec((1, rows, rows), lambda h, m: (m, 0, 0)),
        ],
        out_specs=[per_row] * 4 + [pl.BlockSpec((rows, LANES), lambda h, m: (1 - m, h))],
        out_shape=[of((micro * rows, half), bf16)] * 5,
        scratch_shapes=[
            pltpu.VMEM((count, 3, width, LANES), bf16),
            pltpu.SemaphoreType.DMA((count, 3)),
        ],
    )(x, packed, table)


class Outgoing:
    def __init__(self, buffers, targets, sems):
        self.copies = [
            pltpu.make_async_copy(b, t, sems.at[k]) for k, (b, t) in enumerate(zip(buffers, targets))
        ]

    def send(self, k):
        self.copies[k].start()

    def finish(self):
        for copy in self.copies:
            copy.wait()


def ffn_kernel(
    units, at, axes, s_ref, hidden, own, other, wo, wo_other, gains, target, rows_target, packed,
    mixed_whole, middle_ref, partial, partial_sent, far_a, far_b, gate_out, up_out, inner_out, rows,
    w_gate, w_up, w_down, turned, sems,
):
    copies = [
        pltpu.make_async_copy(packed.at[:, pl.ds(at + k * units, units)], w, sems.at[k])
        for k, w in enumerate((w_gate, w_up, w_down))
    ]
    for copy in copies:
        copy.start()
    section = s_ref[0]
    merge(mixed_whole, section, own[...], other[...])
    whole = mixed_whole[...]
    merge(middle_ref, section, matmul(whole, wo[...]), matmul(whole, wo_other[...]))
    middle = hidden[...].astype(f32) + middle_ref[...]
    middle_ref[...] = middle
    low = (middle * inverse_rms(middle) * gains[3:4]).astype(bf16)
    copies[0].wait()
    gate = matmul(low, w_gate[...])
    copies[1].wait()
    up = matmul(low, w_up[...])
    sigma = jax.nn.sigmoid(gate)
    inner = (gate * sigma * up).astype(bf16)
    copies[2].wait()
    inner_grad = matmul(target[...], w_down[...])
    up_grad = (inner_grad * gate * sigma).astype(bf16)
    gate_grad = (inner_grad * up * sigma * (1.0 + gate * (1.0 - sigma))).astype(bf16)
    gate_out[...], up_out[...], inner_out[...] = gate_grad, up_grad, inner
    total = times_transposed(gate_grad, w_gate[...]) + times_transposed(up_grad, w_up[...])
    partial[...] = total
    partial_sent[...] = swap_rows(total.astype(bf16))
    fill_quarters(low, turned, rows, s_ref, axes, True)
    cut = far_a.shape[1]
    for j, (x, d) in enumerate(((rows, gate_grad), (rows, up_grad), (rows_target, inner))):
        value = matmul(x[2], d).astype(bf16)
        begin, end = j * units, (j + 1) * units
        if end <= cut:
            far_a[:, begin:end] = value
        elif begin >= cut:
            far_b[:, begin - cut : end - cut] = value
        else:
            far_a[:, begin:] = value[:, : cut - begin]
            far_b[:, : end - cut] = value[:, cut - begin :]


def feed_forward(
    scalars, hidden, own, other, wo, wo_other, gains, target, rows, packed, units, at, axes
):
    tokens, width = hidden.shape
    block = width // RING
    cut = 3 * units // 256 * 128
    return kernel_call(
        functools.partial(ffn_kernel, units, at, axes),
        "feed_forward",
        in_specs=[SCALAR] + [WHOLE] * 8 + [IN_HBM],
        out_specs=[WHOLE] * 10,
        out_shape=[
            of((tokens, width), bf16),
            of((tokens, width), f32),
            of((tokens, width), f32),
            of((tokens, width), bf16),
            of((block, cut), bf16),
            of((block, 3 * units - cut), bf16),
        ]
        + [of((tokens, units), bf16)] * 3
        + [of((RING, block, tokens), bf16)],
        scratch_shapes=[pltpu.VMEM((width, units), bf16)] * 3
        + [turned_scratch(tokens, width), pltpu.SemaphoreType.DMA((3,))],
    )(scalars, hidden, own, other, wo, wo_other, gains, target, rows, packed)


def ffn_quarters_kernel(
    at, rows, rows_target, gate_grad, up_grad, inner, middle, packed,
    result, result_sent, up_part, down_part, own_part, up_made, down_made, own_made, w_down, sent, sem,
):
    units = inner.shape[1]
    copy = pltpu.make_async_copy(packed.at[:, pl.ds(at + 2 * units, units)], w_down, sem)
    copy.start()
    outgoing = Outgoing((up_made, down_made, own_made), (up_part, down_part, own_part), sent)
    for n, (k, part) in enumerate(((1, up_made), (3, down_made), (0, own_made))):
        for j, (x, d) in enumerate(((rows, gate_grad), (rows, up_grad), (rows_target, inner))):
            part[:, j * units : (j + 1) * units] = matmul(x[k], d[...]).astype(bf16)
        outgoing.send(n)
    copy.wait()
    half = result.shape[0]
    out = times_transposed(inner[...], w_down[...])
    result[...] = middle[:half] + out[:half]
    result_sent[...] = out[half:].astype(bf16)
    outgoing.finish()


def ffn_quarters(rows, rows_target, gate_grad, up_grad, inner, middle, packed, at):
    tokens, width = middle.shape
    units = inner.shape[1]
    shape = (width // RING, 3 * units)
    return kernel_call(
        functools.partial(ffn_quarters_kernel, at),
        "ffn_quarters",
        in_specs=[WHOLE] * 6 + [IN_HBM],
        out_specs=[WHOLE] * 2 + [IN_HBM] * 3,
        out_shape=[of((tokens // 2, width), f32), of((tokens // 2, width), bf16)]
        + [OUT_HBM(shape, bf16)] * 3,
        scratch_shapes=[pltpu.VMEM(shape, bf16)] * 3
        + [pltpu.VMEM((width, units), bf16)]
        + [pltpu.SemaphoreType.DMA((3,)), pltpu.SemaphoreType.DMA],
    )(rows, rows_target, gate_grad, up_grad, inner, middle, packed)


def global_back_kernel(
    s_ref, target, middle, partial, came, gains, wo, wo_other, q_ref, k_ref, v_ref, table, packed,
    middle_grad, middle_half, dqkv, out, out_sent, mixed_grad, low, w_qkv, sem,
):
    rows, half = table.shape[1], wo.shape[1]
    m, h = pl.program_id(0), pl.program_id(1)
    copy = pltpu.make_async_copy(packed.at[:, pl.ds(0, 3 * half)], w_qkv, sem)

    @pl.when((m == 0) & (h == 0))
    def _():
        copy.start()
        section = s_ref[0]
        v = middle[...]
        grad = partial[...] + came[...].astype(f32)
        grad = target[...].astype(f32) + normalize_back(v, inverse_rms(v), gains[3:4], grad)
        middle_grad[...] = grad
        low[...] = grad.astype(bf16)
        mine, theirs = lanes_of(section, half)
        middle_half[...] = low[:, mine]
        own_rows = pl.ds(pl.multiple_of(section * half, half), half)
        mixed_grad[...] = (
            times_transposed(low[:, mine], wo[own_rows])
            + times_transposed(low[:, theirs], wo_other[own_rows])
        ).astype(bf16)

    here = pl.ds(pl.multiple_of(m * rows, rows), rows)
    at = pl.multiple_of(h * LANES, LANES)
    quad = pl.ds(at, LANES)
    dq, dk, dv = attend_back(
        q_ref[here, quad], k_ref[here, quad], v_ref[here, quad], table[0], mixed_grad[here, quad]
    )
    dqkv[here, quad] = dq
    dqkv[here, pl.ds(at + half, LANES)] = dk
    dqkv[here, pl.ds(at + 2 * half, LANES)] = dv

    @pl.when((m == pl.num_programs(0) - 1) & (h == pl.num_programs(1) - 1))
    def _():
        copy.wait()
        total = times_transposed(dqkv[...], w_qkv[...])
        out[...] = total
        out_sent[...] = swap_rows(total.astype(bf16))


def global_back(section, target, middle, partial, came, gains, wo, wo_other, q, k, v, table, packed):
    micro, rows, _ = table.shape
    tokens, width = middle.shape
    half = wo.shape[1]

    def fixed(shape):
        return pl.BlockSpec(shape, lambda m, h: (0, 0))

    return kernel_call(
        global_back_kernel,
        "global_back",
        grid=(micro, half // LANES),
        in_specs=[SCALAR]
        + [fixed((tokens, width))] * 4
        + [fixed(gains.shape)]
        + [fixed((width, half))] * 2
        + [fixed((tokens, half))] * 3
        + [pl.BlockSpec((1, rows, rows), lambda m, h: (m, 0, 0)), IN_HBM],
        out_specs=[
            fixed((tokens, width)),
            fixed((tokens, half)),
            fixed((tokens, 3 * half)),
            fixed((tokens, width)),
            fixed((tokens, width)),
        ],
        out_shape=[
            of((tokens, width), f32),
            of((tokens, half), bf16),
            of((tokens, 3 * half), bf16),
            of((tokens, width), f32),
            of((tokens, width), bf16),
        ],
        scratch_shapes=[
            pltpu.VMEM((tokens, half), bf16),
            pltpu.VMEM((tokens, width), bf16),
            pltpu.VMEM((width, 3 * half), bf16),
            pltpu.SemaphoreType.DMA,
        ],
    )(section, target, middle, partial, came, gains, wo, wo_other, q, k, v, table, packed)


def global_quarters_kernel(axes, s_ref, x_rows, d_ref, y_ref, e_ref, *refs):
    outs, made, (turned, y_rows, sent) = refs[:4], refs[4:8], refs[8:]
    outgoing = Outgoing(made, outs, sent)
    fill_quarters(y_ref, turned, y_rows, s_ref, axes, True)
    for k in (1, 3, 2, 0):
        made[k][:, : d_ref.shape[1]] = matmul(x_rows[k], d_ref[...]).astype(bf16)
        made[k][:, d_ref.shape[1] :] = matmul(y_rows[k], e_ref[...]).astype(bf16)
        outgoing.send(k)
    outgoing.finish()


def global_quarters(scalars, x_rows, d, y, e, axes):
    tokens, width = y.shape
    shape = (width // RING, d.shape[1] + e.shape[1])
    return kernel_call(
        functools.partial(global_quarters_kernel, axes),
        "global_quarters",
        in_specs=[SCALAR] + [WHOLE] * 4,
        out_specs=[IN_HBM] * 4,
        out_shape=[OUT_HBM(shape, bf16)] * 4,
        scratch_shapes=[pltpu.VMEM(shape, bf16)] * 4
        + quarter_scratch(tokens, width)
        + [pltpu.SemaphoreType.DMA((4,))],
    )(scalars, x_rows, d, y, e)


def encoder_back_kernel(
    s_ref, middle_grad, hidden, partial, came, gains, wo, wo_other, q_ref, k_ref, v_ref, table,
    embed, embed_half, dq_ref, dkv_ref, mixed_grad,
):
    rows, keys = table.shape[1:]
    half = wo.shape[1]
    m, h = pl.program_id(0), pl.program_id(1)

    @pl.when((m == 0) & (h == 0))
    def _():
        section = s_ref[0]
        v = hidden[...].astype(f32)
        grad = partial[...] + came[...].astype(f32)
        grad = middle_grad[...] + normalize_back(v, inverse_rms(v), gains[2:3], grad)
        embed[...] = grad.astype(bf16)
        mine, theirs = lanes_of(section, half)
        embed_half[...] = embed[:, mine]
        own_rows = pl.ds(pl.multiple_of(section * half, half), half)
        mixed_grad[...] = (
            times_transposed(embed[:, mine], wo[own_rows])
            + times_transposed(embed[:, theirs], wo_other[own_rows])
        ).astype(bf16)

    here = pl.ds(pl.multiple_of(m * rows, rows), rows)
    at = pl.multiple_of(h * LANES, LANES)
    dq, dk, dv = attend_back(
        q_ref[...], k_ref[...], v_ref[...], table[0], mixed_grad[here, pl.ds(at, LANES)]
    )
    dq_ref[...] = dq
    there = pl.ds(pl.multiple_of(m * keys, keys), keys)
    dkv_ref[there, pl.ds(at, LANES)] = dk
    dkv_ref[there, pl.ds(at + half, LANES)] = dv


def encoder_back(section, middle_grad, hidden, partial, came, gains, wo, wo_other, q, k, v, table):
    micro, rows, keys = table.shape
    tokens, width = hidden.shape
    half = wo.shape[1]

    def fixed(shape):
        return pl.BlockSpec(shape, lambda m, h: (0, 0))

    per_row = pl.BlockSpec((rows, LANES), lambda m, h: (m, h))
    per_key = pl.BlockSpec((keys, LANES), lambda m, h: (m, h))
    return kernel_call(
        encoder_back_kernel,
        "encoder_back",
        grid=(micro, half // LANES),
        in_specs=[SCALAR]
        + [fixed((tokens, width))] * 4
        + [fixed(gains.shape)]
        + [fixed((width, half))] * 2
        + [per_row, per_key, per_key, pl.BlockSpec((1, rows, keys), lambda m, h: (m, 0, 0))],
        out_specs=[
            fixed((tokens, width)),
            fixed((tokens, half)),
            per_row,
            fixed((micro * keys, 2 * half)),
        ],
        out_shape=[
            of((tokens, width), bf16),
            of((tokens, half), bf16),
            of((tokens, half), bf16),
            of((micro * keys, 2 * half), bf16),
        ],
        scratch_shapes=[pltpu.VMEM((tokens, half), bf16)],
    )(section, middle_grad, hidden, partial, came, gains, wo, wo_other, q, k, v, table)


def encoder_quarters_kernel(b_rows, dkv, x_rows, dq, y_rows, e_ref, *refs):
    outs, made, sent = refs[:4], refs[4:8], refs[8]
    half = dq.shape[1]
    outgoing = Outgoing(made, outs, sent)
    for k in (1, 3, 2, 0):
        for rows, d, at in ((x_rows, dq, 0), (b_rows, dkv, half), (y_rows, e_ref, 3 * half)):
            made[k][:, at : at + d.shape[1]] = matmul(rows[k], d[...]).astype(bf16)
        outgoing.send(k)
    outgoing.finish()


def encoder_quarters(b_rows, dkv, x_rows, dq, y_rows, e):
    shape = (x_rows.shape[1], 4 * dq.shape[1])
    return kernel_call(
        encoder_quarters_kernel,
        "encoder_quarters",
        in_specs=[WHOLE] * 6,
        out_specs=[IN_HBM] * 4,
        out_shape=[OUT_HBM(shape, bf16)] * 4,
        scratch_shapes=[pltpu.VMEM(shape, bf16)] * 4 + [pltpu.SemaphoreType.DMA((4,))],
    )(b_rows, dkv, x_rows, dq, y_rows, e)


def byte_partial_kernel(dkv, dq, wk, wv, wq, own, query_own, sent):
    half = wk.shape[1]
    count, rows = own.shape[0], query_own.shape[0]
    for at, out in ((0, own), (count, sent.at[:count])):
        total = times_transposed(dkv[at : at + count, :half], wk[...])
        total = total + times_transposed(dkv[at : at + count, half:], wv[...])
        out[...] = total.astype(out.dtype)
    total = times_transposed(dq[...], wq[...])
    query_own[...] = total[:rows]
    sent[count:] = total[rows:].astype(bf16)


def byte_partial(dkv, dq, wk, wv, wq):
    width = wk.shape[0]
    count, rows = dkv.shape[0] // 2, dq.shape[0] // 2
    return kernel_call(
        byte_partial_kernel,
        "byte_partial",
        in_specs=[WHOLE] * 5,
        out_specs=[WHOLE] * 3,
        out_shape=[
            of((count, width), f32),
            of((rows, width), f32),
            of((count + rows, width), bf16),
        ],
    )(dkv, dq, wk, wv, wq)


def byte_grad_kernel(raw, own, query_own, came, pooled, embed, member, size, gains, out):
    count = raw.shape[0]
    pool = pooled[...]
    grad = query_own[...] + came[count:].astype(f32)
    share = embed[...].astype(f32) + normalize_back(pool, inverse_rms(pool), gains[0:1], grad)
    share = share / size[...]
    high = share.astype(bf16)
    rest = (share - high.astype(f32)).astype(bf16)
    spread = transposed_times(member[...], high) + transposed_times(member[...], rest)
    v = raw[...].astype(f32)
    grad = own[...] + came[:count].astype(f32)
    out[...] = spread + normalize_back(v, inverse_rms(v), gains[1:2], grad)


def byte_gradient(*args):
    return kernel_call(
        byte_grad_kernel,
        "byte_gradient",
        in_specs=[WHOLE] * 9,
        out_specs=WHOLE,
        out_shape=of(args[0].shape, f32),
    )(*args)


def patch_tables(lengths, documents):
    patches, count = lengths.shape[1], documents.shape[1]
    ends = jnp.cumsum(lengths, axis=1, dtype=jnp.int32)
    starts = ends - lengths
    position = lax.broadcasted_iota(jnp.int32, (1, patches, count), 2)
    member = (position >= starts[:, :, None]) & (position < ends[:, :, None])
    first_doc = jnp.sum(
        jnp.where(position == starts[:, :, None], documents[:, None, :], 0), axis=2
    )
    allowed = member & (documents[:, None, :] == first_doc[:, :, None])
    order_rows = lax.broadcasted_iota(jnp.int32, (1, patches, patches), 1)
    order_cols = lax.broadcasted_iota(jnp.int32, (1, patches, patches), 2)
    causal = (order_cols <= order_rows) & (first_doc[:, None, :] == first_doc[:, :, None])
    return member.astype(bf16), allowed.astype(f32), causal.astype(f32)


def own_first(pair, section):
    return jnp.where(section == 0, pair, pair[::-1])


def shards(
    byte_states,
    patch_lengths,
    doc_ids,
    proj_weights,
    out_weights,
    norm_gains,
    in_weights,
    down_weights,
    cotangent,
):
    section = lax.axis_index("section")
    scalars = jnp.stack([section, place("y"), place("x"), place("z")]).astype(jnp.int32)
    scalars, section = stage(scalars, section)
    width = byte_states.shape[-1]
    half = width // 2
    units = down_weights.shape[1]

    own_w = jnp.concatenate([proj_weights[0], out_weights], axis=0)
    own_w = own_w.transpose(1, 0, 2).reshape(16, 4, 2, half)
    gains_own = jnp.pad(norm_gains[0].T, ((0, 0), (0, 126)))
    keep = jnp.where(section == 0, own_w[:, :, 0], own_w[:, :, 1]).reshape(16, 4 * half)
    give = jnp.where(section == 0, own_w[:, :, 1], own_w[:, :, 0]).reshape(16, 4 * half)
    got = across(jnp.concatenate([give, gains_own], axis=1))
    enc = jnp.where(section == 0, keep, got[:, : 4 * half])
    glob = jnp.where(section == 0, got[:, : 4 * half], keep)
    gains_first = jnp.where(section == 0, gains_own, got[:, 4 * half :])
    gains_last = jnp.where(section == 0, got[:, 4 * half :], gains_own)
    gains = jnp.concatenate([gains_first[:, :2], gains_last[:, :126]], axis=1)
    packed = jnp.concatenate(
        [glob, in_weights[0], in_weights[1], down_weights], axis=1
    )
    packed = lax.all_gather(packed, "fsdp", axis=0, tiled=True)

    pack = jnp.concatenate(
        [enc[:, half : 3 * half], gains, enc[:, :half], enc[:, 3 * half :]], axis=1
    )
    first = 2 * half + 128
    pack = gather_direct(pack[None], "z", 0).reshape(64, -1)
    on_y = gather_direct(pack[None, :, :first], "x", 0).reshape(256, -1)
    on_x = gather_direct(pack[None, :, first:], "y", 0)
    places = jnp.stack([place("y"), place("x")])
    wk0, wv0, gains, wq0, wo0 = lay(places, ring_pieces(on_y, "y"), ring_pieces(on_x, "x"), half)
    pick = (
        lax.broadcasted_iota(jnp.int32, (8, 128), 0) == lax.broadcasted_iota(jnp.int32, (8, 128), 1)
    ).astype(bf16)
    gains = times_transposed(pick, gains)
    wo0_other = across(wo0)

    own_bytes, own_target = byte_states[0, 0], cotangent[0, 0]
    raw = jnp.concatenate([own_bytes, across(own_bytes)], axis=0)
    target = jnp.concatenate([own_target, across(own_target)], axis=0)
    lengths = own_first(patch_lengths[:, 0], section)
    documents = own_first(doc_ids[:, 0], section)
    patches, count = lengths.shape[1], documents.shape[1]
    member, allowed, causal = patch_tables(lengths, documents)
    size = lengths.astype(f32).reshape(-1, 1)

    raw_f32 = raw.astype(f32)
    pooled = lax.dot_general(
        member,
        raw.reshape(2, count, width),
        (((2,), (1,)), ((0,), (0,))),
        preferred_element_type=f32,
    ).reshape(2 * patches, width)
    pooled = pooled / size
    query_low = (pooled * inverse_rms(pooled) * gains[0]).astype(bf16)
    byte_low = (raw_f32 * inverse_rms(raw_f32) * gains[1]).astype(bf16)
    q0, k0, v0, mixed, mixed_sent = encoder_forward(query_low, byte_low, wq0, wk0, wv0, allowed)
    byte_rows, query_rows, target_rows = prepare(
        scalars, byte_low, query_low, target, ENC_AXES, FFN_AXES
    )
    hidden, normed_low, mixed_rows, normed_rows = encoder_out(
        scalars, pooled, mixed, across(mixed_sent), wo0, wo0_other, gains, ENC_AXES, GLOB_AXES[0]
    )
    (
        packed, hidden, normed_low, mixed_rows, normed_rows, byte_rows, query_rows, target_rows, causal,
    ) = stage(
        packed, hidden, normed_low, mixed_rows, normed_rows, byte_rows, query_rows, target_rows, causal,
    )
    wo1 = packed[:, 3 * half : 4 * half]
    wo1_other = across(wo1)
    packed = pltpu.with_memory_space_constraint(packed, pltpu.HBM)
    q1, k1, v1, mixed, mixed_sent = global_forward(normed_low, packed, causal, half)
    (
        mixed1, middle, ffn_partial, ffn_sent, far_a, far_b, gate_grad, up_grad, inner, low_rows,
    ) = feed_forward(
        scalars, hidden, mixed, across(mixed_sent), wo1, wo1_other, gains, target, target_rows,
        packed, units, 4 * half, FFN_AXES,
    )
    far_a, far_b, inner, ffn_sent = stage(far_a, far_b, inner, ffn_sent)
    ffn_came = across(ffn_sent)

    far_a, far_b = shift_by_core(far_a, FFN_AXES, 1), shift_by_core(far_b, FFN_AXES, -1)
    block_out, block_sent, up_part, down_part, own_part = ffn_quarters(
        low_rows, target_rows, gate_grad, up_grad, inner, middle, packed, 4 * half
    )
    ffn_came, up_part, down_part, own_part = stage(ffn_came, up_part, down_part, own_part)
    middle_grad, middle_half, dqkv, normed_partial, normed_sent = global_back(
        scalars, target, middle, ffn_partial, ffn_came, gains, wo1, wo1_other,
        q1, k1, v1, causal, packed,
    )
    glob_parts = global_quarters(
        scalars, normed_rows, dqkv, mixed1, middle_half, GLOB_AXES[0]
    )
    far_a, far_b, normed_sent, glob_parts, up_part, down_part, own_part, block_sent = stage(
        far_a, far_b, normed_sent, glob_parts, up_part, down_part, own_part, block_sent
    )
    block_came = across(block_sent)

    up_part, down_part = near(up_part, down_part, far_a, far_b)
    normed_came, up_part, down_part = stage(across(normed_sent), up_part, down_part)
    up_came, down_came = (
        shift_by_core(up_part, FFN_AXES, 1),
        shift_by_core(down_part, FFN_AXES, -1),
    )
    glob_came = send_near(glob_parts, GLOB_AXES[0])
    embed, embed_half, dq, dkv = encoder_back(
        scalars, middle_grad, hidden, normed_partial, normed_came, gains, wo0, wo0_other,
        q0, k0, v0, allowed,
    )
    enc_parts = encoder_quarters(byte_rows, dkv, query_rows, dq, mixed_rows, embed_half)
    block_out = block_out + block_came.astype(f32)
    up_came, down_came, glob_came, glob_parts, enc_parts, dq, dkv, block_out = stage(
        up_came, down_came, glob_came, glob_parts, enc_parts, dq, dkv, block_out
    )

    enc_came = send_quarters(enc_parts, ENC_AXES)
    glob_came.append(send_far(glob_parts, GLOB_AXES[0]))
    byte_own, query_own, byte_sent = byte_partial(dkv, dq, wk0, wv0, wq0)
    ffn_line = line_total(own_part, up_came, down_came)
    ffn_line, enc_came, enc_parts, glob_came, byte_sent = stage(
        ffn_line, enc_came, enc_parts, glob_came, byte_sent
    )

    glob_parts = split(scalars, [glob_parts[0], *glob_came], GLOB_AXES[1], ("yx", "yx"))
    enc_line = line_total(enc_parts[0], *enc_came)
    ffn_line, glob_parts, enc_line = stage(ffn_line, glob_parts, enc_line)
    ffn_sum = plane_sum(ffn_line, FFN_AXES)
    glob_came = send_quarters(glob_parts, GLOB_AXES[1])
    byte_grad = byte_gradient(
        own_bytes, byte_own, query_own, across(byte_sent), pooled[:patches], embed[:patches],
        member[0], size[:patches], gains,
    )
    glob_came, byte_grad = stage(glob_came, byte_grad)
    glob_parts = split(scalars, [glob_parts[0], *glob_came], GLOB_AXES[2], ("x", "y"))
    ffn_sum, enc_line, glob_parts = stage(ffn_sum, enc_line, glob_parts)
    glob_came = send_quarters(glob_parts, GLOB_AXES[2])

    enc_sum = plane_sum(enc_line, ENC_AXES)
    glob_sum = sum(p.astype(f32) for p in [glob_parts[0], *glob_came])

    gate_sum, up_sum, down_sum = jnp.split(ffn_sum, 3, axis=1)
    mine = jnp.where(section == 0, enc_sum, glob_sum)
    theirs = across(jnp.where(section == 0, glob_sum, enc_sum))
    first = jnp.where(section == 0, mine, theirs)
    last = jnp.where(section == 0, theirs, mine)
    sums = jnp.stack(
        [
            jnp.concatenate([x[:, k * half : (k + 1) * half] for x in (first, last)], axis=1)
            for k in range(4)
        ]
    )

    def against(weight, grad):
        return jnp.sum(weight.astype(f32) * grad, axis=-1)

    own_dots = against(proj_weights[0], sums[:3])
    ffn_dots = against(in_weights[0], gate_sum) + against(in_weights[1], up_sum)
    ffn_dots = ffn_dots + across(ffn_dots)
    gain_sum = jnp.where(
        section == 0,
        jnp.stack([own_dots[0], own_dots[1] + own_dots[2]]),
        jnp.stack([own_dots[0] + own_dots[1] + own_dots[2], ffn_dots]),
    )
    gain_sum = gain_sum / norm_gains[0].astype(f32)
    return (
        block_out[None, None],
        byte_grad[None, None],
        sums[None, :3],
        sums[3:],
        gain_sum[None],
        jnp.stack([gate_sum, up_sum]),
        down_sum,
    )


def solution(mesh):
    in_specs = (
        P("section", "fsdp", None, None),
        P(None, "fsdp", None),
        P(None, "fsdp", None),
        P("section", None, "fsdp", None),
        P("section", "fsdp", None),
        P("section", None, "fsdp"),
        P(None, "fsdp", "section"),
        P("fsdp", "section"),
        P("section", "fsdp", None, None),
    )
    out_specs = (
        P("section", "fsdp", None, None),
        P("section", "fsdp", None, None),
        P("section", None, "fsdp", None),
        P("section", "fsdp", None),
        P("section", None, "fsdp"),
        P(None, "fsdp", "section"),
        P("fsdp", "section"),
    )
    return jax.shard_map(shards, mesh=mesh, in_specs=in_specs, out_specs=out_specs, check_vma=False)
```
